512 devices in a mesh: row: 16 (over y_lo, x, core), col: 32 (over y_hi, z).
Axes of the slice: x: 4, y: 4 (y_hi: 2, y_lo: 2; y = y_hi * 2 + y_lo), z: 16, core: 2. Of those that a mesh axis runs over, the one named last changes fastest.
Arguments:
- valence_orbitals: bfloat16 [4, 48, 2, 2048], P(None, None, None, 'row'), may hold values from -6 to 6
- conduction_orbitals: bfloat16 [4, 64, 2, 2048], P(None, None, None, 'row'), may hold values from -6 to 6
- screened: bfloat16 [2, 2048, 2048], P(None, 'row'), may hold values from -1 to 1, as said below
- valence_index: int32 [4096], replicated, may hold values from 0 to 47
- conduction_index: int32 [4096], replicated, may hold values from 0 to 63
- kpoint_index: int32 [4096], replicated, may hold values from 0 to 3
Outputs:
- kernel: float32 [2, 32, 128, 4096], P(None, None, 'row', 'col')
The draws below stay inside these ranges and needn't reach their ends.
Inputs may be any that keep to these rules, and one draw needn't show every extreme that they name: screened[0] is symmetric and screened[1] antisymmetric: the interaction is Hermitian.
All inputs are finite; a program needn't handle non-finite values.
Results may differ from the reference program's by a relative error of at most 0.0065.
Values may be sent and summed in bfloat16 or wider, within the bound.
No kernel may reach another device: no remote copies, remote signals or barrier semaphores. Data moves between devices by JAX's collectives and lax.ppermute only.
A program may use at most 64 MiB of HBM per device.

```python
import math
import jax
import jax.numpy as jnp
from jax import lax

VAL = 48
CON = 64
KPTS = 4
PLANE = 2048
FINE = 8
STRIDE = 16
SPAN = 32
TRANS = 4096


def draw_screened(key, part):
    key = jax.random.fold_in(key, 11)
    key_sym, key_diag = jax.random.split(key, 2)
    gaussian = jax.random.normal(key_sym, (2, PLANE, PLANE), jnp.float32)
    factor = 0.35 / PLANE
    real_part = (gaussian[0] + gaussian[0].T) * factor
    imag_part = (gaussian[1] - gaussian[1].T) * factor
    diagonal = jnp.exp(jax.random.uniform(key_diag, (PLANE,), jnp.float32, math.log(0.5), math.log(5.0))) * (0.25 / math.sqrt(PLANE))
    real_part = real_part + jnp.diag(diagonal)
    return jnp.stack([real_part, imag_part]).astype(jnp.bfloat16)


def plant(entries, key, smallest, largest):
    index_at = [jax.random.randint(jax.random.fold_in(key, axis), (), 0, length) for axis, length in enumerate(entries.shape)]
    widest = entries.shape.index(max(entries.shape))
    beside = index_at[:widest] + [(index_at[widest] + 1) % entries.shape[widest]] + index_at[widest + 1:]
    return entries.at[tuple(index_at)].set(smallest).at[tuple(beside)].set(largest)


def level_of(rng, dims, cuts, smallest, high):
    level, own = 1.0, jax.random.fold_in(rng, 6)
    for axis_at, parts in cuts:
        draws = jnp.exp(jax.random.uniform(jax.random.fold_in(own, axis_at), (parts,), jnp.float32, smallest / len(cuts), high / len(cuts)))
        level = level * jnp.repeat(draws, dims[axis_at] // parts).reshape([-1 if axis == axis_at else 1 for axis in range(len(dims))])
    return level


def scatter_about(rng, dims, spread, bound, pieces=(), kind=jnp.bfloat16):
    drawn = jax.random.normal(rng, dims, jnp.float32) * spread
    if len(pieces) > 0:
        drawn = level_of(rng, dims, pieces, -0.22, 0.18) * drawn
    return jnp.clip(drawn, min=-bound, max=bound).astype(kind)


def setup_inputs(seed: int = 0) -> dict:
    key_list = jax.random.split(jax.random.key(seed), 7)
    valence_orbitals = scatter_about(key_list[0], (KPTS, VAL, 2, PLANE), 1.0, 6.0, ((3, 16),))
    conduction_orbitals = scatter_about(key_list[1], (KPTS, CON, 2, PLANE), 1.0, 6.0, ((3, 16),))
    screened = draw_screened(jax.random.fold_in(key_list[6], 71), 0)
    valence_index = plant(jax.random.randint(key_list[3], (TRANS,), 0, VAL), jax.random.fold_in(key_list[3], 1), 0, VAL - 1).astype(jnp.int32)
    conduction_index = plant(jax.random.randint(key_list[4], (TRANS,), 0, CON), jax.random.fold_in(key_list[4], 1), 0, CON - 1).astype(jnp.int32)
    kpoint_index = plant(jax.random.randint(key_list[5], (TRANS,), 0, KPTS), jax.random.fold_in(key_list[5], 1), 0, KPTS - 1).astype(jnp.int32)
    return {"valence_orbitals": valence_orbitals, "conduction_orbitals": conduction_orbitals, "screened": screened, "valence_index": valence_index, "conduction_index": conduction_index, "kpoint_index": kpoint_index}


def pair_density(valence_table, conduction_table, valence_pick, conduction_pick, kpoint_pick):
    valence_rows = valence_table[kpoint_pick, valence_pick].astype(jnp.float32)
    conduction_rows = conduction_table[kpoint_pick, conduction_pick].astype(jnp.float32)
    real_part = valence_rows[:, 0] * conduction_rows[:, 0] + valence_rows[:, 1] * conduction_rows[:, 1]
    imag_part = valence_rows[:, 0] * conduction_rows[:, 1] - valence_rows[:, 1] * conduction_rows[:, 0]
    return jnp.stack([real_part, imag_part], 1).astype(jnp.bfloat16)


def formed_blocks():
    blocks = STRIDE * SPAN
    half_span = SPAN // 2
    row_block = jnp.arange(blocks, dtype=jnp.int32)[:, None]
    col_block = jnp.arange(blocks, dtype=jnp.int32)[None, :]
    row_lane = row_block % STRIDE
    row_strip = row_block // STRIDE
    col_group = col_block // STRIDE
    col_lane = col_block % STRIDE
    distance = (col_group - row_strip) % SPAN
    return ((distance >= 1) & (distance < half_span)) | ((distance == 0) & (col_lane >= row_lane)) | ((distance == half_span) & (col_lane <= row_lane))


def reference(valence_orbitals, conduction_orbitals, screened, valence_index, conduction_index, kpoint_index):
    density = pair_density(valence_orbitals, conduction_orbitals, valence_index, conduction_index, kpoint_index)
    flat = density.reshape(TRANS, 2 * PLANE)
    w_real = screened[0]
    w_imag = screened[1]
    w_block = jnp.concatenate([jnp.concatenate([w_real, -w_imag], 1), jnp.concatenate([w_imag, w_real], 1)], 0)
    screened_pairs = lax.dot_general(w_block, flat, (((1,), (1,)), ((), ())), preferred_element_type=jnp.float32).astype(jnp.bfloat16)
    swapped = jnp.concatenate([screened_pairs[PLANE:], -screened_pairs[:PLANE]], 0)
    both_parts = jnp.concatenate([screened_pairs, swapped], 1)
    direct = jnp.dot(flat, both_parts, preferred_element_type=jnp.float32)
    direct_real = direct[:, :TRANS]
    direct_imag = direct[:, TRANS:]
    formed = jnp.repeat(jnp.repeat(formed_blocks(), FINE, 0), FINE, 1)
    kernel_real = jnp.where(formed, direct_real, direct_real.T)
    kernel_imag = jnp.where(formed, direct_imag, -direct_imag.T)
    return jnp.stack([kernel_real, kernel_imag]).reshape(2, SPAN, STRIDE * FINE, TRANS)
```

```python
import functools

import jax
import jax.numpy as jnp
from jax import lax
from jax.experimental import pallas as pl
from jax.experimental.pallas import tpu as pltpu
from jax.sharding import PartitionSpec as P

VAL = 48
CON = 64
FINE = 8
SLICE = 128
HALF = 64
KPAD = 256
VMEM = pltpu.CompilerParams(vmem_limit_bytes=48 * 1024 * 1024)


def lane_matrix(row):
    return jnp.broadcast_to(row.astype(jnp.float32), (128, 128)).T


def one_hot(index):
    lane = lax.broadcasted_iota(jnp.int32, index.shape, 1).astype(jnp.float32)
    low = jnp.where(index == lane, 1.0, 0.0)
    high = jnp.where(index == lane + 128.0, 1.0, 0.0)
    return jnp.concatenate([low, high], 1).astype(jnp.bfloat16)


def densities(valence, conduction):
    width = 2 * SLICE
    v_re, v_im = valence[:, :width], valence[:, width:]
    c_re, c_im = conduction[:, :width], conduction[:, width:]
    return v_re * c_re + v_im * c_im, v_re * c_im - v_im * c_re


def transition_rows(v_ref, n_ref, k_ref, start):
    v = v_ref[pl.ds(start, 1), :]
    n = n_ref[pl.ds(start, 1), :]
    k = k_ref[pl.ds(start, 1), :]
    return lane_matrix(k * VAL + v), lane_matrix(k * CON + n)


def pick(rows, parity, table):
    i = lax.broadcasted_iota(jnp.int32, (rows, table.shape[0]), 0)
    j = lax.broadcasted_iota(jnp.int32, (rows, table.shape[0]), 1)
    mask = jnp.where(j == 2 * i + parity, 1.0, 0.0).astype(jnp.bfloat16)
    return jnp.dot(mask, table, preferred_element_type=jnp.float32).astype(jnp.bfloat16)


def columns_kernel(own_ref, partner_ref, v_ref, n_ref, k_ref, table_ref, out_ref, held):
    core = lax.rem(lax.axis_index("row"), 2)
    column = lax.axis_index("col")
    split = 2 * VAL * 4
    both = jnp.concatenate([own_ref[...], partner_ref[...]], 1)
    for parity in range(2):
        lanes = pl.ds(parity * 2 * SLICE, 2 * SLICE)
        table_ref[0:KPAD, lanes] = pick(KPAD, parity, both[:split])
        table_ref[KPAD:, lanes] = pick(KPAD, parity, both[split:])
    v_at, c_at = transition_rows(v_ref, n_ref, k_ref, column)
    valence = jnp.dot(one_hot(v_at), table_ref[0:KPAD, :], preferred_element_type=jnp.float32)
    conduction = jnp.dot(one_hot(c_at), table_ref[KPAD:, :], preferred_element_type=jnp.float32)
    real, imag = densities(valence, conduction)
    held[0] = real
    held[1] = imag
    rows = pl.ds(pl.multiple_of(core * HALF, HALF), HALF)
    own = pl.ds(pl.multiple_of(core * SLICE, SLICE), SLICE)
    partner = pl.ds(pl.multiple_of((1 - core) * SLICE, SLICE), SLICE)
    for part in range(2):
        mine = held[part, rows, :].astype(jnp.bfloat16)
        for copy in range(out_ref.shape[0]):
            out_ref[copy, part * HALF : (part + 1) * HALF, own] = mine[:, :SLICE]
            out_ref[copy, part * HALF : (part + 1) * HALF, partner] = mine[:, SLICE:]


def direct_kernel(pairs_ref, own_ref, partner_ref, table_ref, v_ref, n_ref, k_ref, out_ref, screened):
    first = lax.broadcasted_iota(jnp.int32, (SLICE, 2 * HALF), 1) < HALF
    sign = jnp.where(first, -1.0, 1.0)
    width = pairs_ref.shape[2]
    for half, w_ref in enumerate((own_ref, partner_ref)):
        parts = []
        for part in range(2):
            total = jnp.zeros((SLICE, 2 * HALF), jnp.float32)
            for chip in range(pairs_ref.shape[0]):
                total += lax.dot_general(
                    w_ref[part, :, chip * width : (chip + 1) * width],
                    pairs_ref[chip],
                    (((1,), (1,)), ((), ())),
                    preferred_element_type=jnp.float32,
                )
            parts.append(total)
        x = (parts[0] + sign * pltpu.roll(parts[1], HALF, 1)).astype(jnp.bfloat16)
        screened[half * SLICE : (half + 1) * SLICE, :] = x
        x = x.astype(jnp.float32)
        turned = -sign * pltpu.roll(x, HALF, 1)
        screened[(2 + half) * SLICE : (3 + half) * SLICE, :] = turned.astype(jnp.bfloat16)

    strips = 4

    def step(m, carry):
        v_at, c_at = [], []
        for s in range(strips):
            v, c = transition_rows(v_ref, n_ref, k_ref, m * strips + s)
            v_at.append(v)
            c_at.append(c)
        valence = jnp.dot(one_hot(jnp.concatenate(v_at, 0)), table_ref[0:KPAD, :], preferred_element_type=jnp.float32)
        conduction = jnp.dot(one_hot(jnp.concatenate(c_at, 0)), table_ref[KPAD:, :], preferred_element_type=jnp.float32)
        density = jnp.concatenate(densities(valence, conduction), 1).astype(jnp.bfloat16)
        direct = jnp.dot(density, screened[...], preferred_element_type=jnp.float32)
        direct = direct.reshape(strips, 16, FINE, 2 * HALF)
        direct = jnp.concatenate([direct[s] for s in range(strips)], 1).astype(jnp.bfloat16)
        out_ref[:, pl.ds(pl.multiple_of(m * strips * FINE, strips * FINE), strips * FINE), :] = direct
        return carry

    lax.fori_loop(0, v_ref.shape[0] // strips, step, 0)


def total_kernel(in_ref, out_ref):
    first = lax.broadcasted_iota(jnp.int32, (in_ref.shape[1], 2 * HALF), 1) < HALF
    sums = []
    for core in range(2):
        total = in_ref[core].astype(jnp.float32)
        for chip in range(1, in_ref.shape[0] // 2):
            total += in_ref[2 * chip + core].astype(jnp.float32)
        sums.append(total)
    out_ref[0] = jnp.where(first, sums[0], pltpu.roll(sums[1], HALF, 1))
    out_ref[1] = jnp.where(first, pltpu.roll(sums[0], HALF, 1), sums[1])


def shards(valence_orbitals, conduction_orbitals, screened, valence_index, conduction_index, kpoint_index):
    rows = lax.axis_size("row")
    chips = rows // 2
    swap = [(i, i ^ 1) for i in range(rows)]
    same_core = [[2 * chip + core for chip in range(chips)] for core in range(2)]
    tables = jnp.concatenate(
        [valence_orbitals.reshape(-1, SLICE), conduction_orbitals.reshape(-1, SLICE)], 0
    )
    partner_tables = lax.ppermute(tables, "row", swap)
    partner_screened = lax.ppermute(screened, "row", swap)
    v = valence_index.reshape(-1, 128)
    n = conduction_index.reshape(-1, 128)
    k = kpoint_index.reshape(-1, 128)
    bf16 = jnp.bfloat16
    table, pairs = pl.pallas_call(
        columns_kernel,
        out_shape=(
            jax.ShapeDtypeStruct((2 * KPAD, 4 * SLICE), bf16),
            jax.ShapeDtypeStruct((chips, 2 * HALF, 2 * SLICE), bf16),
        ),
        scratch_shapes=[pltpu.VMEM((2, 128, 2 * SLICE), jnp.float32)],
        compiler_params=VMEM,
        name="columns",
    )(tables, partner_tables, v, n, k)
    pairs = lax.all_to_all(pairs, "row", 0, 0, axis_index_groups=same_core, tiled=True)
    partial = pl.pallas_call(
        direct_kernel,
        out_shape=jax.ShapeDtypeStruct((rows, v.shape[0] * FINE, 2 * HALF), bf16),
        scratch_shapes=[pltpu.VMEM((4 * SLICE, 2 * HALF), bf16)],
        compiler_params=VMEM,
        name="direct",
    )(pairs, screened, partner_screened, table, v, n, k)
    partial = lax.all_to_all(partial, "row", 0, 0, tiled=True)
    out = pl.pallas_call(
        total_kernel,
        out_shape=jax.ShapeDtypeStruct((2, partial.shape[1], 2 * HALF), jnp.float32),
        compiler_params=VMEM,
        name="total",
    )(partial)
    return out.reshape(2, v.shape[0], FINE, 2 * HALF)


def solution(mesh):
    in_specs = (
        P(None, None, None, "row"),
        P(None, None, None, "row"),
        P(None, "row", None),
        P(),
        P(),
        P(),
    )
    return jax.shard_map(
        shards, mesh=mesh, in_specs=in_specs, out_specs=P(None, None, "row", "col"), check_vma=False
    )
```

```python
import functools

import jax
import jax.numpy as jnp
from jax import lax
from jax.experimental import pallas as pl
from jax.experimental.pallas import tpu as pltpu
from jax.sharding import PartitionSpec as P

VAL = 48
CON = 64
FINE = 8
SLICE = 128
HALF = 64
KPAD = 256
STRIPS = 4
VMEM = pltpu.CompilerParams(vmem_limit_bytes=16 * 1024 * 1024)
MOST = pltpu.CompilerParams(vmem_limit_bytes=50 * 1024 * 1024)


def lane_matrix(row):
    return jnp.broadcast_to(row, (128, 128)).T


def one_hot(index):
    lane = lax.broadcasted_iota(jnp.int32, index.shape, 1).astype(jnp.float32)
    low = jnp.where(index == lane, 1.0, 0.0)
    high = jnp.where(index == lane + 128.0, 1.0, 0.0)
    return jnp.concatenate([low, high], 1).astype(jnp.bfloat16)


def densities(valence, conduction):
    width = 2 * SLICE
    v_re, v_im = valence[:, :width], valence[:, width:]
    c_re, c_im = conduction[:, :width], conduction[:, width:]
    return v_re * c_re + v_im * c_im, v_re * c_im - v_im * c_re


def transition_rows(at_ref, start):
    return lane_matrix(at_ref[0, pl.ds(start, 1), :]), lane_matrix(at_ref[1, pl.ds(start, 1), :])


def pick(rows, parity, table):
    i = lax.broadcasted_iota(jnp.int32, (rows, table.shape[0]), 0)
    j = lax.broadcasted_iota(jnp.int32, (rows, table.shape[0]), 1)
    mask = jnp.where(j == 2 * i + parity, 1.0, 0.0).astype(jnp.bfloat16)
    return jnp.dot(mask, table, preferred_element_type=jnp.float32).astype(jnp.bfloat16)


def columns_kernel(own_ref, partner_ref, at_ref, table_ref, out_ref, held):
    core = lax.rem(lax.axis_index("row"), 2)
    column = lax.axis_index("col")
    split = 2 * VAL * 4
    both = jnp.concatenate([own_ref[...], partner_ref[...]], 1)
    for parity in range(2):
        lanes = pl.ds(parity * 2 * SLICE, 2 * SLICE)
        table_ref[0:KPAD, lanes] = pick(KPAD, parity, both[:split])
        table_ref[KPAD:, lanes] = pick(KPAD, parity, both[split:])
    v_at, c_at = transition_rows(at_ref, column)
    valence = jnp.dot(one_hot(v_at), table_ref[0:KPAD, :], preferred_element_type=jnp.float32)
    conduction = jnp.dot(one_hot(c_at), table_ref[KPAD:, :], preferred_element_type=jnp.float32)
    real, imag = densities(valence, conduction)
    held[0] = real
    held[1] = imag
    rows = pl.ds(pl.multiple_of(core * HALF, HALF), HALF)
    own = pl.ds(pl.multiple_of(core * SLICE, SLICE), SLICE)
    partner = pl.ds(pl.multiple_of((1 - core) * SLICE, SLICE), SLICE)
    for part in range(2):
        mine = held[part, rows, :].astype(jnp.bfloat16)
        for copy in range(out_ref.shape[0]):
            out_ref[copy, part * HALF : (part + 1) * HALF, own] = mine[:, :SLICE]
            out_ref[copy, part * HALF : (part + 1) * HALF, partner] = mine[:, SLICE:]


def direct_kernel(pairs_ref, own_ref, partner_ref, density_ref, out_ref, screened):
    @pl.when(pl.program_id(0) == 0)
    def _():
        first = lax.broadcasted_iota(jnp.int32, (SLICE, 2 * HALF), 1) < HALF
        sign = jnp.where(first, -1.0, 1.0)
        width = pairs_ref.shape[2]
        for half, w_ref in enumerate((own_ref, partner_ref)):
            parts = []
            for part in range(2):
                total = jnp.zeros((SLICE, 2 * HALF), jnp.float32)
                for chip in range(pairs_ref.shape[0]):
                    total += lax.dot_general(
                        w_ref[part, :, chip * width : (chip + 1) * width],
                        pairs_ref[chip],
                        (((1,), (1,)), ((), ())),
                        preferred_element_type=jnp.float32,
                    )
                parts.append(total)
            x = (parts[0] + sign * pltpu.roll(parts[1], HALF, 1)).astype(jnp.bfloat16)
            screened[half * SLICE : (half + 1) * SLICE, :] = x
            x = x.astype(jnp.float32)
            turned = -sign * pltpu.roll(x, HALF, 1)
            screened[(2 + half) * SLICE : (3 + half) * SLICE, :] = turned.astype(jnp.bfloat16)

    direct = jnp.dot(density_ref[...], screened[...], preferred_element_type=jnp.float32)
    direct = direct.reshape(STRIPS, 16, FINE, 2 * HALF)
    out_ref[...] = jnp.concatenate([direct[s] for s in range(STRIPS)], 1).astype(jnp.bfloat16)


def rows_kernel(table_ref, at_ref, density_ref):
    v_at, c_at = [], []
    for s in range(STRIPS):
        v, c = transition_rows(at_ref, pl.program_id(0) * STRIPS + s)
        v_at.append(v)
        c_at.append(c)
    valence = jnp.dot(one_hot(jnp.concatenate(v_at, 0)), table_ref[0:KPAD, :], preferred_element_type=jnp.float32)
    conduction = jnp.dot(one_hot(jnp.concatenate(c_at, 0)), table_ref[KPAD:, :], preferred_element_type=jnp.float32)
    density_ref[...] = jnp.concatenate(densities(valence, conduction), 1).astype(jnp.bfloat16)


def total_kernel(in_ref, out_ref):
    first = lax.broadcasted_iota(jnp.int32, (in_ref.shape[1], 2 * HALF), 1) < HALF
    sums = []
    for core in range(2):
        total = in_ref[core].astype(jnp.float32)
        for chip in range(1, in_ref.shape[0] // 2):
            total += in_ref[2 * chip + core].astype(jnp.float32)
        sums.append(total)
    out_ref[0] = jnp.where(first, sums[0], pltpu.roll(sums[1], HALF, 1))
    out_ref[1] = jnp.where(first, pltpu.roll(sums[0], HALF, 1), sums[1])


def whole(array):
    return pl.BlockSpec(array.shape, lambda *_: (0,) * array.ndim)


def shards(valence_orbitals, conduction_orbitals, screened, valence_index, conduction_index, kpoint_index):
    rows = lax.axis_size("row")
    chips = rows // 2
    swap = [(i, i ^ 1) for i in range(rows)]
    same_core = [[2 * chip + core for chip in range(chips)] for core in range(2)]
    tables = jnp.concatenate(
        [valence_orbitals.reshape(-1, SLICE), conduction_orbitals.reshape(-1, SLICE)], 0
    )
    screened, tables = lax.optimization_barrier((screened, tables))
    partner_screened = lax.ppermute(screened, "row", swap)
    partner_tables = lax.ppermute(tables, "row", swap)
    at = jnp.stack([kpoint_index * VAL + valence_index, kpoint_index * CON + conduction_index])
    at = at.reshape(2, -1, 128).astype(jnp.float32)
    strips = at.shape[1]
    steps = strips // STRIPS
    bf16 = jnp.bfloat16
    table, pairs = pl.pallas_call(
        columns_kernel,
        out_shape=(
            jax.ShapeDtypeStruct((2 * KPAD, 4 * SLICE), bf16),
            jax.ShapeDtypeStruct((chips, 2 * HALF, 2 * SLICE), bf16),
        ),
        scratch_shapes=[pltpu.VMEM((2, 128, 2 * SLICE), jnp.float32)],
        compiler_params=VMEM,
        name="columns",
    )(tables, partner_tables, at)
    pairs = lax.all_to_all(pairs, "row", 0, 0, axis_index_groups=same_core, tiled=True)
    density = pl.pallas_call(
        rows_kernel,
        out_shape=jax.ShapeDtypeStruct((strips * 128, 4 * SLICE), bf16),
        grid=(steps,),
        in_specs=[whole(table), whole(at)],
        out_specs=pl.BlockSpec((STRIPS * 128, 4 * SLICE), lambda m: (m, 0)),
        compiler_params=VMEM,
        cost_estimate=pl.CostEstimate(
            flops=4 * strips * 128 * KPAD * 4 * SLICE, bytes_accessed=5 << 20, transcendentals=0
        ),
        name="rows",
    )(table, at)
    partial = pl.pallas_call(
        direct_kernel,
        out_shape=jax.ShapeDtypeStruct((rows, strips * FINE, 2 * HALF), bf16),
        grid=(steps,),
        in_specs=[
            whole(pairs),
            whole(screened),
            whole(partner_screened),
            pl.BlockSpec((STRIPS * 128, 4 * SLICE), lambda m: (m, 0)),
        ],
        out_specs=pl.BlockSpec((rows, STRIPS * FINE, 2 * HALF), lambda m: (0, m, 0)),
        scratch_shapes=[pltpu.VMEM((4 * SLICE, 2 * HALF), bf16)],
        compiler_params=MOST,
        name="direct",
    )(pairs, screened, partner_screened, density)
    partial = lax.all_to_all(partial, "row", 0, 0, tiled=True)
    out = pl.pallas_call(
        total_kernel,
        out_shape=jax.ShapeDtypeStruct((2, partial.shape[1], 2 * HALF), jnp.float32),
        compiler_params=VMEM,
        name="total",
    )(partial)
    return out.reshape(2, strips, FINE, 2 * HALF)


def solution(mesh):
    in_specs = (
        P(None, None, None, "row"),
        P(None, None, None, "row"),
        P(None, "row", None),
        P(),
        P(),
        P(),
    )
    return jax.shard_map(
        shards, mesh=mesh, in_specs=in_specs, out_specs=P(None, None, "row", "col"), check_vma=False
    )
```

```python
import functools

import jax
import jax.numpy as jnp
from jax import lax
from jax.experimental import pallas as pl
from jax.experimental.pallas import tpu as pltpu
from jax.sharding import PartitionSpec as P

VAL = 48
CON = 64
FINE = 8
SLICE = 128
HALF = 64
KPAD = 256
STRIPS = 8
VMEM = pltpu.CompilerParams(vmem_limit_bytes=16 * 1024 * 1024)
MOST = pltpu.CompilerParams(vmem_limit_bytes=50 * 1024 * 1024)


def lane_matrix(row):
    return jnp.broadcast_to(row, (128, 128)).T


def one_hot(index, width):
    lane = lax.broadcasted_iota(jnp.int32, index.shape, 1).astype(jnp.float32)
    parts = [jnp.where(index == lane + float(at), 1.0, 0.0) for at in range(0, width, index.shape[1])]
    return jnp.concatenate(parts, 1).astype(jnp.bfloat16)


def densities(valence, conduction):
    width = 2 * SLICE
    v_re, v_im = valence[:, :width], valence[:, width:]
    c_re, c_im = conduction[:, :width], conduction[:, width:]
    return v_re * c_re + v_im * c_im, v_re * c_im - v_im * c_re


def transition_rows(at_ref, start):
    return lane_matrix(at_ref[0, pl.ds(start, 1), :]), lane_matrix(at_ref[1, pl.ds(start, 1), :])


def pick(rows, parity, table):
    i = lax.broadcasted_iota(jnp.int32, (rows, table.shape[0]), 0)
    j = lax.broadcasted_iota(jnp.int32, (rows, table.shape[0]), 1)
    mask = jnp.where(j == 2 * i + parity, 1.0, 0.0).astype(jnp.bfloat16)
    return jnp.dot(mask, table, preferred_element_type=jnp.float32).astype(jnp.bfloat16)


def columns_kernel(own_ref, partner_ref, at_ref, out_ref, held):
    core = lax.rem(lax.axis_index("row"), 2)
    split = 2 * VAL * 4
    both = jnp.concatenate([own_ref[...], partner_ref[...]], 1)
    picked = []
    for index, table in zip(transition_rows(at_ref, lax.axis_index("col")), (both[:split], both[split:])):
        for parity in range(2):
            hot = one_hot(2.0 * index + parity, table.shape[0])
            picked.append(jnp.dot(hot, table, preferred_element_type=jnp.float32))
    v_re, v_im, c_re, c_im = picked
    real = (v_re * c_re + v_im * c_im).T
    imag = (v_re * c_im - v_im * c_re).T
    first = lax.broadcasted_iota(jnp.int32, real.shape, 1) < HALF
    held[0] = jnp.where(first, real, pltpu.roll(imag, HALF, 1))
    held[1] = jnp.where(first, pltpu.roll(real, HALF, 1), imag)
    mine = held[core].astype(jnp.bfloat16)
    own = pl.ds(pl.multiple_of(core * SLICE, SLICE), SLICE)
    partner = pl.ds(pl.multiple_of((1 - core) * SLICE, SLICE), SLICE)
    for copy in range(out_ref.shape[0]):
        out_ref[copy, own, :] = mine[:SLICE]
        out_ref[copy, partner, :] = mine[SLICE:]


def rows_kernel(own_ref, partner_ref, at_ref, density_ref, table):
    @pl.when(pl.program_id(0) == 0)
    def _():
        both = jnp.concatenate([own_ref[...], partner_ref[...]], 1)
        split = 2 * VAL * 4
        for parity in range(2):
            lanes = pl.ds(parity * 2 * SLICE, 2 * SLICE)
            table[0:KPAD, lanes] = pick(KPAD, parity, both[:split])
            table[KPAD:, lanes] = pick(KPAD, parity, both[split:])

    v_at, c_at = [], []
    for s in range(STRIPS):
        v, c = transition_rows(at_ref, pl.program_id(0) * STRIPS + s)
        v_at.append(v)
        c_at.append(c)
    valence = jnp.dot(one_hot(jnp.concatenate(v_at, 0), KPAD), table[0:KPAD, :], preferred_element_type=jnp.float32)
    conduction = jnp.dot(one_hot(jnp.concatenate(c_at, 0), KPAD), table[KPAD:, :], preferred_element_type=jnp.float32)
    density_ref[...] = jnp.concatenate(densities(valence, conduction), 1).astype(jnp.bfloat16)


def direct_kernel(pairs_ref, own_ref, partner_ref, density_ref, out_ref, held, screened, sems):
    steps, strip = held.shape[:2]
    copies = []
    for m in range(steps):
        span = pl.ds(m * strip, strip)
        copies.append(pltpu.make_async_copy(density_ref.at[span, :], held.at[m], sems.at[m]))
    for copy in copies:
        copy.start()
    first = lax.broadcasted_iota(jnp.int32, (SLICE, 2 * HALF), 1) < HALF
    sign = jnp.where(first, -1.0, 1.0)
    pairs = pairs_ref[...].reshape(-1, 2 * HALF)
    for half, w_ref in enumerate((own_ref, partner_ref)):
        parts = [jnp.dot(w_ref[part], pairs, preferred_element_type=jnp.float32) for part in range(2)]
        x = (parts[0] + sign * pltpu.roll(parts[1], HALF, 1)).astype(jnp.bfloat16)
        screened[half * SLICE : (half + 1) * SLICE, :] = x
        turned = -sign * pltpu.roll(x.astype(jnp.float32), HALF, 1)
        screened[(2 + half) * SLICE : (3 + half) * SLICE, :] = turned.astype(jnp.bfloat16)
    lanes = strip // 16
    for m, copy in enumerate(copies):
        copy.wait()
        direct = jnp.dot(held[m], screened[...], preferred_element_type=jnp.float32)
        direct = direct.reshape(strip // 128, 16, FINE, 2 * HALF)
        direct = jnp.concatenate([direct[s] for s in range(strip // 128)], 1).astype(jnp.bfloat16)
        out_ref[:, m * lanes : (m + 1) * lanes, :] = direct


def total_kernel(in_ref, out_ref):
    first = lax.broadcasted_iota(jnp.int32, (in_ref.shape[1], 2 * HALF), 1) < HALF
    sums = []
    for core in range(2):
        total = in_ref[core].astype(jnp.float32)
        for chip in range(1, in_ref.shape[0] // 2):
            total += in_ref[2 * chip + core].astype(jnp.float32)
        sums.append(total)
    out_ref[0] = jnp.where(first, sums[0], pltpu.roll(sums[1], HALF, 1))
    out_ref[1] = jnp.where(first, pltpu.roll(sums[0], HALF, 1), sums[1])


def whole(array):
    return pl.BlockSpec(array.shape, lambda *_: (0,) * array.ndim)


def shards(valence_orbitals, conduction_orbitals, screened, valence_index, conduction_index, kpoint_index):
    rows = lax.axis_size("row")
    chips = rows // 2
    swap = [(i, i ^ 1) for i in range(rows)]
    same_core = [[2 * chip + core for chip in range(chips)] for core in range(2)]
    tables = jnp.concatenate(
        [valence_orbitals.reshape(-1, SLICE), conduction_orbitals.reshape(-1, SLICE)], 0
    )
    screened, tables = lax.optimization_barrier((screened, tables))
    partner_screened = lax.ppermute(screened, "row", swap)
    partner_tables = lax.ppermute(tables, "row", swap)
    at = jnp.stack([kpoint_index * VAL + valence_index, kpoint_index * CON + conduction_index])
    at = at.reshape(2, -1, 128).astype(jnp.float32)
    strips = at.shape[1]
    steps = strips // STRIPS
    bf16 = jnp.bfloat16
    pairs = pl.pallas_call(
        columns_kernel,
        out_shape=jax.ShapeDtypeStruct((chips, 2 * SLICE, 2 * HALF), bf16),
        scratch_shapes=[pltpu.VMEM((2, 2 * SLICE, 2 * HALF), jnp.float32)],
        compiler_params=VMEM,
        name="columns",
    )(tables, partner_tables, at)
    pairs = lax.all_to_all(pairs, "row", 0, 0, axis_index_groups=same_core, tiled=True)
    density = pl.pallas_call(
        rows_kernel,
        out_shape=jax.ShapeDtypeStruct((strips * 128, 4 * SLICE), bf16),
        grid=(steps,),
        in_specs=[whole(tables), whole(partner_tables), whole(at)],
        out_specs=pl.BlockSpec((STRIPS * 128, 4 * SLICE), lambda m: (m, 0)),
        scratch_shapes=[pltpu.VMEM((2 * KPAD, 4 * SLICE), bf16)],
        compiler_params=VMEM,
        cost_estimate=pl.CostEstimate(
            flops=4 * strips * 128 * KPAD * 4 * SLICE, bytes_accessed=5 << 20, transcendentals=0
        ),
        name="rows",
    )(tables, partner_tables, at)
    partial = pl.pallas_call(
        direct_kernel,
        out_shape=jax.ShapeDtypeStruct((rows, strips * FINE, 2 * HALF), bf16),
        in_specs=[pl.BlockSpec(memory_space=pltpu.VMEM)] * 3 + [pl.BlockSpec(memory_space=pl.ANY)],
        scratch_shapes=[
            pltpu.VMEM((steps, STRIPS * 128, 4 * SLICE), bf16),
            pltpu.VMEM((4 * SLICE, 2 * HALF), bf16),
            pltpu.SemaphoreType.DMA((steps,)),
        ],
        compiler_params=MOST,
        name="direct",
    )(pairs, screened, partner_screened, density)
    partial = lax.all_to_all(partial, "row", 0, 0, tiled=True)
    out = pl.pallas_call(
        total_kernel,
        out_shape=jax.ShapeDtypeStruct((2, partial.shape[1], 2 * HALF), jnp.float32),
        compiler_params=VMEM,
        name="total",
    )(partial)
    return out.reshape(2, strips, FINE, 2 * HALF)


def solution(mesh):
    in_specs = (
        P(None, None, None, "row"),
        P(None, None, None, "row"),
        P(None, "row", None),
        P(),
        P(),
        P(),
    )
    return jax.shard_map(
        shards, mesh=mesh, in_specs=in_specs, out_specs=P(None, None, "row", "col"), check_vma=False
    )
```

```python
import jax
import jax.numpy as jnp
from jax import lax
from jax.experimental import pallas as pl
from jax.experimental.pallas import tpu as pltpu
from jax.sharding import PartitionSpec as P

VAL = 48
CON = 64
FINE = 8
SLICE = 128
WIDTH = 128
KPAD = 256
RING = (0, 1, 2, 3, 7, 6, 5, 4)
STRIPS = 16
MIB = 1024 * 1024
LITTLE = pltpu.CompilerParams(vmem_limit_bytes=16 * MIB)
MUCH = pltpu.CompilerParams(vmem_limit_bytes=48 * MIB)
ALL = pltpu.CompilerParams(vmem_limit_bytes=63 * MIB)


def core_of():
    return lax.rem(lax.axis_index("row"), 2)


def lane_matrix(row):
    return jnp.broadcast_to(row, (128, 128)).T


def one_hot(index, width):
    lane = lax.broadcasted_iota(jnp.int32, index.shape, 1).astype(jnp.float32)
    parts = [jnp.where(index == lane + float(at), 1.0, 0.0) for at in range(0, width, index.shape[1])]
    return jnp.concatenate(parts, 1).astype(jnp.bfloat16)


def densities(valence, conduction):
    width = valence.shape[1] // 2
    v_re, v_im = valence[:, :width], valence[:, width:]
    c_re, c_im = conduction[:, :width], conduction[:, width:]
    return v_re * c_re + v_im * c_im, v_re * c_im - v_im * c_re


def pick(rows, parity, table):
    i = lax.broadcasted_iota(jnp.int32, (rows, table.shape[0]), 0)
    j = lax.broadcasted_iota(jnp.int32, (rows, table.shape[0]), 1)
    mask = jnp.where(j == 2 * i + parity, 1.0, 0.0).astype(jnp.bfloat16)
    return jnp.dot(mask, table, preferred_element_type=jnp.float32).astype(jnp.bfloat16)


def columns_kernel(
    valence_ref, conduction_ref, v_ref, n_ref, k_ref, w_ref, at_ref, table_ref, out_ref, re_ref, im_ref, sems
):
    core = core_of()
    copies = []
    for part, ref in enumerate((re_ref, im_ref)):
        for place, chip in enumerate(RING):
            lanes = pl.ds(pl.multiple_of((2 * chip + 1 - core) * SLICE, SLICE), SLICE)
            to = ref.at[:, place * SLICE : (place + 1) * SLICE]
            copies.append(pltpu.make_async_copy(w_ref.at[part, :, lanes], to, sems.at[part, place]))
    for copy in copies:
        copy.start()
    split = valence_ref.shape[0]
    table_ref[0:split, :] = valence_ref[...]
    table_ref[split:, :] = conduction_ref[...]
    at_ref[0] = (k_ref[...] * VAL + v_ref[...]).astype(jnp.float32)
    at_ref[1] = (k_ref[...] * CON + n_ref[...]).astype(jnp.float32)
    picked = []
    for which, ref in enumerate((valence_ref, conduction_ref)):
        index = lane_matrix(at_ref[which, pl.ds(lax.axis_index("col"), 1), :])
        parts = []
        for parity in range(2):
            hot = one_hot(2.0 * index + parity, ref.shape[0])
            parts.append(jnp.dot(hot, ref[...], preferred_element_type=jnp.float32))
        picked.append(jnp.concatenate(parts, 1))
    real, imag = densities(*picked)
    both = jnp.concatenate([real.T, imag.T], 1).astype(jnp.bfloat16)
    for place in range(out_ref.shape[0]):
        out_ref[place] = both
    for copy in copies:
        copy.wait()


def rows_kernel(own_ref, partner_ref, at_ref, density_ref, table):
    core = core_of()

    @pl.when(pl.program_id(0) == 0)
    def _():
        both = jnp.concatenate([own_ref[...], partner_ref[...]], 1)
        split = 2 * VAL * 4
        for parity in range(2):
            lanes = pl.ds(parity * 2 * SLICE, 2 * SLICE)
            table[0:KPAD, lanes] = pick(KPAD, parity, both[:split])
            table[KPAD:, lanes] = pick(KPAD, parity, both[split:])

    picked = []
    for which in range(2):
        index = []
        for s in range(STRIPS):
            strip = lane_matrix(at_ref[which, pl.ds(pl.program_id(0) * STRIPS + s, 1), :]).reshape(-1, 2, FINE, 128)
            index.append(jnp.where(core == 0, strip[:, 0], strip[:, 1]).reshape(-1, 128))
        hot = one_hot(jnp.concatenate(index, 0), KPAD)
        picked.append(
            jnp.dot(hot, table[which * KPAD : (which + 1) * KPAD, :], preferred_element_type=jnp.float32)
        )
    density_ref[...] = jnp.concatenate(densities(*picked), 1).astype(jnp.bfloat16)


def screened_kernel(pairs_ref, own_ref, re_ref, im_ref, density_ref, out_ref, near_ref, sem):
    core = core_of()
    copy = pltpu.make_async_copy(density_ref, near_ref, sem)
    copy.start()
    for half in range(2):
        parts = []
        for part in range(2):
            total = jnp.zeros((SLICE, 2 * WIDTH), jnp.float32)
            for place, chip in enumerate(RING):
                if half == 0:
                    w = own_ref[part, :, pl.ds(pl.multiple_of((2 * chip + core) * SLICE, SLICE), SLICE)]
                else:
                    w = (re_ref, im_ref)[part][:, place * SLICE : (place + 1) * SLICE]
                total += jnp.dot(w, pairs_ref[place], preferred_element_type=jnp.float32)
            parts.append(total)
        out_ref[half, :, :WIDTH] = parts[0][:, :WIDTH] - parts[1][:, WIDTH:]
        out_ref[half, :, WIDTH:] = parts[0][:, WIDTH:] + parts[1][:, :WIDTH]
    copy.wait()


def direct_kernel(mine_ref, other_ref, density_ref, out_ref, screened):
    for half in range(2):
        x = (mine_ref[half] + other_ref[1 - half]).astype(jnp.bfloat16)
        screened[half * SLICE : (half + 1) * SLICE, :] = x
        screened[(2 + half) * SLICE : (3 + half) * SLICE, :WIDTH] = x[:, WIDTH:]
        screened[(2 + half) * SLICE : (3 + half) * SLICE, WIDTH:] = -x[:, :WIDTH]
    parts = 4
    rows = density_ref.shape[0] // parts
    strips = rows // 64
    for m in range(parts):
        direct = jnp.dot(
            density_ref[m * rows : (m + 1) * rows, :], screened[...], preferred_element_type=jnp.float32
        )
        direct = direct.reshape(strips, -1, FINE, 2 * WIDTH)
        direct = jnp.concatenate([direct[s] for s in range(strips)], 1).astype(jnp.bfloat16)
        for place, chip in enumerate(RING):
            out_ref[place, m * strips * FINE : (m + 1) * strips * FINE, :] = direct[chip]


def total_kernel(in_ref, out_ref):
    for part in range(2):
        lanes = slice(part * WIDTH, (part + 1) * WIDTH)
        total = in_ref[0, :, lanes].astype(jnp.float32)
        for chip in range(1, in_ref.shape[0]):
            total += in_ref[chip, :, lanes].astype(jnp.float32)
        out_ref[part] = total


def whole(array):
    return pl.BlockSpec(array.shape, lambda *_: (0,) * len(array.shape))


def shards(valence_orbitals, conduction_orbitals, screened, valence_index, conduction_index, kpoint_index):
    bf16, f32 = jnp.bfloat16, jnp.float32
    rows = lax.axis_size("row")
    chips = rows // 2
    swap = [(i, i ^ 1) for i in range(rows)]
    same_core = [[2 * chip + core for chip in RING] for core in range(2)]
    anywhere = pl.BlockSpec(memory_space=pl.ANY)
    in_vmem = pl.BlockSpec(memory_space=pltpu.VMEM)
    index = [array.reshape(-1, 128) for array in (valence_index, conduction_index, kpoint_index)]
    strips = index[0].shape[0]
    valence = valence_orbitals.reshape(-1, SLICE)
    conduction = conduction_orbitals.reshape(-1, SLICE)
    raw = (valence, conduction, *index)
    shapes = (
        jax.ShapeDtypeStruct((2, strips, 128), f32),
        jax.ShapeDtypeStruct((valence.shape[0] + conduction.shape[0], SLICE), bf16),
        jax.ShapeDtypeStruct((chips, SLICE, 2 * WIDTH), bf16),
    )
    half_w = jax.ShapeDtypeStruct((SLICE, chips * SLICE), bf16)
    at, tables, pairs, w_re, w_im = pl.pallas_call(
        columns_kernel,
        out_shape=(*shapes, half_w, half_w),
        grid=(1,),
        in_specs=[whole(array) for array in raw] + [anywhere],
        out_specs=(*[whole(array) for array in shapes], anywhere, anywhere),
        scratch_shapes=[pltpu.SemaphoreType.DMA((2, chips))],
        compiler_params=ALL,
        name="columns",
    )(*raw, screened)
    pairs = lax.all_to_all(pairs, "row", 0, 0, axis_index_groups=same_core, tiled=True)
    partner_tables = lax.ppermute(tables, "row", swap)
    w_re = lax.ppermute(w_re, "row", swap)
    w_im = lax.ppermute(w_im, "row", swap)
    density = pl.pallas_call(
        rows_kernel,
        out_shape=jax.ShapeDtypeStruct((strips * 64, 4 * SLICE), bf16),
        grid=(strips // STRIPS,),
        in_specs=[whole(tables), whole(partner_tables), whole(at)],
        out_specs=pl.BlockSpec((STRIPS * 64, 4 * SLICE), lambda m: (m, 0)),
        scratch_shapes=[pltpu.VMEM((2 * KPAD, 4 * SLICE), bf16)],
        compiler_params=LITTLE,
        cost_estimate=pl.CostEstimate(
            flops=4 * strips * 64 * KPAD * 4 * SLICE, bytes_accessed=3 << 20, transcendentals=0
        ),
        name="rows",
    )(tables, partner_tables, at)
    pairs, density = lax.optimization_barrier((pairs, density))
    mine, density = pl.pallas_call(
        screened_kernel,
        out_shape=(
            jax.ShapeDtypeStruct((2, SLICE, 2 * WIDTH), f32),
            jax.ShapeDtypeStruct(density.shape, bf16),
        ),
        in_specs=[in_vmem] * 4 + [anywhere],
        scratch_shapes=[pltpu.SemaphoreType.DMA],
        compiler_params=MUCH,
        name="screened",
    )(pairs, screened, w_re, w_im, density)
    other = lax.ppermute(mine, "row", swap)
    partial = pl.pallas_call(
        direct_kernel,
        out_shape=jax.ShapeDtypeStruct((chips, strips * FINE, 2 * WIDTH), bf16),
        scratch_shapes=[pltpu.VMEM((4 * SLICE, 2 * WIDTH), bf16)],
        compiler_params=LITTLE,
        name="direct",
    )(mine, other, density)
    partial = lax.all_to_all(partial, "row", 0, 0, axis_index_groups=same_core, tiled=True)
    out = pl.pallas_call(
        total_kernel,
        out_shape=jax.ShapeDtypeStruct((2, strips * FINE, WIDTH), f32),
        compiler_params=LITTLE,
        name="total",
    )(partial)
    return out.reshape(2, strips, FINE, WIDTH)


def solution(mesh):
    in_specs = (
        P(None, None, None, "row"),
        P(None, None, None, "row"),
        P(None, "row", None),
        P(),
        P(),
        P(),
    )
    return jax.shard_map(
        shards, mesh=mesh, in_specs=in_specs, out_specs=P(None, None, "row", "col"), check_vma=False
    )
```

```python
import jax
import jax.numpy as jnp
from jax import lax
from jax.experimental import pallas as pl
from jax.experimental.pallas import tpu as pltpu
from jax.sharding import PartitionSpec as P

VAL = 48
CON = 64
FINE = 8
SLICE = 128
WIDTH = 128
KPAD = 256
RING = (0, 1, 2, 3, 7, 6, 5, 4)
STRIPS = 16
MIB = 1024 * 1024
LITTLE = pltpu.CompilerParams(vmem_limit_bytes=16 * MIB)
MUCH = pltpu.CompilerParams(vmem_limit_bytes=48 * MIB)
ALL = pltpu.CompilerParams(vmem_limit_bytes=63 * MIB)


def core_of():
    return lax.rem(lax.axis_index("row"), 2)


def lane_matrix(row):
    return jnp.broadcast_to(row, (128, 128)).T


def one_hot(index, width):
    lane = lax.broadcasted_iota(jnp.int32, index.shape, 1).astype(jnp.float32)
    parts = [jnp.where(index == lane + float(at), 1.0, 0.0) for at in range(0, width, index.shape[1])]
    return jnp.concatenate(parts, 1).astype(jnp.bfloat16)


def densities(valence, conduction):
    width = valence.shape[1] // 2
    v_re, v_im = valence[:, :width], valence[:, width:]
    c_re, c_im = conduction[:, :width], conduction[:, width:]
    return v_re * c_re + v_im * c_im, v_re * c_im - v_im * c_re


def pick(rows, parity, table):
    i = lax.broadcasted_iota(jnp.int32, (rows, table.shape[0]), 0)
    j = lax.broadcasted_iota(jnp.int32, (rows, table.shape[0]), 1)
    mask = jnp.where(j == 2 * i + parity, 1.0, 0.0).astype(jnp.bfloat16)
    return jnp.dot(mask, table, preferred_element_type=jnp.float32).astype(jnp.bfloat16)


def columns_kernel(
    valence_ref, conduction_ref, v_ref, n_ref, k_ref, w_ref, at_ref, table_ref, out_ref, re_ref, im_ref, sems
):
    core = core_of()
    copies = []
    for part, ref in enumerate((re_ref, im_ref)):
        for place, chip in enumerate(RING):
            lanes = pl.ds(pl.multiple_of((2 * chip + 1 - core) * SLICE, SLICE), SLICE)
            to = ref.at[:, place * SLICE : (place + 1) * SLICE]
            copies.append(pltpu.make_async_copy(w_ref.at[part, :, lanes], to, sems.at[part, place]))
    for copy in copies:
        copy.start()
    split = valence_ref.shape[0]
    table_ref[0:split, :] = valence_ref[...]
    table_ref[split:, :] = conduction_ref[...]
    at_ref[0] = (k_ref[...] * VAL + v_ref[...]).astype(jnp.float32)
    at_ref[1] = (k_ref[...] * CON + n_ref[...]).astype(jnp.float32)
    picked = []
    for which, ref in enumerate((valence_ref, conduction_ref)):
        index = lane_matrix(at_ref[which, pl.ds(lax.axis_index("col"), 1), :])
        parts = []
        for parity in range(2):
            hot = one_hot(2.0 * index + parity, ref.shape[0])
            parts.append(jnp.dot(hot, ref[...], preferred_element_type=jnp.float32))
        picked.append(jnp.concatenate(parts, 1))
    real, imag = densities(*picked)
    both = jnp.concatenate([real.T, imag.T], 1).astype(jnp.bfloat16)
    for place in range(out_ref.shape[0]):
        out_ref[place] = both
    for copy in copies:
        copy.wait()


def rows_kernel(own_ref, partner_ref, at_ref, density_ref, table):
    core = core_of()

    @pl.when(pl.program_id(0) == 0)
    def _():
        both = jnp.concatenate([own_ref[...], partner_ref[...]], 1)
        split = 2 * VAL * 4
        for parity in range(2):
            lanes = pl.ds(parity * 2 * SLICE, 2 * SLICE)
            table[0:KPAD, lanes] = pick(KPAD, parity, both[:split])
            table[KPAD:, lanes] = pick(KPAD, parity, both[split:])

    picked = []
    for which in range(2):
        index = []
        for s in range(STRIPS):
            strip = lane_matrix(at_ref[which, pl.ds(pl.program_id(0) * STRIPS + s, 1), :]).reshape(-1, 2, FINE, 128)
            index.append(jnp.where(core == 0, strip[:, 0], strip[:, 1]).reshape(-1, 128))
        hot = one_hot(jnp.concatenate(index, 0), KPAD)
        picked.append(
            jnp.dot(hot, table[which * KPAD : (which + 1) * KPAD, :], preferred_element_type=jnp.float32)
        )
    density_ref[...] = jnp.concatenate(densities(*picked), 1).astype(jnp.bfloat16)


def screened_kernel(pairs_ref, own_ref, re_ref, im_ref, density_ref, out_ref, near_ref, sem):
    core = core_of()
    copy = pltpu.make_async_copy(density_ref, near_ref, sem)
    copy.start()
    for half in range(2):
        parts = []
        for part in range(2):
            total = jnp.zeros((SLICE, 2 * WIDTH), jnp.float32)
            for place, chip in enumerate(RING):
                if half == 0:
                    w = own_ref[part, :, pl.ds(pl.multiple_of((2 * chip + core) * SLICE, SLICE), SLICE)]
                else:
                    w = (re_ref, im_ref)[part][:, place * SLICE : (place + 1) * SLICE]
                total += jnp.dot(w, pairs_ref[place], preferred_element_type=jnp.float32)
            parts.append(total)
        out_ref[half, :, :WIDTH] = parts[0][:, :WIDTH] - parts[1][:, WIDTH:]
        out_ref[half, :, WIDTH:] = parts[0][:, WIDTH:] + parts[1][:, :WIDTH]
    copy.wait()


def direct_kernel(mine_ref, other_ref, density_ref, out_ref, screened):
    for half in range(2):
        x = (mine_ref[half] + other_ref[1 - half]).astype(jnp.bfloat16)
        screened[half * SLICE : (half + 1) * SLICE, :] = x
        screened[(2 + half) * SLICE : (3 + half) * SLICE, :WIDTH] = x[:, WIDTH:]
        screened[(2 + half) * SLICE : (3 + half) * SLICE, WIDTH:] = -x[:, :WIDTH]
    parts = 4
    rows = density_ref.shape[0] // parts
    strips = rows // 64
    for m in range(parts):
        direct = jnp.dot(
            density_ref[m * rows : (m + 1) * rows, :], screened[...], preferred_element_type=jnp.float32
        )
        direct = direct.reshape(strips, -1, FINE, 2 * WIDTH)
        direct = jnp.concatenate([direct[s] for s in range(strips)], 1).astype(jnp.bfloat16)
        for place, chip in enumerate(RING):
            out_ref[place, m * strips * FINE : (m + 1) * strips * FINE, :] = direct[chip]


def total_kernel(in_ref, out_ref):
    for part in range(2):
        lanes = slice(part * WIDTH, (part + 1) * WIDTH)
        total = in_ref[0, :, lanes].astype(jnp.float32)
        for chip in range(1, in_ref.shape[0]):
            total += in_ref[chip, :, lanes].astype(jnp.float32)
        out_ref[part] = total


def whole(array):
    return pl.BlockSpec(array.shape, lambda *_: (0,) * len(array.shape))


def shards(valence_orbitals, conduction_orbitals, screened, valence_index, conduction_index, kpoint_index):
    bf16, f32 = jnp.bfloat16, jnp.float32
    rows = lax.axis_size("row")
    chips = rows // 2
    swap = [(i, i ^ 1) for i in range(rows)]
    same_core = [[2 * chip + core for chip in RING] for core in range(2)]
    anywhere = pl.BlockSpec(memory_space=pl.ANY)
    in_vmem = pl.BlockSpec(memory_space=pltpu.VMEM)
    index = [array.reshape(-1, 128) for array in (valence_index, conduction_index, kpoint_index)]
    strips = index[0].shape[0]
    valence = valence_orbitals.reshape(-1, SLICE)
    conduction = conduction_orbitals.reshape(-1, SLICE)
    raw = (valence, conduction, *index)
    shapes = (
        jax.ShapeDtypeStruct((2, strips, 128), f32),
        jax.ShapeDtypeStruct((valence.shape[0] + conduction.shape[0], SLICE), bf16),
        jax.ShapeDtypeStruct((chips, SLICE, 2 * WIDTH), bf16),
    )
    half_w = jax.ShapeDtypeStruct((SLICE, chips * SLICE), bf16)
    at, tables, pairs, w_re, w_im = pl.pallas_call(
        columns_kernel,
        out_shape=(*shapes, half_w, half_w),
        grid=(1,),
        in_specs=[whole(array) for array in raw] + [anywhere],
        out_specs=tuple(whole(array) for array in (*shapes, half_w, half_w)),
        scratch_shapes=[pltpu.SemaphoreType.DMA((2, chips))],
        compiler_params=ALL,
        name="columns",
    )(*raw, screened)
    pairs = lax.all_to_all(pairs, "row", 0, 0, axis_index_groups=same_core, tiled=True)
    partner_tables = lax.ppermute(tables, "row", swap)
    w_re = lax.ppermute(w_re, "row", swap)
    w_im = lax.ppermute(w_im, "row", swap)
    density = pl.pallas_call(
        rows_kernel,
        out_shape=jax.ShapeDtypeStruct((strips * 64, 4 * SLICE), bf16),
        grid=(strips // STRIPS,),
        in_specs=[whole(tables), whole(partner_tables), whole(at)],
        out_specs=pl.BlockSpec((STRIPS * 64, 4 * SLICE), lambda m: (m, 0)),
        scratch_shapes=[pltpu.VMEM((2 * KPAD, 4 * SLICE), bf16)],
        compiler_params=LITTLE,
        cost_estimate=pl.CostEstimate(
            flops=4 * strips * 64 * KPAD * 4 * SLICE, bytes_accessed=3 << 20, transcendentals=0
        ),
        name="rows",
    )(tables, partner_tables, at)
    pairs, density = lax.optimization_barrier((pairs, density))
    mine, density = pl.pallas_call(
        screened_kernel,
        out_shape=(
            jax.ShapeDtypeStruct((2, SLICE, 2 * WIDTH), f32),
            jax.ShapeDtypeStruct(density.shape, bf16),
        ),
        in_specs=[in_vmem] * 4 + [anywhere],
        scratch_shapes=[pltpu.SemaphoreType.DMA],
        compiler_params=MUCH,
        name="screened",
    )(pairs, screened, w_re, w_im, density)
    other = lax.ppermute(mine, "row", swap)
    partial = pl.pallas_call(
        direct_kernel,
        out_shape=jax.ShapeDtypeStruct((chips, strips * FINE, 2 * WIDTH), bf16),
        scratch_shapes=[pltpu.VMEM((4 * SLICE, 2 * WIDTH), bf16)],
        compiler_params=LITTLE,
        name="direct",
    )(mine, other, density)
    partial = lax.all_to_all(partial, "row", 0, 0, axis_index_groups=same_core, tiled=True)
    out = pl.pallas_call(
        total_kernel,
        out_shape=jax.ShapeDtypeStruct((2, strips * FINE, WIDTH), f32),
        compiler_params=LITTLE,
        name="total",
    )(partial)
    return out.reshape(2, strips, FINE, WIDTH)


def solution(mesh):
    in_specs = (
        P(None, None, None, "row"),
        P(None, None, None, "row"),
        P(None, "row", None),
        P(),
        P(),
        P(),
    )
    return jax.shard_map(
        shards, mesh=mesh, in_specs=in_specs, out_specs=P(None, None, "row", "col"), check_vma=False
    )
```

```python
import jax
import jax.numpy as jnp
from jax import lax
from jax.experimental import pallas as pl
from jax.experimental.pallas import tpu as pltpu
from jax.sharding import PartitionSpec as P

VAL = 48
CON = 64
FINE = 8
SLICE = 128
WIDTH = 128
KPAD = 256
RING = (0, 1, 2, 3, 7, 6, 5, 4)
STRIPS = 16
MIB = 1024 * 1024
LITTLE = pltpu.CompilerParams(vmem_limit_bytes=16 * MIB)
MUCH = pltpu.CompilerParams(vmem_limit_bytes=52 * MIB)
ALL = pltpu.CompilerParams(vmem_limit_bytes=63 * MIB)


def core_of():
    return lax.rem(lax.axis_index("row"), 2)


def lane_matrix(row):
    return jnp.broadcast_to(row, (128, 128)).T


def one_hot(index, width):
    lane = lax.broadcasted_iota(jnp.int32, index.shape, 1).astype(jnp.float32)
    parts = [jnp.where(index == lane + float(at), 1.0, 0.0) for at in range(0, width, index.shape[1])]
    return jnp.concatenate(parts, 1).astype(jnp.bfloat16)


def densities(valence, conduction):
    width = valence.shape[1] // 2
    v_re, v_im = valence[:, :width], valence[:, width:]
    c_re, c_im = conduction[:, :width], conduction[:, width:]
    return v_re * c_re + v_im * c_im, v_re * c_im - v_im * c_re


def pick(rows, parity, table):
    i = lax.broadcasted_iota(jnp.int32, (rows, table.shape[0]), 0)
    j = lax.broadcasted_iota(jnp.int32, (rows, table.shape[0]), 1)
    mask = jnp.where(j == 2 * i + parity, 1.0, 0.0).astype(jnp.bfloat16)
    return jnp.dot(mask, table, preferred_element_type=jnp.float32).astype(jnp.bfloat16)


def columns_kernel(
    valence_ref, conduction_ref, v_ref, n_ref, k_ref, w_ref, table_ref, out_ref, re_ref, im_ref, sems
):
    core = core_of()
    copies = []
    for part, ref in enumerate((re_ref, im_ref)):
        for place, chip in enumerate(RING):
            lanes = pl.ds(pl.multiple_of((2 * chip + 1 - core) * SLICE, SLICE), SLICE)
            to = ref.at[:, place * SLICE : (place + 1) * SLICE]
            copies.append(pltpu.make_async_copy(w_ref.at[part, :, lanes], to, sems.at[part, place]))
    for copy in copies:
        copy.start()
    bands = valence_ref.shape[0] + conduction_ref.shape[0]
    strips = v_ref.shape[0]
    table_ref[0 : valence_ref.shape[0], :] = valence_ref[...]
    table_ref[valence_ref.shape[0] : bands, :] = conduction_ref[...]
    picked = []
    for which, (index_ref, count, ref) in enumerate(((v_ref, VAL, valence_ref), (n_ref, CON, conduction_ref))):
        place = bands + which * strips
        table_ref[place : place + strips, :] = (
            (k_ref[...] * count + index_ref[...]).astype(jnp.float32).astype(jnp.bfloat16)
        )
        own = pl.ds(lax.axis_index("col"), 1)
        index = lane_matrix((k_ref[own, :] * count + index_ref[own, :]).astype(jnp.float32))
        parts = []
        for parity in range(2):
            hot = one_hot(2.0 * index + parity, ref.shape[0])
            parts.append(jnp.dot(hot, ref[...], preferred_element_type=jnp.float32))
        picked.append(jnp.concatenate(parts, 1))
    real, imag = densities(*picked)
    both = jnp.concatenate([real.T, imag.T], 1).astype(jnp.bfloat16)
    for place in range(out_ref.shape[0]):
        out_ref[place] = both
    for copy in copies:
        copy.wait()


def rows_kernel(own_ref, partner_ref, density_ref, table, at_ref):
    core = core_of()

    @pl.when(pl.program_id(0) == 0)
    def _():
        strips = at_ref.shape[1]
        split = 2 * VAL * 4
        bands = own_ref.shape[0] - 2 * strips
        at_ref[0] = own_ref[bands : bands + strips, :].astype(jnp.float32)
        at_ref[1] = own_ref[bands + strips :, :].astype(jnp.float32)
        both = jnp.concatenate([own_ref[...], partner_ref[...]], 1)
        for parity in range(2):
            lanes = pl.ds(parity * 2 * SLICE, 2 * SLICE)
            table[0:KPAD, lanes] = pick(KPAD, parity, both[:split])
            table[KPAD:, lanes] = pick(KPAD, parity, both[split:bands])

    picked = []
    for which in range(2):
        index = []
        for s in range(STRIPS):
            strip = lane_matrix(at_ref[which, pl.ds(pl.program_id(0) * STRIPS + s, 1), :]).reshape(-1, 2, FINE, 128)
            index.append(jnp.where(core == 0, strip[:, 0], strip[:, 1]).reshape(-1, 128))
        hot = one_hot(jnp.concatenate(index, 0), KPAD)
        picked.append(
            jnp.dot(hot, table[which * KPAD : (which + 1) * KPAD, :], preferred_element_type=jnp.float32)
        )
    density_ref[...] = jnp.concatenate(densities(*picked), 1).astype(jnp.bfloat16)


def screened_kernel(pairs_ref, own_ref, re_ref, im_ref, out_ref, held, sems):
    core = core_of()
    copies = []
    for place, chip in enumerate(RING):
        lanes = pl.ds(pl.multiple_of((2 * chip + core) * SLICE, SLICE), SLICE)
        to = held.at[:, :, place * SLICE : (place + 1) * SLICE]
        copies.append(pltpu.make_async_copy(own_ref.at[:, :, lanes], to, sems.at[place]))
    for copy in copies:
        copy.start()
    pairs = pairs_ref[...].reshape(-1, 2 * WIDTH)
    for half in (1, 0):
        if half == 0:
            for copy in copies:
                copy.wait()
        parts = []
        for part in range(2):
            w = (re_ref, im_ref)[part][...] if half else held[part]
            parts.append(jnp.dot(w, pairs, preferred_element_type=jnp.float32))
        out_ref[half, :, :WIDTH] = parts[0][:, :WIDTH] - parts[1][:, WIDTH:]
        out_ref[half, :, WIDTH:] = parts[0][:, WIDTH:] + parts[1][:, :WIDTH]


def direct_kernel(mine_ref, other_ref, density_ref, out_ref, screened):
    for half in range(2):
        x = (mine_ref[half] + other_ref[1 - half]).astype(jnp.bfloat16)
        screened[half * SLICE : (half + 1) * SLICE, :] = x
        screened[(2 + half) * SLICE : (3 + half) * SLICE, :WIDTH] = x[:, WIDTH:]
        screened[(2 + half) * SLICE : (3 + half) * SLICE, WIDTH:] = -x[:, :WIDTH]
    parts = 4
    rows = density_ref.shape[0] // parts
    strips = rows // 64
    for m in range(parts):
        direct = jnp.dot(
            density_ref[m * rows : (m + 1) * rows, :], screened[...], preferred_element_type=jnp.float32
        )
        direct = direct.reshape(strips, -1, FINE, 2 * WIDTH)
        direct = jnp.concatenate([direct[s] for s in range(strips)], 1).astype(jnp.bfloat16)
        for place, chip in enumerate(RING):
            out_ref[place, m * strips * FINE : (m + 1) * strips * FINE, :] = direct[chip]


def total_kernel(in_ref, out_ref):
    for part in range(2):
        lanes = slice(part * WIDTH, (part + 1) * WIDTH)
        total = in_ref[0, :, lanes].astype(jnp.float32)
        for chip in range(1, in_ref.shape[0]):
            total += in_ref[chip, :, lanes].astype(jnp.float32)
        out_ref[part] = total


def whole(array):
    return pl.BlockSpec(array.shape, lambda *_: (0,) * len(array.shape))


def shards(valence_orbitals, conduction_orbitals, screened, valence_index, conduction_index, kpoint_index):
    bf16, f32 = jnp.bfloat16, jnp.float32
    rows = lax.axis_size("row")
    chips = rows // 2
    swap = [(i, i ^ 1) for i in range(rows)]
    same_core = [[2 * chip + core for chip in RING] for core in range(2)]
    anywhere = pl.BlockSpec(memory_space=pl.ANY)
    in_vmem = pl.BlockSpec(memory_space=pltpu.VMEM)
    index = [array.reshape(-1, 128) for array in (valence_index, conduction_index, kpoint_index)]
    strips = index[0].shape[0]
    valence = valence_orbitals.reshape(-1, SLICE)
    conduction = conduction_orbitals.reshape(-1, SLICE)
    raw = (valence, conduction, *index)
    shapes = (
        jax.ShapeDtypeStruct((valence.shape[0] + conduction.shape[0] + 2 * strips, SLICE), bf16),
        jax.ShapeDtypeStruct((chips, SLICE, 2 * WIDTH), bf16),
    )
    half_w = jax.ShapeDtypeStruct((SLICE, chips * SLICE), bf16)
    tables, pairs, w_re, w_im = pl.pallas_call(
        columns_kernel,
        out_shape=(*shapes, half_w, half_w),
        grid=(1,),
        in_specs=[whole(array) for array in raw] + [anywhere],
        out_specs=tuple(whole(array) for array in (*shapes, half_w, half_w)),
        scratch_shapes=[pltpu.SemaphoreType.DMA((2, chips))],
        compiler_params=ALL,
        name="columns",
    )(*raw, screened)
    pairs = lax.all_to_all(pairs, "row", 0, 0, axis_index_groups=same_core, tiled=True)
    partner_tables = lax.ppermute(tables, "row", swap)
    w_re = lax.ppermute(w_re, "row", swap)
    w_im = lax.ppermute(w_im, "row", swap)
    density = pl.pallas_call(
        rows_kernel,
        out_shape=jax.ShapeDtypeStruct((strips * 64, 4 * SLICE), bf16),
        grid=(strips // STRIPS,),
        in_specs=[whole(tables), whole(partner_tables)],
        out_specs=pl.BlockSpec((STRIPS * 64, 4 * SLICE), lambda m: (m, 0)),
        scratch_shapes=[pltpu.VMEM((2 * KPAD, 4 * SLICE), bf16), pltpu.VMEM((2, strips, 128), f32)],
        compiler_params=LITTLE,
        cost_estimate=pl.CostEstimate(
            flops=4 * strips * 64 * KPAD * 4 * SLICE, bytes_accessed=3 << 20, transcendentals=0
        ),
        name="rows",
    )(tables, partner_tables)
    pairs, density = lax.optimization_barrier((pairs, density))
    mine = pl.pallas_call(
        screened_kernel,
        out_shape=jax.ShapeDtypeStruct((2, SLICE, 2 * WIDTH), f32),
        in_specs=[in_vmem, anywhere, in_vmem, in_vmem],
        scratch_shapes=[pltpu.VMEM((2, SLICE, chips * SLICE), bf16), pltpu.SemaphoreType.DMA((chips,))],
        compiler_params=MUCH,
        name="screened",
    )(pairs, screened, w_re, w_im)
    other = lax.ppermute(mine, "row", swap)
    partial = pl.pallas_call(
        direct_kernel,
        out_shape=jax.ShapeDtypeStruct((chips, strips * FINE, 2 * WIDTH), bf16),
        scratch_shapes=[pltpu.VMEM((4 * SLICE, 2 * WIDTH), bf16)],
        compiler_params=LITTLE,
        name="direct",
    )(mine, other, density)
    partial = lax.all_to_all(partial, "row", 0, 0, axis_index_groups=same_core, tiled=True)
    out = pl.pallas_call(
        total_kernel,
        out_shape=jax.ShapeDtypeStruct((2, strips * FINE, WIDTH), f32),
        compiler_params=LITTLE,
        name="total",
    )(partial)
    return out.reshape(2, strips, FINE, WIDTH)


def solution(mesh):
    in_specs = (
        P(None, None, None, "row"),
        P(None, None, None, "row"),
        P(None, "row", None),
        P(),
        P(),
        P(),
    )
    return jax.shard_map(
        shards, mesh=mesh, in_specs=in_specs, out_specs=P(None, None, "row", "col"), check_vma=False
    )
```

```python
import jax
import jax.numpy as jnp
from jax import lax
from jax.experimental import pallas as pl
from jax.experimental.pallas import tpu as pltpu
from jax.sharding import PartitionSpec as P

VAL = 48
CON = 64
FINE = 8
SLICE = 128
WIDTH = 128
KPAD = 256
RING = (0, 1, 2, 3, 7, 6, 5, 4)
STRIPS = 16
JOINED = 2
MIB = 1024 * 1024
LITTLE = pltpu.CompilerParams(vmem_limit_bytes=16 * MIB)
MUCH = pltpu.CompilerParams(vmem_limit_bytes=52 * MIB)
ALL = pltpu.CompilerParams(vmem_limit_bytes=63 * MIB)


def core_of():
    return lax.rem(lax.axis_index("row"), 2)


def lane_matrix(row):
    return jnp.broadcast_to(row, (128, 128)).T


def one_hot(index, width):
    lane = lax.broadcasted_iota(jnp.int32, index.shape, 1).astype(jnp.float32)
    parts = [jnp.where(index == lane + float(at), 1.0, 0.0) for at in range(0, width, index.shape[1])]
    return jnp.concatenate(parts, 1).astype(jnp.bfloat16)


def densities(valence, conduction):
    width = valence.shape[1] // 2
    v_re, v_im = valence[:, :width], valence[:, width:]
    c_re, c_im = conduction[:, :width], conduction[:, width:]
    return v_re * c_re + v_im * c_im, v_re * c_im - v_im * c_re


def pick(rows, parity, table):
    i = lax.broadcasted_iota(jnp.int32, (rows, table.shape[0]), 0)
    j = lax.broadcasted_iota(jnp.int32, (rows, table.shape[0]), 1)
    mask = jnp.where(j == 2 * i + parity, 1.0, 0.0).astype(jnp.bfloat16)
    return jnp.dot(mask, table, preferred_element_type=jnp.float32).astype(jnp.bfloat16)


def columns_kernel(
    valence_ref, conduction_ref, v_ref, n_ref, k_ref, w_ref,
    table_ref, out_ref, block_ref,
    bands, index, sums, pairs, blocks, in_sems, w_sems, out_sems, pair_sems,
):
    core = core_of()
    split = valence_ref.shape[0]
    count, strips = bands.shape[0], index.shape[1]
    places = [bands.at[pl.ds(0, split), :], bands.at[pl.ds(split, count - split), :], *[index.at[i] for i in range(3)]]
    loads = []
    for i, (ref, place) in enumerate(zip((valence_ref, conduction_ref, v_ref, n_ref, k_ref), places)):
        loads.append(pltpu.make_async_copy(ref, place, in_sems.at[i]))
    for copy in loads:
        copy.start()
    gathers = []
    for part in range(2):
        for place, chip in enumerate(RING):
            lanes = pl.ds(pl.multiple_of((2 * chip + 1 - core) * SLICE, SLICE), SLICE)
            to = blocks.at[pl.ds((part * len(RING) + place) * SLICE, SLICE), :]
            gathers.append(pltpu.make_async_copy(w_ref.at[part, :, lanes], to, w_sems.at[part, place]))
    for copy in gathers:
        copy.start()
    for copy in loads:
        copy.wait()
    stores = [pltpu.make_async_copy(bands, table_ref.at[pl.ds(0, count), :], out_sems.at[0])]
    stores[0].start()
    own = pl.ds(lax.axis_index("col"), 1)
    picked = []
    for which, (width, start, stop) in enumerate(((VAL, 0, split), (CON, split, count))):
        sums[which * strips : (which + 1) * strips, :] = (
            (index[2] * width + index[which]).astype(jnp.float32).astype(jnp.bfloat16)
        )
        here = lane_matrix((index[2, own, :] * width + index[which, own, :]).astype(jnp.float32))
        parts = []
        for parity in range(2):
            hot = one_hot(2.0 * here + parity, stop - start)
            parts.append(jnp.dot(hot, bands[start:stop, :], preferred_element_type=jnp.float32))
        picked.append(jnp.concatenate(parts, 1))
    stores.append(pltpu.make_async_copy(sums, table_ref.at[pl.ds(count, 2 * strips), :], out_sems.at[1]))
    stores[-1].start()
    real, imag = densities(*picked)
    pairs[...] = jnp.concatenate([real.T, imag.T], 1).astype(jnp.bfloat16)
    for place in range(out_ref.shape[0]):
        stores.append(pltpu.make_async_copy(pairs, out_ref.at[place], pair_sems.at[place]))
        stores[-1].start()
    for copy in gathers:
        copy.wait()
    joined = JOINED * SLICE
    rest = blocks.shape[0] - joined
    to = table_ref.at[pl.ds(count + 2 * strips, joined), :]
    stores.append(pltpu.make_async_copy(blocks.at[pl.ds(0, joined), :], to, out_sems.at[2]))
    stores[-1].start()
    stores.append(pltpu.make_async_copy(blocks.at[pl.ds(joined, rest), :], block_ref, out_sems.at[3]))
    stores[-1].start()
    for copy in stores:
        copy.wait()


def rows_kernel(own_ref, partner_ref, density_ref, table, at_ref):
    core = core_of()

    @pl.when(pl.program_id(0) == 0)
    def _():
        strips = at_ref.shape[1]
        split = 2 * VAL * 4
        bands = 2 * (VAL + CON) * 4
        at_ref[0] = own_ref[bands : bands + strips, :].astype(jnp.float32)
        at_ref[1] = own_ref[bands + strips : bands + 2 * strips, :].astype(jnp.float32)
        both = jnp.concatenate([own_ref[0:bands, :], partner_ref[0:bands, :]], 1)
        for parity in range(2):
            lanes = pl.ds(parity * 2 * SLICE, 2 * SLICE)
            table[0:KPAD, lanes] = pick(KPAD, parity, both[:split])
            table[KPAD:, lanes] = pick(KPAD, parity, both[split:bands])

    picked = []
    for which in range(2):
        index = []
        for s in range(STRIPS):
            strip = lane_matrix(at_ref[which, pl.ds(pl.program_id(0) * STRIPS + s, 1), :]).reshape(-1, 2, FINE, 128)
            index.append(jnp.where(core == 0, strip[:, 0], strip[:, 1]).reshape(-1, 128))
        hot = one_hot(jnp.concatenate(index, 0), KPAD)
        picked.append(
            jnp.dot(hot, table[which * KPAD : (which + 1) * KPAD, :], preferred_element_type=jnp.float32)
        )
    density_ref[...] = jnp.concatenate(densities(*picked), 1).astype(jnp.bfloat16)


def screened_kernel(pairs_ref, own_ref, joined_ref, block_ref, out_ref, held, sems):
    core = core_of()
    copies = []
    for place, chip in enumerate(RING):
        lanes = pl.ds(pl.multiple_of((2 * chip + core) * SLICE, SLICE), SLICE)
        to = held.at[:, :, place * SLICE : (place + 1) * SLICE]
        copies.append(pltpu.make_async_copy(own_ref.at[:, :, lanes], to, sems.at[place]))
    for copy in copies:
        copy.start()
    pairs = pairs_ref[...].reshape(-1, 2 * WIDTH)
    chips = len(RING)
    start = joined_ref.shape[0] - JOINED * SLICE
    blocks = [joined_ref[start + i * SLICE : start + (i + 1) * SLICE, :] for i in range(JOINED)]
    blocks += [block_ref[i * SLICE : (i + 1) * SLICE, :] for i in range(2 * chips - JOINED)]
    for half in (1, 0):
        if half == 0:
            for copy in copies:
                copy.wait()
        parts = []
        for part in range(2):
            w = jnp.concatenate(blocks[part * chips : (part + 1) * chips], 1) if half else held[part]
            parts.append(jnp.dot(w, pairs, preferred_element_type=jnp.float32))
        out_ref[half, :, :WIDTH] = parts[0][:, :WIDTH] - parts[1][:, WIDTH:]
        out_ref[half, :, WIDTH:] = parts[0][:, WIDTH:] + parts[1][:, :WIDTH]


def direct_kernel(mine_ref, other_ref, density_ref, out_ref, screened):
    for half in range(2):
        x = (mine_ref[half] + other_ref[1 - half]).astype(jnp.bfloat16)
        screened[half * SLICE : (half + 1) * SLICE, :] = x
        screened[(2 + half) * SLICE : (3 + half) * SLICE, :WIDTH] = x[:, WIDTH:]
        screened[(2 + half) * SLICE : (3 + half) * SLICE, WIDTH:] = -x[:, :WIDTH]
    parts = 4
    rows = density_ref.shape[0] // parts
    strips = rows // 64
    for m in range(parts):
        direct = jnp.dot(
            density_ref[m * rows : (m + 1) * rows, :], screened[...], preferred_element_type=jnp.float32
        )
        direct = direct.reshape(strips, -1, FINE, 2 * WIDTH)
        direct = jnp.concatenate([direct[s] for s in range(strips)], 1).astype(jnp.bfloat16)
        for place, chip in enumerate(RING):
            out_ref[place, m * strips * FINE : (m + 1) * strips * FINE, :] = direct[chip]


def total_kernel(in_ref, out_ref):
    for part in range(2):
        lanes = slice(part * WIDTH, (part + 1) * WIDTH)
        total = in_ref[0, :, lanes].astype(jnp.float32)
        for chip in range(1, in_ref.shape[0]):
            total += in_ref[chip, :, lanes].astype(jnp.float32)
        out_ref[part] = total


def whole(array):
    return pl.BlockSpec(array.shape, lambda *_: (0,) * len(array.shape))


def shards(valence_orbitals, conduction_orbitals, screened, valence_index, conduction_index, kpoint_index):
    bf16, f32 = jnp.bfloat16, jnp.float32
    rows = lax.axis_size("row")
    chips = rows // 2
    swap = [(i, i ^ 1) for i in range(rows)]
    same_core = [[2 * chip + core for chip in RING] for core in range(2)]
    anywhere = pl.BlockSpec(memory_space=pl.ANY)
    in_vmem = pl.BlockSpec(memory_space=pltpu.VMEM)
    index = [array.reshape(-1, 128) for array in (valence_index, conduction_index, kpoint_index)]
    strips = index[0].shape[0]
    valence = valence_orbitals.reshape(-1, SLICE)
    conduction = conduction_orbitals.reshape(-1, SLICE)
    raw = (valence, conduction, *index)
    bands = valence.shape[0] + conduction.shape[0]
    dma = pltpu.SemaphoreType.DMA
    tables, pairs, blocks = pl.pallas_call(
        columns_kernel,
        out_shape=(
            jax.ShapeDtypeStruct((bands + 2 * strips + JOINED * SLICE, SLICE), bf16),
            jax.ShapeDtypeStruct((chips, SLICE, 2 * WIDTH), bf16),
            jax.ShapeDtypeStruct(((2 * chips - JOINED) * SLICE, SLICE), bf16),
        ),
        in_specs=[anywhere] * 6,
        out_specs=(anywhere,) * 3,
        scratch_shapes=[
            pltpu.VMEM((bands, SLICE), bf16),
            pltpu.VMEM((3, strips, 128), jnp.int32),
            pltpu.VMEM((2 * strips, 128), bf16),
            pltpu.VMEM((SLICE, 2 * WIDTH), bf16),
            pltpu.VMEM((2 * chips * SLICE, SLICE), bf16),
            dma((5,)),
            dma((2, chips)),
            dma((4,)),
            dma((chips,)),
        ],
        compiler_params=ALL,
        name="columns",
    )(*raw, screened)
    pairs = lax.all_to_all(pairs, "row", 0, 0, axis_index_groups=same_core, tiled=True)
    partner_tables = lax.ppermute(tables, "row", swap)
    blocks = lax.ppermute(blocks, "row", swap)
    density = pl.pallas_call(
        rows_kernel,
        out_shape=jax.ShapeDtypeStruct((strips * 64, 4 * SLICE), bf16),
        grid=(strips // STRIPS,),
        in_specs=[whole(tables), whole(partner_tables)],
        out_specs=pl.BlockSpec((STRIPS * 64, 4 * SLICE), lambda m: (m, 0)),
        scratch_shapes=[pltpu.VMEM((2 * KPAD, 4 * SLICE), bf16), pltpu.VMEM((2, strips, 128), f32)],
        compiler_params=LITTLE,
        cost_estimate=pl.CostEstimate(
            flops=2 * strips * 64 * KPAD * 4 * SLICE, bytes_accessed=1 << 20, transcendentals=0
        ),
        name="rows",
    )(tables, partner_tables)
    pairs, density = lax.optimization_barrier((pairs, density))
    mine = pl.pallas_call(
        screened_kernel,
        out_shape=jax.ShapeDtypeStruct((2, SLICE, 2 * WIDTH), f32),
        in_specs=[in_vmem, anywhere, in_vmem, in_vmem],
        scratch_shapes=[pltpu.VMEM((2, SLICE, chips * SLICE), bf16), pltpu.SemaphoreType.DMA((chips,))],
        compiler_params=MUCH,
        name="screened",
    )(pairs, screened, partner_tables, blocks)
    other = lax.ppermute(mine, "row", swap)
    partial = pl.pallas_call(
        direct_kernel,
        out_shape=jax.ShapeDtypeStruct((chips, strips * FINE, 2 * WIDTH), bf16),
        scratch_shapes=[pltpu.VMEM((4 * SLICE, 2 * WIDTH), bf16)],
        compiler_params=LITTLE,
        name="direct",
    )(mine, other, density)
    partial = lax.all_to_all(partial, "row", 0, 0, axis_index_groups=same_core, tiled=True)
    out = pl.pallas_call(
        total_kernel,
        out_shape=jax.ShapeDtypeStruct((2, strips * FINE, WIDTH), f32),
        compiler_params=LITTLE,
        name="total",
    )(partial)
    return out.reshape(2, strips, FINE, WIDTH)


def solution(mesh):
    in_specs = (
        P(None, None, None, "row"),
        P(None, None, None, "row"),
        P(None, "row", None),
        P(),
        P(),
        P(),
    )
    return jax.shard_map(
        shards, mesh=mesh, in_specs=in_specs, out_specs=P(None, None, "row", "col"), check_vma=False
    )
```

```python
import jax
import jax.numpy as jnp
from jax import lax
from jax.experimental import pallas as pl
from jax.experimental.pallas import tpu as pltpu
from jax.sharding import PartitionSpec as P

VAL = 48
CON = 64
FINE = 8
SLICE = 128
WIDTH = 128
KPAD = 256
RING = (0, 1, 2, 3, 7, 6, 5, 4)
STRIPS = 16
JOINED = 5
MIB = 1024 * 1024
LITTLE = pltpu.CompilerParams(vmem_limit_bytes=16 * MIB)
MUCH = pltpu.CompilerParams(vmem_limit_bytes=52 * MIB)
ALL = pltpu.CompilerParams(vmem_limit_bytes=63 * MIB)


def core_of():
    return lax.rem(lax.axis_index("row"), 2)


def lane_matrix(row):
    return jnp.broadcast_to(row, (128, 128)).T


def one_hot(index, width):
    lane = lax.broadcasted_iota(jnp.int32, index.shape, 1).astype(jnp.float32)
    parts = [jnp.where(index == lane + float(at), 1.0, 0.0) for at in range(0, width, index.shape[1])]
    return jnp.concatenate(parts, 1).astype(jnp.bfloat16)


def densities(valence, conduction):
    width = valence.shape[1] // 2
    v_re, v_im = valence[:, :width], valence[:, width:]
    c_re, c_im = conduction[:, :width], conduction[:, width:]
    return v_re * c_re + v_im * c_im, v_re * c_im - v_im * c_re


def pick(rows, parity, table):
    i = lax.broadcasted_iota(jnp.int32, (rows, table.shape[0]), 0)
    j = lax.broadcasted_iota(jnp.int32, (rows, table.shape[0]), 1)
    mask = jnp.where(j == 2 * i + parity, 1.0, 0.0).astype(jnp.bfloat16)
    return jnp.dot(mask, table, preferred_element_type=jnp.float32).astype(jnp.bfloat16)


def columns_kernel(
    valence_ref, conduction_ref, v_ref, n_ref, k_ref, w_ref,
    table_ref, out_ref, block_ref,
    bands, index, sums, pairs, blocks, in_sems, w_sems, out_sems, pair_sems,
):
    core = core_of()
    split = valence_ref.shape[0]
    count, strips = bands.shape[0], index.shape[1]
    places = [bands.at[pl.ds(0, split), :], bands.at[pl.ds(split, count - split), :], *[index.at[i] for i in range(3)]]
    loads = []
    for i, (ref, place) in enumerate(zip((valence_ref, conduction_ref, v_ref, n_ref, k_ref), places)):
        loads.append(pltpu.make_async_copy(ref, place, in_sems.at[i]))
    for copy in loads:
        copy.start()
    gathers = []
    for part in range(2):
        for place, chip in enumerate(RING):
            lanes = pl.ds(pl.multiple_of((2 * chip + 1 - core) * SLICE, SLICE), SLICE)
            to = blocks.at[pl.ds((part * len(RING) + place) * SLICE, SLICE), :]
            gathers.append(pltpu.make_async_copy(w_ref.at[part, :, lanes], to, w_sems.at[part, place]))
    for copy in gathers:
        copy.start()
    for copy in loads:
        copy.wait()
    stores = [pltpu.make_async_copy(bands, table_ref.at[pl.ds(0, count), :], out_sems.at[0])]
    stores[0].start()
    own = pl.ds(lax.axis_index("col"), 1)
    picked = []
    for which, (width, start, stop) in enumerate(((VAL, 0, split), (CON, split, count))):
        sums[which * strips : (which + 1) * strips, :] = (
            (index[2] * width + index[which]).astype(jnp.float32).astype(jnp.bfloat16)
        )
        here = lane_matrix((index[2, own, :] * width + index[which, own, :]).astype(jnp.float32))
        parts = []
        for parity in range(2):
            hot = one_hot(2.0 * here + parity, stop - start)
            parts.append(jnp.dot(hot, bands[start:stop, :], preferred_element_type=jnp.float32))
        picked.append(jnp.concatenate(parts, 1))
    stores.append(pltpu.make_async_copy(sums, table_ref.at[pl.ds(count, 2 * strips), :], out_sems.at[1]))
    stores[-1].start()
    real, imag = densities(*picked)
    pairs[...] = jnp.concatenate([real.T, imag.T], 1).astype(jnp.bfloat16)
    for place in range(out_ref.shape[0]):
        stores.append(pltpu.make_async_copy(pairs, out_ref.at[place], pair_sems.at[place]))
        stores[-1].start()
    for copy in gathers:
        copy.wait()
    joined = JOINED * SLICE
    rest = blocks.shape[0] - joined
    to = table_ref.at[pl.ds(count + 2 * strips, joined), :]
    stores.append(pltpu.make_async_copy(blocks.at[pl.ds(0, joined), :], to, out_sems.at[2]))
    stores[-1].start()
    stores.append(pltpu.make_async_copy(blocks.at[pl.ds(joined, rest), :], block_ref, out_sems.at[3]))
    stores[-1].start()
    for copy in stores:
        copy.wait()


def rows_kernel(own_ref, partner_ref, density_ref, table, at_ref):
    core = core_of()

    @pl.when(pl.program_id(0) == 0)
    def _():
        strips = at_ref.shape[1]
        split = 2 * VAL * 4
        bands = 2 * (VAL + CON) * 4
        at_ref[0] = own_ref[bands : bands + strips, :].astype(jnp.float32)
        at_ref[1] = own_ref[bands + strips : bands + 2 * strips, :].astype(jnp.float32)
        both = jnp.concatenate([own_ref[0:bands, :], partner_ref[0:bands, :]], 1)
        for parity in range(2):
            lanes = pl.ds(parity * 2 * SLICE, 2 * SLICE)
            table[0:KPAD, lanes] = pick(KPAD, parity, both[:split])
            table[KPAD:, lanes] = pick(KPAD, parity, both[split:bands])

    picked = []
    for which in range(2):
        index = []
        for s in range(STRIPS):
            strip = lane_matrix(at_ref[which, pl.ds(pl.program_id(0) * STRIPS + s, 1), :]).reshape(-1, 2, FINE, 128)
            index.append(jnp.where(core == 0, strip[:, 0], strip[:, 1]).reshape(-1, 128))
        hot = one_hot(jnp.concatenate(index, 0), KPAD)
        picked.append(
            jnp.dot(hot, table[which * KPAD : (which + 1) * KPAD, :], preferred_element_type=jnp.float32)
        )
    density_ref[...] = jnp.concatenate(densities(*picked), 1).astype(jnp.bfloat16)


def screened_kernel(pairs_ref, own_ref, joined_ref, block_ref, out_ref, held, sems):
    core = core_of()
    copies = []
    for place, chip in enumerate(RING):
        lanes = pl.ds(pl.multiple_of((2 * chip + core) * SLICE, SLICE), SLICE)
        to = held.at[:, :, place * SLICE : (place + 1) * SLICE]
        copies.append(pltpu.make_async_copy(own_ref.at[:, :, lanes], to, sems.at[place]))
    for copy in copies:
        copy.start()
    pairs = pairs_ref[...].reshape(-1, 2 * WIDTH)
    chips = len(RING)
    start = joined_ref.shape[0] - JOINED * SLICE
    blocks = [joined_ref[start + i * SLICE : start + (i + 1) * SLICE, :] for i in range(JOINED)]
    blocks += [block_ref[i * SLICE : (i + 1) * SLICE, :] for i in range(2 * chips - JOINED)]
    for half in (1, 0):
        if half == 0:
            for copy in copies:
                copy.wait()
        parts = []
        for part in range(2):
            w = jnp.concatenate(blocks[part * chips : (part + 1) * chips], 1) if half else held[part]
            parts.append(jnp.dot(w, pairs, preferred_element_type=jnp.float32))
        out_ref[half, :, :WIDTH] = parts[0][:, :WIDTH] - parts[1][:, WIDTH:]
        out_ref[half, :, WIDTH:] = parts[0][:, WIDTH:] + parts[1][:, :WIDTH]


def direct_kernel(mine_ref, other_ref, density_ref, out_ref, screened):
    for half in range(2):
        x = (mine_ref[half] + other_ref[1 - half]).astype(jnp.bfloat16)
        screened[half * SLICE : (half + 1) * SLICE, :] = x
        screened[(2 + half) * SLICE : (3 + half) * SLICE, :WIDTH] = x[:, WIDTH:]
        screened[(2 + half) * SLICE : (3 + half) * SLICE, WIDTH:] = -x[:, :WIDTH]
    parts = 4
    rows = density_ref.shape[0] // parts
    strips = rows // 64
    for m in range(parts):
        direct = jnp.dot(
            density_ref[m * rows : (m + 1) * rows, :], screened[...], preferred_element_type=jnp.float32
        )
        direct = direct.reshape(strips, -1, FINE, 2 * WIDTH)
        direct = jnp.concatenate([direct[s] for s in range(strips)], 1).astype(jnp.bfloat16)
        for place, chip in enumerate(RING):
            out_ref[place, m * strips * FINE : (m + 1) * strips * FINE, :] = direct[chip]


def total_kernel(in_ref, out_ref):
    for part in range(2):
        lanes = slice(part * WIDTH, (part + 1) * WIDTH)
        total = in_ref[0, :, lanes].astype(jnp.float32)
        for chip in range(1, in_ref.shape[0]):
            total += in_ref[chip, :, lanes].astype(jnp.float32)
        out_ref[part] = total


def whole(array):
    return pl.BlockSpec(array.shape, lambda *_: (0,) * len(array.shape))


def shards(valence_orbitals, conduction_orbitals, screened, valence_index, conduction_index, kpoint_index):
    bf16, f32 = jnp.bfloat16, jnp.float32
    rows = lax.axis_size("row")
    chips = rows // 2
    swap = [(i, i ^ 1) for i in range(rows)]
    same_core = [[2 * chip + core for chip in RING] for core in range(2)]
    anywhere = pl.BlockSpec(memory_space=pl.ANY)
    in_vmem = pl.BlockSpec(memory_space=pltpu.VMEM)
    index = [array.reshape(-1, 128) for array in (valence_index, conduction_index, kpoint_index)]
    strips = index[0].shape[0]
    valence = valence_orbitals.reshape(-1, SLICE)
    conduction = conduction_orbitals.reshape(-1, SLICE)
    raw = (valence, conduction, *index)
    bands = valence.shape[0] + conduction.shape[0]
    dma = pltpu.SemaphoreType.DMA
    tables, pairs, blocks = pl.pallas_call(
        columns_kernel,
        out_shape=(
            jax.ShapeDtypeStruct((bands + 2 * strips + JOINED * SLICE, SLICE), bf16),
            jax.ShapeDtypeStruct((chips, SLICE, 2 * WIDTH), bf16),
            jax.ShapeDtypeStruct(((2 * chips - JOINED) * SLICE, SLICE), bf16),
        ),
        in_specs=[anywhere] * 6,
        out_specs=(anywhere,) * 3,
        scratch_shapes=[
            pltpu.VMEM((bands, SLICE), bf16),
            pltpu.VMEM((3, strips, 128), jnp.int32),
            pltpu.VMEM((2 * strips, 128), bf16),
            pltpu.VMEM((SLICE, 2 * WIDTH), bf16),
            pltpu.VMEM((2 * chips * SLICE, SLICE), bf16),
            dma((5,)),
            dma((2, chips)),
            dma((4,)),
            dma((chips,)),
        ],
        compiler_params=ALL,
        name="columns",
    )(*raw, screened)
    pairs = lax.all_to_all(pairs, "row", 0, 0, axis_index_groups=same_core, tiled=True)
    partner_tables = lax.ppermute(tables, "row", swap)
    blocks = lax.ppermute(blocks, "row", swap)
    density = pl.pallas_call(
        rows_kernel,
        out_shape=jax.ShapeDtypeStruct((strips * 64, 4 * SLICE), bf16),
        grid=(strips // STRIPS,),
        in_specs=[whole(tables), whole(partner_tables)],
        out_specs=pl.BlockSpec((STRIPS * 64, 4 * SLICE), lambda m: (m, 0)),
        scratch_shapes=[pltpu.VMEM((2 * KPAD, 4 * SLICE), bf16), pltpu.VMEM((2, strips, 128), f32)],
        compiler_params=LITTLE,
        cost_estimate=pl.CostEstimate(flops=0, bytes_accessed=0, transcendentals=0),
        name="rows",
    )(tables, partner_tables)
    pairs, density = lax.optimization_barrier((pairs, density))
    mine = pl.pallas_call(
        screened_kernel,
        out_shape=jax.ShapeDtypeStruct((2, SLICE, 2 * WIDTH), f32),
        in_specs=[in_vmem, anywhere, in_vmem, in_vmem],
        scratch_shapes=[pltpu.VMEM((2, SLICE, chips * SLICE), bf16), pltpu.SemaphoreType.DMA((chips,))],
        compiler_params=MUCH,
        name="screened",
    )(pairs, screened, partner_tables, blocks)
    other = lax.ppermute(mine, "row", swap)
    partial = pl.pallas_call(
        direct_kernel,
        out_shape=jax.ShapeDtypeStruct((chips, strips * FINE, 2 * WIDTH), bf16),
        scratch_shapes=[pltpu.VMEM((4 * SLICE, 2 * WIDTH), bf16)],
        compiler_params=LITTLE,
        name="direct",
    )(mine, other, density)
    partial = lax.all_to_all(partial, "row", 0, 0, axis_index_groups=same_core, tiled=True)
    out = pl.pallas_call(
        total_kernel,
        out_shape=jax.ShapeDtypeStruct((2, strips * FINE, WIDTH), f32),
        compiler_params=LITTLE,
        name="total",
    )(partial)
    return out.reshape(2, strips, FINE, WIDTH)


def solution(mesh):
    in_specs = (
        P(None, None, None, "row"),
        P(None, None, None, "row"),
        P(None, "row", None),
        P(),
        P(),
        P(),
    )
    return jax.shard_map(
        shards, mesh=mesh, in_specs=in_specs, out_specs=P(None, None, "row", "col"), check_vma=False
    )
```

```python
import jax
import jax.numpy as jnp
from jax import lax
from jax.experimental import pallas as pl
from jax.experimental.pallas import tpu as pltpu
from jax.sharding import PartitionSpec as P

VAL = 48
CON = 64
FINE = 8
SLICE = 128
WIDTH = 128
KPAD = 256
RING = (0, 1, 2, 3, 7, 6, 5, 4)
STRIPS = 8
JOINED = 5
MIB = 1024 * 1024
LITTLE = pltpu.CompilerParams(vmem_limit_bytes=16 * MIB)
MUCH = pltpu.CompilerParams(vmem_limit_bytes=52 * MIB)
ALL = pltpu.CompilerParams(vmem_limit_bytes=63 * MIB)


def core_of():
    return lax.rem(lax.axis_index("row"), 2)


def lane_matrix(row):
    return jnp.broadcast_to(row, (128, 128)).T


def one_hot(index, width):
    lane = lax.broadcasted_iota(jnp.int32, index.shape, 1).astype(jnp.float32)
    parts = [jnp.where(index == lane + float(at), 1.0, 0.0) for at in range(0, width, index.shape[1])]
    return jnp.concatenate(parts, 1).astype(jnp.bfloat16)


def densities(valence, conduction):
    width = valence.shape[1] // 2
    v_re, v_im = valence[:, :width], valence[:, width:]
    c_re, c_im = conduction[:, :width], conduction[:, width:]
    return v_re * c_re + v_im * c_im, v_re * c_im - v_im * c_re


def pick(rows, parity, table):
    i = lax.broadcasted_iota(jnp.int32, (rows, table.shape[0]), 0)
    j = lax.broadcasted_iota(jnp.int32, (rows, table.shape[0]), 1)
    mask = jnp.where(j == 2 * i + parity, 1.0, 0.0).astype(jnp.bfloat16)
    return jnp.dot(mask, table, preferred_element_type=jnp.float32).astype(jnp.bfloat16)


def columns_kernel(
    valence_ref, conduction_ref, v_ref, n_ref, k_ref, w_ref,
    table_ref, out_ref, block_ref,
    bands, index, sums, pairs, blocks, in_sems, w_sems, out_sems, pair_sems,
):
    core = core_of()
    split = valence_ref.shape[0]
    count, strips = bands.shape[0], index.shape[1]
    places = [bands.at[pl.ds(0, split), :], bands.at[pl.ds(split, count - split), :], *[index.at[i] for i in range(3)]]
    loads = []
    for i, (ref, place) in enumerate(zip((valence_ref, conduction_ref, v_ref, n_ref, k_ref), places)):
        loads.append(pltpu.make_async_copy(ref, place, in_sems.at[i]))
    for copy in loads:
        copy.start()
    gathers = []
    for part in range(2):
        for place, chip in enumerate(RING):
            lanes = pl.ds(pl.multiple_of((2 * chip + 1 - core) * SLICE, SLICE), SLICE)
            to = blocks.at[pl.ds((part * len(RING) + place) * SLICE, SLICE), :]
            gathers.append(pltpu.make_async_copy(w_ref.at[part, :, lanes], to, w_sems.at[part, place]))
    for copy in gathers:
        copy.start()
    for copy in loads:
        copy.wait()
    stores = [pltpu.make_async_copy(bands, table_ref.at[pl.ds(0, count), :], out_sems.at[0])]
    stores[0].start()
    for copy in gathers:
        copy.wait()
    joined = JOINED * SLICE
    rest = blocks.shape[0] - joined
    to = table_ref.at[pl.ds(count + 2 * strips, joined), :]
    stores.append(pltpu.make_async_copy(blocks.at[pl.ds(0, joined), :], to, out_sems.at[2]))
    stores[-1].start()
    stores.append(pltpu.make_async_copy(blocks.at[pl.ds(joined, rest), :], block_ref, out_sems.at[3]))
    stores[-1].start()
    own = pl.ds(lax.axis_index("col"), 1)
    picked = []
    for which, (width, start, stop) in enumerate(((VAL, 0, split), (CON, split, count))):
        sums[which * strips : (which + 1) * strips, :] = (
            (index[2] * width + index[which]).astype(jnp.float32).astype(jnp.bfloat16)
        )
        here = lane_matrix((index[2, own, :] * width + index[which, own, :]).astype(jnp.float32))
        parts = []
        for parity in range(2):
            hot = one_hot(2.0 * here + parity, stop - start)
            parts.append(jnp.dot(hot, bands[start:stop, :], preferred_element_type=jnp.float32))
        picked.append(jnp.concatenate(parts, 1))
    stores.append(pltpu.make_async_copy(sums, table_ref.at[pl.ds(count, 2 * strips), :], out_sems.at[1]))
    stores[-1].start()
    real, imag = densities(*picked)
    pairs[...] = jnp.concatenate([real.T, imag.T], 1).astype(jnp.bfloat16)
    for place in range(out_ref.shape[0]):
        stores.append(pltpu.make_async_copy(pairs, out_ref.at[place], pair_sems.at[place]))
        stores[-1].start()
    for copy in stores:
        copy.wait()


def rows_kernel(own_ref, partner_ref, density_ref, table, at_ref):
    first = core_of() * (at_ref.shape[1] // 2) + pl.program_id(0) * STRIPS

    @pl.when(pl.program_id(0) == 0)
    def _():
        strips = at_ref.shape[1]
        split = 2 * VAL * 4
        bands = 2 * (VAL + CON) * 4
        at_ref[0] = own_ref[bands : bands + strips, :].astype(jnp.float32)
        at_ref[1] = own_ref[bands + strips : bands + 2 * strips, :].astype(jnp.float32)
        both = jnp.concatenate([own_ref[0:bands, :], partner_ref[0:bands, :]], 1)
        for parity in range(2):
            lanes = pl.ds(parity * 2 * SLICE, 2 * SLICE)
            table[0:KPAD, lanes] = pick(KPAD, parity, both[:split])
            table[KPAD:, lanes] = pick(KPAD, parity, both[split:bands])

    picked = []
    for which in range(2):
        index = [lane_matrix(at_ref[which, pl.ds(first + s, 1), :]) for s in range(STRIPS)]
        hot = one_hot(jnp.concatenate(index, 0), KPAD)
        picked.append(
            jnp.dot(hot, table[which * KPAD : (which + 1) * KPAD, :], preferred_element_type=jnp.float32)
        )
    density_ref[...] = jnp.concatenate(densities(*picked), 1).astype(jnp.bfloat16)


def screened_kernel(pairs_ref, own_ref, joined_ref, block_ref, out_ref, held, sems):
    core = core_of()
    copies = []
    for place, chip in enumerate(RING):
        lanes = pl.ds(pl.multiple_of((2 * chip + core) * SLICE, SLICE), SLICE)
        to = held.at[:, :, place * SLICE : (place + 1) * SLICE]
        copies.append(pltpu.make_async_copy(own_ref.at[:, :, lanes], to, sems.at[place]))
    for copy in copies:
        copy.start()
    pairs = pairs_ref[...].reshape(-1, 2 * WIDTH)
    chips = len(RING)
    start = joined_ref.shape[0] - JOINED * SLICE
    blocks = [joined_ref[start + i * SLICE : start + (i + 1) * SLICE, :] for i in range(JOINED)]
    blocks += [block_ref[i * SLICE : (i + 1) * SLICE, :] for i in range(2 * chips - JOINED)]
    for half in (1, 0):
        if half == 0:
            for copy in copies:
                copy.wait()
        parts = []
        for part in range(2):
            w = jnp.concatenate(blocks[part * chips : (part + 1) * chips], 1) if half else held[part]
            parts.append(jnp.dot(w, pairs, preferred_element_type=jnp.float32))
        out_ref[half, :, :WIDTH] = parts[0][:, :WIDTH] - parts[1][:, WIDTH:]
        out_ref[half, :, WIDTH:] = parts[0][:, WIDTH:] + parts[1][:, :WIDTH]


def direct_kernel(mine_ref, other_ref, density_ref, out_ref, screened):
    for half in range(2):
        x = (mine_ref[half] + other_ref[1 - half]).astype(jnp.bfloat16)
        screened[half * SLICE : (half + 1) * SLICE, :] = x
        screened[(2 + half) * SLICE : (3 + half) * SLICE, :WIDTH] = x[:, WIDTH:]
        screened[(2 + half) * SLICE : (3 + half) * SLICE, WIDTH:] = -x[:, :WIDTH]
    parts = 4
    rows = density_ref.shape[0] // parts
    strips = rows // 128
    for m in range(parts):
        direct = jnp.dot(
            density_ref[m * rows : (m + 1) * rows, :], screened[...], preferred_element_type=jnp.float32
        )
        direct = direct.reshape(strips, -1, FINE, 2 * WIDTH)
        direct = jnp.concatenate([direct[s] for s in range(strips)], 1).astype(jnp.bfloat16)
        out_ref[:, m * strips * FINE : (m + 1) * strips * FINE, :] = direct


def total_kernel(in_ref, out_ref):
    rows = in_ref.shape[1]
    for core in range(2):
        for part in range(2):
            lanes = slice(part * WIDTH, (part + 1) * WIDTH)
            total = in_ref[core, :, lanes].astype(jnp.float32)
            for chip in range(1, in_ref.shape[0] // 2):
                total += in_ref[2 * chip + core, :, lanes].astype(jnp.float32)
            out_ref[part, core * rows : (core + 1) * rows, :] = total


def whole(array):
    return pl.BlockSpec(array.shape, lambda *_: (0,) * len(array.shape))


def shards(valence_orbitals, conduction_orbitals, screened, valence_index, conduction_index, kpoint_index):
    bf16, f32 = jnp.bfloat16, jnp.float32
    rows = lax.axis_size("row")
    chips = rows // 2
    swap = [(i, i ^ 1) for i in range(rows)]
    same_core = [[2 * chip + core for chip in RING] for core in range(2)]
    anywhere = pl.BlockSpec(memory_space=pl.ANY)
    in_vmem = pl.BlockSpec(memory_space=pltpu.VMEM)
    index = [array.reshape(-1, 128) for array in (valence_index, conduction_index, kpoint_index)]
    strips = index[0].shape[0]
    valence = valence_orbitals.reshape(-1, SLICE)
    conduction = conduction_orbitals.reshape(-1, SLICE)
    raw = (valence, conduction, *index)
    bands = valence.shape[0] + conduction.shape[0]
    dma = pltpu.SemaphoreType.DMA
    tables, pairs, blocks = pl.pallas_call(
        columns_kernel,
        out_shape=(
            jax.ShapeDtypeStruct((bands + 2 * strips + JOINED * SLICE, SLICE), bf16),
            jax.ShapeDtypeStruct((chips, SLICE, 2 * WIDTH), bf16),
            jax.ShapeDtypeStruct(((2 * chips - JOINED) * SLICE, SLICE), bf16),
        ),
        in_specs=[anywhere] * 6,
        out_specs=(anywhere,) * 3,
        scratch_shapes=[
            pltpu.VMEM((bands, SLICE), bf16),
            pltpu.VMEM((3, strips, 128), jnp.int32),
            pltpu.VMEM((2 * strips, 128), bf16),
            pltpu.VMEM((SLICE, 2 * WIDTH), bf16),
            pltpu.VMEM((2 * chips * SLICE, SLICE), bf16),
            dma((5,)),
            dma((2, chips)),
            dma((4,)),
            dma((chips,)),
        ],
        compiler_params=ALL,
        name="columns",
    )(*raw, screened)
    pairs = lax.all_to_all(pairs, "row", 0, 0, axis_index_groups=same_core, tiled=True)
    partner_tables = lax.ppermute(tables, "row", swap)
    blocks = lax.ppermute(blocks, "row", swap)
    density = pl.pallas_call(
        rows_kernel,
        out_shape=jax.ShapeDtypeStruct((strips * 64, 4 * SLICE), bf16),
        grid=(strips // 2 // STRIPS,),
        in_specs=[whole(tables), whole(partner_tables)],
        out_specs=pl.BlockSpec((STRIPS * 128, 4 * SLICE), lambda m: (m, 0)),
        scratch_shapes=[pltpu.VMEM((2 * KPAD, 4 * SLICE), bf16), pltpu.VMEM((2, strips, 128), f32)],
        compiler_params=LITTLE,
        cost_estimate=pl.CostEstimate(flops=0, bytes_accessed=0, transcendentals=0),
        name="rows",
    )(tables, partner_tables)
    pairs, density = lax.optimization_barrier((pairs, density))
    mine = pl.pallas_call(
        screened_kernel,
        out_shape=jax.ShapeDtypeStruct((2, SLICE, 2 * WIDTH), f32),
        in_specs=[in_vmem, anywhere, in_vmem, in_vmem],
        scratch_shapes=[pltpu.VMEM((2, SLICE, chips * SLICE), bf16), pltpu.SemaphoreType.DMA((chips,))],
        compiler_params=MUCH,
        name="screened",
    )(pairs, screened, partner_tables, blocks)
    other = lax.ppermute(mine, "row", swap)
    partial = pl.pallas_call(
        direct_kernel,
        out_shape=jax.ShapeDtypeStruct((rows, strips // 2 * FINE, 2 * WIDTH), bf16),
        scratch_shapes=[pltpu.VMEM((4 * SLICE, 2 * WIDTH), bf16)],
        compiler_params=LITTLE,
        name="direct",
    )(mine, other, density)
    partial = lax.all_to_all(partial, "row", 0, 0, tiled=True)
    out = pl.pallas_call(
        total_kernel,
        out_shape=jax.ShapeDtypeStruct((2, strips * FINE, WIDTH), f32),
        compiler_params=LITTLE,
        name="total",
    )(partial)
    return out.reshape(2, strips, FINE, WIDTH)


def solution(mesh):
    in_specs = (
        P(None, None, None, "row"),
        P(None, None, None, "row"),
        P(None, "row", None),
        P(),
        P(),
        P(),
    )
    return jax.shard_map(
        shards, mesh=mesh, in_specs=in_specs, out_specs=P(None, None, "row", "col"), check_vma=False
    )
```

```python
import jax
import jax.numpy as jnp
from jax import lax
from jax.experimental import pallas as pl
from jax.experimental.pallas import tpu as pltpu
from jax.sharding import PartitionSpec as P

VAL = 48
CON = 64
FINE = 8
SLICE = 128
WIDTH = 128
KPAD = 256
RING = (0, 1, 2, 3, 7, 6, 5, 4)
STRIPS = 16
JOINED = 5
MIB = 1024 * 1024
LITTLE = pltpu.CompilerParams(vmem_limit_bytes=16 * MIB)
MUCH = pltpu.CompilerParams(vmem_limit_bytes=52 * MIB)
ALL = pltpu.CompilerParams(vmem_limit_bytes=63 * MIB)


def core_of():
    return lax.rem(lax.axis_index("row"), 2)


def lane_matrix(row):
    return jnp.broadcast_to(row, (128, 128)).T


def one_hot(index, width):
    lane = lax.broadcasted_iota(jnp.int32, index.shape, 1).astype(jnp.float32)
    parts = [jnp.where(index == lane + float(at), 1.0, 0.0) for at in range(0, width, index.shape[1])]
    return jnp.concatenate(parts, 1).astype(jnp.bfloat16)


def densities(valence, conduction):
    width = valence.shape[1] // 2
    v_re, v_im = valence[:, :width], valence[:, width:]
    c_re, c_im = conduction[:, :width], conduction[:, width:]
    return v_re * c_re + v_im * c_im, v_re * c_im - v_im * c_re


def pick(rows, parity, table):
    i = lax.broadcasted_iota(jnp.int32, (rows, table.shape[0]), 0)
    j = lax.broadcasted_iota(jnp.int32, (rows, table.shape[0]), 1)
    mask = jnp.where(j == 2 * i + parity, 1.0, 0.0).astype(jnp.bfloat16)
    return jnp.dot(mask, table, preferred_element_type=jnp.float32).astype(jnp.bfloat16)


def columns_kernel(
    valence_ref, conduction_ref, v_ref, n_ref, k_ref, w_ref,
    table_ref, out_ref, block_ref,
    bands, index, sums, pairs, blocks, in_sems, w_sems, out_sems, pair_sems,
):
    core = core_of()
    split = valence_ref.shape[0]
    count, strips = bands.shape[0], index.shape[1]
    places = [bands.at[pl.ds(0, split), :], bands.at[pl.ds(split, count - split), :], *[index.at[i] for i in range(3)]]
    loads = []
    for i, (ref, place) in enumerate(zip((valence_ref, conduction_ref, v_ref, n_ref, k_ref), places)):
        loads.append(pltpu.make_async_copy(ref, place, in_sems.at[i]))
    for copy in loads:
        copy.start()
    gathers = []
    for part in range(2):
        for place, chip in enumerate(RING):
            lanes = pl.ds(pl.multiple_of((2 * chip + 1 - core) * SLICE, SLICE), SLICE)
            to = blocks.at[pl.ds((part * len(RING) + place) * SLICE, SLICE), :]
            gathers.append(pltpu.make_async_copy(w_ref.at[part, :, lanes], to, w_sems.at[part, place]))
    for copy in gathers:
        copy.start()
    for copy in loads:
        copy.wait()
    stores = [pltpu.make_async_copy(bands, table_ref.at[pl.ds(0, count), :], out_sems.at[0])]
    stores[0].start()
    for copy in gathers:
        copy.wait()
    joined = JOINED * SLICE
    rest = blocks.shape[0] - joined
    to = table_ref.at[pl.ds(count + 2 * strips, joined), :]
    stores.append(pltpu.make_async_copy(blocks.at[pl.ds(0, joined), :], to, out_sems.at[2]))
    stores[-1].start()
    stores.append(pltpu.make_async_copy(blocks.at[pl.ds(joined, rest), :], block_ref, out_sems.at[3]))
    stores[-1].start()
    own = pl.ds(lax.axis_index("col"), 1)
    picked = []
    for which, (width, start, stop) in enumerate(((VAL, 0, split), (CON, split, count))):
        sums[which * strips : (which + 1) * strips, :] = (
            (index[2] * width + index[which]).astype(jnp.float32).astype(jnp.bfloat16)
        )
        here = lane_matrix((index[2, own, :] * width + index[which, own, :]).astype(jnp.float32))
        parts = []
        for parity in range(2):
            hot = one_hot(2.0 * here + parity, stop - start)
            parts.append(jnp.dot(hot, bands[start:stop, :], preferred_element_type=jnp.float32))
        picked.append(jnp.concatenate(parts, 1))
    stores.append(pltpu.make_async_copy(sums, table_ref.at[pl.ds(count, 2 * strips), :], out_sems.at[1]))
    stores[-1].start()
    real, imag = densities(*picked)
    pairs[...] = jnp.concatenate([real.T, imag.T], 1).astype(jnp.bfloat16)
    for place in range(out_ref.shape[0]):
        stores.append(pltpu.make_async_copy(pairs, out_ref.at[place], pair_sems.at[place]))
        stores[-1].start()
    for copy in stores:
        copy.wait()


def rows_kernel(own_ref, partner_ref, density_ref, table, at_ref):
    core = core_of()

    @pl.when(pl.program_id(0) == 0)
    def _():
        strips = at_ref.shape[1]
        split = 2 * VAL * 4
        bands = 2 * (VAL + CON) * 4
        at_ref[0] = own_ref[bands : bands + strips, :].astype(jnp.float32)
        at_ref[1] = own_ref[bands + strips : bands + 2 * strips, :].astype(jnp.float32)
        both = jnp.concatenate([own_ref[0:bands, :], partner_ref[0:bands, :]], 1)
        for parity in range(2):
            lanes = pl.ds(parity * 2 * SLICE, 2 * SLICE)
            table[0:KPAD, lanes] = pick(KPAD, parity, both[:split])
            table[KPAD:, lanes] = pick(KPAD, parity, both[split:bands])

    picked = []
    for which in range(2):
        index = []
        for s in range(STRIPS):
            strip = lane_matrix(at_ref[which, pl.ds(pl.program_id(0) * STRIPS + s, 1), :]).reshape(-1, 2, FINE, 128)
            index.append(jnp.where(core == 0, strip[:, 0], strip[:, 1]).reshape(-1, 128))
        hot = one_hot(jnp.concatenate(index, 0), KPAD)
        picked.append(
            jnp.dot(hot, table[which * KPAD : (which + 1) * KPAD, :], preferred_element_type=jnp.float32)
        )
    density_ref[...] = jnp.concatenate(densities(*picked), 1).astype(jnp.bfloat16)


def screened_kernel(pairs_ref, own_ref, joined_ref, block_ref, out_ref, sent_ref, held, sems):
    core = core_of()
    copies = []
    for place, chip in enumerate(RING):
        lanes = pl.ds(pl.multiple_of((2 * chip + core) * SLICE, SLICE), SLICE)
        to = held.at[:, :, place * SLICE : (place + 1) * SLICE]
        copies.append(pltpu.make_async_copy(own_ref.at[:, :, lanes], to, sems.at[place]))
    for copy in copies:
        copy.start()
    pairs = pairs_ref[...].reshape(-1, 2 * WIDTH)
    chips = len(RING)
    start = joined_ref.shape[0] - JOINED * SLICE
    blocks = [joined_ref[start + i * SLICE : start + (i + 1) * SLICE, :] for i in range(JOINED)]
    blocks += [block_ref[i * SLICE : (i + 1) * SLICE, :] for i in range(2 * chips - JOINED)]
    for half in (1, 0):
        if half == 0:
            for copy in copies:
                copy.wait()
        parts = []
        for part in range(2):
            w = jnp.concatenate(blocks[part * chips : (part + 1) * chips], 1) if half else held[part]
            parts.append(jnp.dot(w, pairs, preferred_element_type=jnp.float32))
        real = parts[0][:, :WIDTH] - parts[1][:, WIDTH:]
        imag = parts[0][:, WIDTH:] + parts[1][:, :WIDTH]
        both = jnp.concatenate([real, imag], 1)
        out_ref[half] = both
        sent_ref[half] = both.astype(jnp.bfloat16)


def direct_kernel(mine_ref, other_ref, density_ref, out_ref, screened):
    for half in range(2):
        x = (mine_ref[half] + other_ref[1 - half].astype(jnp.float32)).astype(jnp.bfloat16)
        screened[half * SLICE : (half + 1) * SLICE, :] = x
        screened[(2 + half) * SLICE : (3 + half) * SLICE, :WIDTH] = x[:, WIDTH:]
        screened[(2 + half) * SLICE : (3 + half) * SLICE, WIDTH:] = -x[:, :WIDTH]
    parts = 4
    rows = density_ref.shape[0] // parts
    strips = rows // 64
    for m in range(parts):
        direct = jnp.dot(
            density_ref[m * rows : (m + 1) * rows, :], screened[...], preferred_element_type=jnp.float32
        )
        direct = direct.reshape(strips, -1, FINE, 2 * WIDTH)
        direct = jnp.concatenate([direct[s] for s in range(strips)], 1).astype(jnp.bfloat16)
        for place, chip in enumerate(RING):
            out_ref[place, m * strips * FINE : (m + 1) * strips * FINE, :] = direct[chip]


def total_kernel(in_ref, out_ref):
    for part in range(2):
        lanes = slice(part * WIDTH, (part + 1) * WIDTH)
        total = in_ref[0, :, lanes].astype(jnp.float32)
        for chip in range(1, in_ref.shape[0]):
            total += in_ref[chip, :, lanes].astype(jnp.float32)
        out_ref[part] = total


def whole(array):
    return pl.BlockSpec(array.shape, lambda *_: (0,) * len(array.shape))


def shards(valence_orbitals, conduction_orbitals, screened, valence_index, conduction_index, kpoint_index):
    bf16, f32 = jnp.bfloat16, jnp.float32
    rows = lax.axis_size("row")
    chips = rows // 2
    swap = [(i, i ^ 1) for i in range(rows)]
    same_core = [[2 * chip + core for chip in RING] for core in range(2)]
    anywhere = pl.BlockSpec(memory_space=pl.ANY)
    in_vmem = pl.BlockSpec(memory_space=pltpu.VMEM)
    index = [array.reshape(-1, 128) for array in (valence_index, conduction_index, kpoint_index)]
    strips = index[0].shape[0]
    valence = valence_orbitals.reshape(-1, SLICE)
    conduction = conduction_orbitals.reshape(-1, SLICE)
    raw = (valence, conduction, *index)
    bands = valence.shape[0] + conduction.shape[0]
    dma = pltpu.SemaphoreType.DMA
    tables, pairs, blocks = pl.pallas_call(
        columns_kernel,
        out_shape=(
            jax.ShapeDtypeStruct((bands + 2 * strips + JOINED * SLICE, SLICE), bf16),
            jax.ShapeDtypeStruct((chips, SLICE, 2 * WIDTH), bf16),
            jax.ShapeDtypeStruct(((2 * chips - JOINED) * SLICE, SLICE), bf16),
        ),
        in_specs=[anywhere] * 6,
        out_specs=(anywhere,) * 3,
        scratch_shapes=[
            pltpu.VMEM((bands, SLICE), bf16),
            pltpu.VMEM((3, strips, 128), jnp.int32),
            pltpu.VMEM((2 * strips, 128), bf16),
            pltpu.VMEM((SLICE, 2 * WIDTH), bf16),
            pltpu.VMEM((2 * chips * SLICE, SLICE), bf16),
            dma((5,)),
            dma((2, chips)),
            dma((4,)),
            dma((chips,)),
        ],
        compiler_params=ALL,
        name="columns",
    )(*raw, screened)
    pairs = lax.all_to_all(pairs, "row", 0, 0, axis_index_groups=same_core, tiled=True)
    partner_tables = lax.ppermute(tables, "row", swap)
    blocks = lax.ppermute(blocks, "row", swap)
    density = pl.pallas_call(
        rows_kernel,
        out_shape=jax.ShapeDtypeStruct((strips * 64, 4 * SLICE), bf16),
        grid=(strips // STRIPS,),
        in_specs=[whole(tables), whole(partner_tables)],
        out_specs=pl.BlockSpec((STRIPS * 64, 4 * SLICE), lambda m: (m, 0)),
        scratch_shapes=[pltpu.VMEM((2 * KPAD, 4 * SLICE), bf16), pltpu.VMEM((2, strips, 128), f32)],
        compiler_params=LITTLE,
        cost_estimate=pl.CostEstimate(flops=0, bytes_accessed=0, transcendentals=0),
        name="rows",
    )(tables, partner_tables)
    pairs, density = lax.optimization_barrier((pairs, density))
    mine, other = pl.pallas_call(
        screened_kernel,
        out_shape=tuple(jax.ShapeDtypeStruct((2, SLICE, 2 * WIDTH), kind) for kind in (f32, bf16)),
        in_specs=[in_vmem, anywhere, in_vmem, in_vmem],
        scratch_shapes=[pltpu.VMEM((2, SLICE, chips * SLICE), bf16), pltpu.SemaphoreType.DMA((chips,))],
        compiler_params=MUCH,
        name="screened",
    )(pairs, screened, partner_tables, blocks)
    other = lax.ppermute(other, "row", swap)
    partial = pl.pallas_call(
        direct_kernel,
        out_shape=jax.ShapeDtypeStruct((chips, strips * FINE, 2 * WIDTH), bf16),
        scratch_shapes=[pltpu.VMEM((4 * SLICE, 2 * WIDTH), bf16)],
        compiler_params=LITTLE,
        name="direct",
    )(mine, other, density)
    partial = lax.all_to_all(partial, "row", 0, 0, axis_index_groups=same_core, tiled=True)
    out = pl.pallas_call(
        total_kernel,
        out_shape=jax.ShapeDtypeStruct((2, strips * FINE, WIDTH), f32),
        compiler_params=LITTLE,
        name="total",
    )(partial)
    return out.reshape(2, strips, FINE, WIDTH)


def solution(mesh):
    in_specs = (
        P(None, None, None, "row"),
        P(None, None, None, "row"),
        P(None, "row", None),
        P(),
        P(),
        P(),
    )
    return jax.shard_map(
        shards, mesh=mesh, in_specs=in_specs, out_specs=P(None, None, "row", "col"), check_vma=False
    )
```

```python
import jax
import jax.numpy as jnp
from jax import lax
from jax.experimental import pallas as pl
from jax.experimental.pallas import tpu as pltpu
from jax.sharding import PartitionSpec as P

VAL = 48
CON = 64
FINE = 8
SLICE = 128
WIDTH = 128
KPAD = 256
RING = (0, 1, 2, 3, 7, 6, 5, 4)
STRIPS = 8
ROOM = 16384
FAR = 512
JOINED = 5
MIB = 1024 * 1024
LITTLE = pltpu.CompilerParams(vmem_limit_bytes=16 * MIB)
MUCH = pltpu.CompilerParams(vmem_limit_bytes=52 * MIB)
ALL = pltpu.CompilerParams(vmem_limit_bytes=63 * MIB)


def core_of():
    return lax.rem(lax.axis_index("row"), 2)


def lane_matrix(row):
    return jnp.broadcast_to(row, (128, 128)).T


def one_hot(index, width):
    lane = lax.broadcasted_iota(jnp.int32, index.shape, 1).astype(jnp.float32)
    parts = [jnp.where(index == lane + float(at), 1.0, 0.0) for at in range(0, width, index.shape[1])]
    return jnp.concatenate(parts, 1).astype(jnp.bfloat16)


def densities(valence, conduction):
    width = valence.shape[1] // 2
    v_re, v_im = valence[:, :width], valence[:, width:]
    c_re, c_im = conduction[:, :width], conduction[:, width:]
    return v_re * c_re + v_im * c_im, v_re * c_im - v_im * c_re


def pick(rows, parity, table):
    i = lax.broadcasted_iota(jnp.int32, (rows, table.shape[0]), 0)
    j = lax.broadcasted_iota(jnp.int32, (rows, table.shape[0]), 1)
    mask = jnp.where(j == 2 * i + parity, 1.0, 0.0).astype(jnp.bfloat16)
    return jnp.dot(mask, table, preferred_element_type=jnp.float32).astype(jnp.bfloat16)


def columns_kernel(
    valence_ref, conduction_ref, v_ref, n_ref, k_ref, w_ref,
    table_ref, out_ref, block_ref,
    bands, index, sums, pairs, blocks, in_sems, w_sems, out_sems, pair_sems,
):
    core = core_of()
    split = valence_ref.shape[0]
    count, strips = bands.shape[0], index.shape[1]
    places = [bands.at[pl.ds(0, split), :], bands.at[pl.ds(split, count - split), :], *[index.at[i] for i in range(3)]]
    loads = []
    for i, (ref, place) in enumerate(zip((valence_ref, conduction_ref, v_ref, n_ref, k_ref), places)):
        loads.append(pltpu.make_async_copy(ref, place, in_sems.at[i]))
    for copy in loads:
        copy.start()
    gathers = []
    for part in range(2):
        for place, chip in enumerate(RING):
            lanes = pl.ds(pl.multiple_of((2 * chip + 1 - core) * SLICE, SLICE), SLICE)
            to = blocks.at[pl.ds((part * len(RING) + place) * SLICE, SLICE), :]
            gathers.append(pltpu.make_async_copy(w_ref.at[part, :, lanes], to, w_sems.at[part, place]))
    for copy in gathers:
        copy.start()
    for copy in loads:
        copy.wait()
    stores = [pltpu.make_async_copy(bands, table_ref.at[pl.ds(0, count), :], out_sems.at[0])]
    stores[0].start()
    for copy in gathers:
        copy.wait()
    joined = JOINED * SLICE
    rest = blocks.shape[0] - joined
    to = table_ref.at[pl.ds(count + 2 * strips, joined), :]
    stores.append(pltpu.make_async_copy(blocks.at[pl.ds(0, joined), :], to, out_sems.at[2]))
    stores[-1].start()
    stores.append(pltpu.make_async_copy(blocks.at[pl.ds(joined, rest), :], block_ref, out_sems.at[3]))
    stores[-1].start()
    own = pl.ds(lax.axis_index("col"), 1)
    picked = []
    for which, (width, start, stop) in enumerate(((VAL, 0, split), (CON, split, count))):
        sums[which * strips : (which + 1) * strips, :] = (
            (index[2] * width + index[which]).astype(jnp.float32).astype(jnp.bfloat16)
        )
        here = lane_matrix((index[2, own, :] * width + index[which, own, :]).astype(jnp.float32))
        parts = []
        for parity in range(2):
            hot = one_hot(2.0 * here + parity, stop - start)
            parts.append(jnp.dot(hot, bands[start:stop, :], preferred_element_type=jnp.float32))
        picked.append(jnp.concatenate(parts, 1))
    stores.append(pltpu.make_async_copy(sums, table_ref.at[pl.ds(count, 2 * strips), :], out_sems.at[1]))
    stores[-1].start()
    real, imag = densities(*picked)
    pairs[...] = jnp.concatenate([real.T, imag.T], 1).astype(jnp.bfloat16)
    for place in range(out_ref.shape[0]):
        stores.append(pltpu.make_async_copy(pairs, out_ref.at[place], pair_sems.at[place]))
        stores[-1].start()
    for copy in stores:
        copy.wait()


def own_blocks(w_ref, to_ref, sems):
    copies = []
    for place, chip in enumerate(RING):
        lanes = pl.ds(pl.multiple_of((2 * chip + core_of()) * SLICE, SLICE), SLICE)
        to = to_ref.at[:, :, pl.ds(place * SLICE, SLICE)]
        copies.append(pltpu.make_async_copy(w_ref.at[:, :, lanes], to, sems.at[place]))
    return copies


def rows_kernel(own_ref, partner_ref, w_ref, near_ref, far_ref, kept_ref, table, at_ref, held, sems, out_sems):
    core = core_of()
    copies = own_blocks(w_ref, kept_ref, sems)
    for copy in copies:
        copy.start()
    strips = at_ref.shape[1]
    split = 2 * VAL * 4
    bands = 2 * (VAL + CON) * 4
    at_ref[0] = own_ref[bands : bands + strips, :].astype(jnp.float32)
    at_ref[1] = own_ref[bands + strips : bands + 2 * strips, :].astype(jnp.float32)
    both = jnp.concatenate([own_ref[0:bands, :], partner_ref[0:bands, :]], 1)
    for parity in range(2):
        lanes = pl.ds(parity * 2 * SLICE, 2 * SLICE)
        table[0:KPAD, lanes] = pick(KPAD, parity, both[:split])
        table[KPAD:, lanes] = pick(KPAD, parity, both[split:bands])
    rows = STRIPS * 64
    stores = []
    near = near_ref.shape[0] // rows
    for m in range(held.shape[0]):
        picked = []
        for which in range(2):
            index = []
            for s in range(m * STRIPS, (m + 1) * STRIPS):
                strip = lane_matrix(at_ref[which, s : s + 1, :]).reshape(-1, 2, FINE, 128)
                index.append(jnp.where(core == 0, strip[:, 0], strip[:, 1]).reshape(-1, 128))
            hot = one_hot(jnp.concatenate(index, 0), KPAD)
            picked.append(
                jnp.dot(hot, table[which * KPAD : (which + 1) * KPAD, :], preferred_element_type=jnp.float32)
            )
        held[m] = jnp.concatenate(densities(*picked), 1).astype(jnp.bfloat16)
        ref, at = (near_ref, m) if m < near else (far_ref, m - near)
        stores.append(pltpu.make_async_copy(held.at[m], ref.at[pl.ds(at * rows, rows), :], out_sems.at[m]))
        stores[-1].start()
    for copy in stores + copies:
        copy.wait()


def screened_kernel(pairs_ref, kept_ref, joined_ref, block_ref, far_ref, out_ref, sent_ref, back_ref, sem):
    copy = pltpu.make_async_copy(far_ref.at[pl.ds(0, FAR), :], back_ref, sem)
    copy.start()
    pairs = pairs_ref[...].reshape(-1, 2 * WIDTH)
    chips = len(RING)
    start = joined_ref.shape[0] - JOINED * SLICE
    blocks = [joined_ref[start + i * SLICE : start + (i + 1) * SLICE, :] for i in range(JOINED)]
    blocks += [block_ref[i * SLICE : (i + 1) * SLICE, :] for i in range(2 * chips - JOINED)]
    for half in range(2):
        parts = []
        for part in range(2):
            w = jnp.concatenate(blocks[part * chips : (part + 1) * chips], 1) if half else kept_ref[part]
            parts.append(jnp.dot(w, pairs, preferred_element_type=jnp.float32))
        real = parts[0][:, :WIDTH] - parts[1][:, WIDTH:]
        imag = parts[0][:, WIDTH:] + parts[1][:, :WIDTH]
        both = jnp.concatenate([real, imag], 1)
        out_ref[half] = both
        sent_ref[half] = both.astype(jnp.bfloat16)
    copy.wait()


def direct_kernel(mine_ref, other_ref, near_ref, far_ref, out_ref, screened):
    for half in range(2):
        x = (mine_ref[half] + other_ref[1 - half].astype(jnp.float32)).astype(jnp.bfloat16)
        screened[half * SLICE : (half + 1) * SLICE, :] = x
        screened[(2 + half) * SLICE : (3 + half) * SLICE, :WIDTH] = x[:, WIDTH:]
        screened[(2 + half) * SLICE : (3 + half) * SLICE, WIDTH:] = -x[:, :WIDTH]
    rows = 512
    strips = rows // 64
    near = near_ref.shape[0] // rows
    for m in range(near + far_ref.shape[0] // rows):
        ref, at = (near_ref, m * rows) if m < near else (far_ref, (m - near) * rows)
        direct = jnp.dot(ref[at : at + rows, :], screened[...], preferred_element_type=jnp.float32)
        direct = direct.reshape(strips, -1, FINE, 2 * WIDTH)
        direct = jnp.concatenate([direct[s] for s in range(strips)], 1).astype(jnp.bfloat16)
        for place, chip in enumerate(RING):
            out_ref[place, m * strips * FINE : (m + 1) * strips * FINE, :] = direct[chip]


def total_kernel(in_ref, out_ref):
    for part in range(2):
        lanes = slice(part * WIDTH, (part + 1) * WIDTH)
        total = in_ref[0, :, lanes].astype(jnp.float32)
        for chip in range(1, in_ref.shape[0]):
            total += in_ref[chip, :, lanes].astype(jnp.float32)
        out_ref[part] = total


def whole(array):
    return pl.BlockSpec(array.shape, lambda *_: (0,) * len(array.shape))


def shards(valence_orbitals, conduction_orbitals, screened, valence_index, conduction_index, kpoint_index):
    bf16, f32 = jnp.bfloat16, jnp.float32
    rows = lax.axis_size("row")
    chips = rows // 2
    swap = [(i, i ^ 1) for i in range(rows)]
    same_core = [[2 * chip + core for chip in RING] for core in range(2)]
    anywhere = pl.BlockSpec(memory_space=pl.ANY)
    in_vmem = pl.BlockSpec(memory_space=pltpu.VMEM)
    index = [array.reshape(-1, 128) for array in (valence_index, conduction_index, kpoint_index)]
    strips = index[0].shape[0]
    valence = valence_orbitals.reshape(-1, SLICE)
    conduction = conduction_orbitals.reshape(-1, SLICE)
    raw = (valence, conduction, *index)
    bands = valence.shape[0] + conduction.shape[0]
    dma = pltpu.SemaphoreType.DMA
    tables, pairs, blocks = pl.pallas_call(
        columns_kernel,
        out_shape=(
            jax.ShapeDtypeStruct((bands + 2 * strips + JOINED * SLICE, SLICE), bf16),
            jax.ShapeDtypeStruct((chips, SLICE, 2 * WIDTH), bf16),
            jax.ShapeDtypeStruct(((2 * chips - JOINED) * SLICE, SLICE), bf16),
        ),
        in_specs=[anywhere] * 6,
        out_specs=(anywhere,) * 3,
        scratch_shapes=[
            pltpu.VMEM((bands, SLICE), bf16),
            pltpu.VMEM((3, strips, 128), jnp.int32),
            pltpu.VMEM((2 * strips, 128), bf16),
            pltpu.VMEM((SLICE, 2 * WIDTH), bf16),
            pltpu.VMEM((2 * chips * SLICE, SLICE), bf16),
            dma((5,)),
            dma((2, chips)),
            dma((4,)),
            dma((chips,)),
        ],
        compiler_params=ALL,
        name="columns",
    )(*raw, screened)
    pairs = lax.all_to_all(pairs, "row", 0, 0, axis_index_groups=same_core, tiled=True)
    partner_tables = lax.ppermute(tables, "row", swap)
    blocks = lax.ppermute(blocks, "row", swap)
    near = jax.ShapeDtypeStruct((strips * 64 - FAR, 4 * SLICE), bf16)
    far = jax.ShapeDtypeStruct((ROOM, 4 * SLICE), bf16)
    kept = jax.ShapeDtypeStruct((2, SLICE, chips * SLICE), bf16)
    near, far, kept = pl.pallas_call(
        rows_kernel,
        out_shape=(near, far, kept),
        in_specs=[in_vmem, in_vmem, anywhere],
        out_specs=(anywhere, anywhere, in_vmem),
        scratch_shapes=[
            pltpu.VMEM((2 * KPAD, 4 * SLICE), bf16),
            pltpu.VMEM((2, strips, 128), f32),
            pltpu.VMEM((strips // STRIPS, STRIPS * 64, 4 * SLICE), bf16),
            dma((chips,)),
            dma((strips // STRIPS,)),
        ],
        compiler_params=pltpu.CompilerParams(vmem_limit_bytes=52 * MIB),
        cost_estimate=pl.CostEstimate(flops=0, bytes_accessed=0, transcendentals=0),
        name="rows",
    )(tables, partner_tables, screened)
    pairs, near = lax.optimization_barrier((pairs, near))
    mine, other, back = pl.pallas_call(
        screened_kernel,
        out_shape=(
            *[jax.ShapeDtypeStruct((2, SLICE, 2 * WIDTH), kind) for kind in (f32, bf16)],
            jax.ShapeDtypeStruct((FAR, 4 * SLICE), bf16),
        ),
        in_specs=[in_vmem] * 4 + [anywhere],
        scratch_shapes=[dma],
        compiler_params=pltpu.CompilerParams(vmem_limit_bytes=46 * MIB),
        name="screened",
    )(pairs, kept, partner_tables, blocks, far)
    other = lax.ppermute(other, "row", swap)
    partial = pl.pallas_call(
        direct_kernel,
        out_shape=jax.ShapeDtypeStruct((chips, strips * FINE, 2 * WIDTH), bf16),
        scratch_shapes=[pltpu.VMEM((4 * SLICE, 2 * WIDTH), bf16)],
        compiler_params=LITTLE,
        name="direct",
    )(mine, other, near, back)
    partial = lax.all_to_all(partial, "row", 0, 0, axis_index_groups=same_core, tiled=True)
    out = pl.pallas_call(
        total_kernel,
        out_shape=jax.ShapeDtypeStruct((2, strips * FINE, WIDTH), f32),
        compiler_params=LITTLE,
        name="total",
    )(partial)
    return out.reshape(2, strips, FINE, WIDTH)


def solution(mesh):
    in_specs = (
        P(None, None, None, "row"),
        P(None, None, None, "row"),
        P(None, "row", None),
        P(),
        P(),
        P(),
    )
    return jax.shard_map(
        shards, mesh=mesh, in_specs=in_specs, out_specs=P(None, None, "row", "col"), check_vma=False
    )
```

```python
import jax
import jax.numpy as jnp
from jax import lax
from jax.experimental import pallas as pl
from jax.experimental.pallas import tpu as pltpu
from jax.sharding import PartitionSpec as P

VAL = 48
CON = 64
FINE = 8
SLICE = 128
WIDTH = 128
KPAD = 256
RING = (0, 4, 1, 5, 2, 6, 3, 7)
STRIPS = 16
JOINED = 5
MIB = 1024 * 1024
LITTLE = pltpu.CompilerParams(vmem_limit_bytes=16 * MIB)
MUCH = pltpu.CompilerParams(vmem_limit_bytes=52 * MIB)
ALL = pltpu.CompilerParams(vmem_limit_bytes=63 * MIB)


def core_of():
    return lax.rem(lax.axis_index("row"), 2)


def lane_matrix(row):
    return jnp.broadcast_to(row, (128, 128)).T


def one_hot(index, width):
    lane = lax.broadcasted_iota(jnp.int32, index.shape, 1).astype(jnp.float32)
    parts = [jnp.where(index == lane + float(at), 1.0, 0.0) for at in range(0, width, index.shape[1])]
    return jnp.concatenate(parts, 1).astype(jnp.bfloat16)


def densities(valence, conduction):
    width = valence.shape[1] // 2
    v_re, v_im = valence[:, :width], valence[:, width:]
    c_re, c_im = conduction[:, :width], conduction[:, width:]
    return v_re * c_re + v_im * c_im, v_re * c_im - v_im * c_re


def pick(rows, parity, table):
    i = lax.broadcasted_iota(jnp.int32, (rows, table.shape[0]), 0)
    j = lax.broadcasted_iota(jnp.int32, (rows, table.shape[0]), 1)
    mask = jnp.where(j == 2 * i + parity, 1.0, 0.0).astype(jnp.bfloat16)
    return jnp.dot(mask, table, preferred_element_type=jnp.float32).astype(jnp.bfloat16)


def columns_kernel(
    valence_ref, conduction_ref, v_ref, n_ref, k_ref, w_ref,
    table_ref, out_ref, block_ref,
    bands, index, sums, pairs, blocks, in_sems, w_sems, out_sems, pair_sems,
):
    core = core_of()
    split = valence_ref.shape[0]
    count, strips = bands.shape[0], index.shape[1]
    places = [bands.at[pl.ds(0, split), :], bands.at[pl.ds(split, count - split), :], *[index.at[i] for i in range(3)]]
    loads = []
    for i, (ref, place) in enumerate(zip((valence_ref, conduction_ref, v_ref, n_ref, k_ref), places)):
        loads.append(pltpu.make_async_copy(ref, place, in_sems.at[i]))
    for copy in loads:
        copy.start()
    gathers = []
    for part in range(2):
        for place, chip in enumerate(RING):
            lanes = pl.ds(pl.multiple_of((2 * chip + 1 - core) * SLICE, SLICE), SLICE)
            to = blocks.at[pl.ds((part * len(RING) + place) * SLICE, SLICE), :]
            gathers.append(pltpu.make_async_copy(w_ref.at[part, :, lanes], to, w_sems.at[part, place]))
    for copy in gathers:
        copy.start()
    for copy in loads:
        copy.wait()
    stores = [pltpu.make_async_copy(bands, table_ref.at[pl.ds(0, count), :], out_sems.at[0])]
    stores[0].start()
    for copy in gathers:
        copy.wait()
    joined = JOINED * SLICE
    rest = blocks.shape[0] - joined
    to = table_ref.at[pl.ds(count + 2 * strips, joined), :]
    stores.append(pltpu.make_async_copy(blocks.at[pl.ds(0, joined), :], to, out_sems.at[2]))
    stores[-1].start()
    stores.append(pltpu.make_async_copy(blocks.at[pl.ds(joined, rest), :], block_ref, out_sems.at[3]))
    stores[-1].start()
    own = pl.ds(lax.axis_index("col"), 1)
    picked = []
    for which, (width, start, stop) in enumerate(((VAL, 0, split), (CON, split, count))):
        sums[which * strips : (which + 1) * strips, :] = (
            (index[2] * width + index[which]).astype(jnp.float32).astype(jnp.bfloat16)
        )
        here = lane_matrix((index[2, own, :] * width + index[which, own, :]).astype(jnp.float32))
        parts = []
        for parity in range(2):
            hot = one_hot(2.0 * here + parity, stop - start)
            parts.append(jnp.dot(hot, bands[start:stop, :], preferred_element_type=jnp.float32))
        picked.append(jnp.concatenate(parts, 1))
    stores.append(pltpu.make_async_copy(sums, table_ref.at[pl.ds(count, 2 * strips), :], out_sems.at[1]))
    stores[-1].start()
    real, imag = densities(*picked)
    pairs[...] = jnp.concatenate([real.T, imag.T], 1).astype(jnp.bfloat16)
    for place in range(out_ref.shape[0]):
        stores.append(pltpu.make_async_copy(pairs, out_ref.at[place], pair_sems.at[place]))
        stores[-1].start()
    for copy in stores:
        copy.wait()


def rows_kernel(own_ref, partner_ref, density_ref, table, at_ref):
    core = core_of()

    @pl.when(pl.program_id(0) == 0)
    def _():
        strips = at_ref.shape[1]
        split = 2 * VAL * 4
        bands = 2 * (VAL + CON) * 4
        at_ref[0] = own_ref[bands : bands + strips, :].astype(jnp.float32)
        at_ref[1] = own_ref[bands + strips : bands + 2 * strips, :].astype(jnp.float32)
        both = jnp.concatenate([own_ref[0:bands, :], partner_ref[0:bands, :]], 1)
        for parity in range(2):
            lanes = pl.ds(parity * 2 * SLICE, 2 * SLICE)
            table[0:KPAD, lanes] = pick(KPAD, parity, both[:split])
            table[KPAD:, lanes] = pick(KPAD, parity, both[split:bands])

    picked = []
    for which in range(2):
        index = []
        for s in range(STRIPS):
            strip = lane_matrix(at_ref[which, pl.ds(pl.program_id(0) * STRIPS + s, 1), :]).reshape(-1, 2, FINE, 128)
            index.append(jnp.where(core == 0, strip[:, 0], strip[:, 1]).reshape(-1, 128))
        hot = one_hot(jnp.concatenate(index, 0), KPAD)
        picked.append(
            jnp.dot(hot, table[which * KPAD : (which + 1) * KPAD, :], preferred_element_type=jnp.float32)
        )
    density_ref[...] = jnp.concatenate(densities(*picked), 1).astype(jnp.bfloat16)


def screened_kernel(pairs_ref, own_ref, joined_ref, block_ref, out_ref, sent_ref, held, sems):
    core = core_of()
    copies = []
    for place, chip in enumerate(RING):
        lanes = pl.ds(pl.multiple_of((2 * chip + core) * SLICE, SLICE), SLICE)
        to = held.at[:, :, place * SLICE : (place + 1) * SLICE]
        copies.append(pltpu.make_async_copy(own_ref.at[:, :, lanes], to, sems.at[place]))
    for copy in copies:
        copy.start()
    pairs = pairs_ref[...].reshape(-1, 2 * WIDTH)
    chips = len(RING)
    start = joined_ref.shape[0] - JOINED * SLICE
    blocks = [joined_ref[start + i * SLICE : start + (i + 1) * SLICE, :] for i in range(JOINED)]
    blocks += [block_ref[i * SLICE : (i + 1) * SLICE, :] for i in range(2 * chips - JOINED)]
    for half in (1, 0):
        if half == 0:
            for copy in copies:
                copy.wait()
        parts = []
        for part in range(2):
            w = jnp.concatenate(blocks[part * chips : (part + 1) * chips], 1) if half else held[part]
            parts.append(jnp.dot(w, pairs, preferred_element_type=jnp.float32))
        real = parts[0][:, :WIDTH] - parts[1][:, WIDTH:]
        imag = parts[0][:, WIDTH:] + parts[1][:, :WIDTH]
        both = jnp.concatenate([real, imag], 1)
        out_ref[half] = both
        sent_ref[half] = both.astype(jnp.bfloat16)


def direct_kernel(mine_ref, other_ref, density_ref, out_ref, screened):
    for half in range(2):
        x = (mine_ref[half] + other_ref[1 - half].astype(jnp.float32)).astype(jnp.bfloat16)
        screened[half * SLICE : (half + 1) * SLICE, :] = x
        screened[(2 + half) * SLICE : (3 + half) * SLICE, :WIDTH] = x[:, WIDTH:]
        screened[(2 + half) * SLICE : (3 + half) * SLICE, WIDTH:] = -x[:, :WIDTH]
    parts = 4
    rows = density_ref.shape[0] // parts
    strips = rows // 64
    for m in range(parts):
        direct = jnp.dot(
            density_ref[m * rows : (m + 1) * rows, :], screened[...], preferred_element_type=jnp.float32
        )
        direct = direct.reshape(strips, -1, FINE, 2 * WIDTH)
        direct = jnp.concatenate([direct[s] for s in range(strips)], 1).astype(jnp.bfloat16)
        for place, chip in enumerate(RING):
            out_ref[place, m * strips * FINE : (m + 1) * strips * FINE, :] = direct[chip]


def total_kernel(in_ref, out_ref):
    for part in range(2):
        lanes = slice(part * WIDTH, (part + 1) * WIDTH)
        total = in_ref[0, :, lanes].astype(jnp.float32)
        for chip in range(1, in_ref.shape[0]):
            total += in_ref[chip, :, lanes].astype(jnp.float32)
        out_ref[part] = total


def whole(array):
    return pl.BlockSpec(array.shape, lambda *_: (0,) * len(array.shape))


def shards(valence_orbitals, conduction_orbitals, screened, valence_index, conduction_index, kpoint_index):
    bf16, f32 = jnp.bfloat16, jnp.float32
    rows = lax.axis_size("row")
    chips = rows // 2
    swap = [(i, i ^ 1) for i in range(rows)]
    same_core = [[2 * chip + core for chip in RING] for core in range(2)]
    anywhere = pl.BlockSpec(memory_space=pl.ANY)
    in_vmem = pl.BlockSpec(memory_space=pltpu.VMEM)
    index = [array.reshape(-1, 128) for array in (valence_index, conduction_index, kpoint_index)]
    strips = index[0].shape[0]
    valence = valence_orbitals.reshape(-1, SLICE)
    conduction = conduction_orbitals.reshape(-1, SLICE)
    raw = (valence, conduction, *index)
    bands = valence.shape[0] + conduction.shape[0]
    dma = pltpu.SemaphoreType.DMA
    tables, pairs, blocks = pl.pallas_call(
        columns_kernel,
        out_shape=(
            jax.ShapeDtypeStruct((bands + 2 * strips + JOINED * SLICE, SLICE), bf16),
            jax.ShapeDtypeStruct((chips, SLICE, 2 * WIDTH), bf16),
            jax.ShapeDtypeStruct(((2 * chips - JOINED) * SLICE, SLICE), bf16),
        ),
        in_specs=[anywhere] * 6,
        out_specs=(anywhere,) * 3,
        scratch_shapes=[
            pltpu.VMEM((bands, SLICE), bf16),
            pltpu.VMEM((3, strips, 128), jnp.int32),
            pltpu.VMEM((2 * strips, 128), bf16),
            pltpu.VMEM((SLICE, 2 * WIDTH), bf16),
            pltpu.VMEM((2 * chips * SLICE, SLICE), bf16),
            dma((5,)),
            dma((2, chips)),
            dma((4,)),
            dma((chips,)),
        ],
        compiler_params=ALL,
        name="columns",
    )(*raw, screened)
    pairs = lax.all_to_all(pairs, "row", 0, 0, axis_index_groups=same_core, tiled=True)
    partner_tables = lax.ppermute(tables, "row", swap)
    blocks = lax.ppermute(blocks, "row", swap)
    density = pl.pallas_call(
        rows_kernel,
        out_shape=jax.ShapeDtypeStruct((strips * 64, 4 * SLICE), bf16),
        grid=(strips // STRIPS,),
        in_specs=[whole(tables), whole(partner_tables)],
        out_specs=pl.BlockSpec((STRIPS * 64, 4 * SLICE), lambda m: (m, 0)),
        scratch_shapes=[pltpu.VMEM((2 * KPAD, 4 * SLICE), bf16), pltpu.VMEM((2, strips, 128), f32)],
        compiler_params=LITTLE,
        cost_estimate=pl.CostEstimate(flops=0, bytes_accessed=0, transcendentals=0),
        name="rows",
    )(tables, partner_tables)
    pairs, density = lax.optimization_barrier((pairs, density))
    mine, other = pl.pallas_call(
        screened_kernel,
        out_shape=tuple(jax.ShapeDtypeStruct((2, SLICE, 2 * WIDTH), kind) for kind in (f32, bf16)),
        in_specs=[in_vmem, anywhere, in_vmem, in_vmem],
        scratch_shapes=[pltpu.VMEM((2, SLICE, chips * SLICE), bf16), pltpu.SemaphoreType.DMA((chips,))],
        compiler_params=MUCH,
        name="screened",
    )(pairs, screened, partner_tables, blocks)
    other = lax.ppermute(other, "row", swap)
    partial = pl.pallas_call(
        direct_kernel,
        out_shape=jax.ShapeDtypeStruct((chips, strips * FINE, 2 * WIDTH), bf16),
        scratch_shapes=[pltpu.VMEM((4 * SLICE, 2 * WIDTH), bf16)],
        compiler_params=LITTLE,
        name="direct",
    )(mine, other, density)
    partial = lax.all_to_all(partial, "row", 0, 0, axis_index_groups=same_core, tiled=True)
    out = pl.pallas_call(
        total_kernel,
        out_shape=jax.ShapeDtypeStruct((2, strips * FINE, WIDTH), f32),
        compiler_params=LITTLE,
        name="total",
    )(partial)
    return out.reshape(2, strips, FINE, WIDTH)


def solution(mesh):
    in_specs = (
        P(None, None, None, "row"),
        P(None, None, None, "row"),
        P(None, "row", None),
        P(),
        P(),
        P(),
    )
    return jax.shard_map(
        shards, mesh=mesh, in_specs=in_specs, out_specs=P(None, None, "row", "col"), check_vma=False
    )
```

```python
import jax
import jax.numpy as jnp
from jax import lax
from jax.experimental import pallas as pl
from jax.experimental.pallas import tpu as pltpu
from jax.sharding import PartitionSpec as P

VAL = 48
CON = 64
FINE = 8
SLICE = 128
WIDTH = 128
KPAD = 256
RING = (0, 4, 1, 5, 2, 6, 3, 7)
STRIPS = 32
JOINED = 5
MIB = 1024 * 1024
LITTLE = pltpu.CompilerParams(vmem_limit_bytes=16 * MIB)
MUCH = pltpu.CompilerParams(vmem_limit_bytes=52 * MIB)
ALL = pltpu.CompilerParams(vmem_limit_bytes=63 * MIB)


def core_of():
    return lax.rem(lax.axis_index("row"), 2)


def lane_matrix(row):
    return jnp.broadcast_to(row, (128, 128)).T


def one_hot(index, width):
    lane = lax.broadcasted_iota(jnp.int32, index.shape, 1).astype(jnp.float32)
    parts = [jnp.where(index == lane + float(at), 1.0, 0.0) for at in range(0, width, index.shape[1])]
    return jnp.concatenate(parts, 1).astype(jnp.bfloat16)


def densities(valence, conduction):
    width = valence.shape[1] // 2
    v_re, v_im = valence[:, :width], valence[:, width:]
    c_re, c_im = conduction[:, :width], conduction[:, width:]
    return v_re * c_re + v_im * c_im, v_re * c_im - v_im * c_re


def pick(parity, table):
    i = lax.broadcasted_iota(jnp.int32, (128, 256), 0)
    j = lax.broadcasted_iota(jnp.int32, (128, 256), 1)
    mask = jnp.where(j == 2 * i + parity, 1.0, 0.0).astype(jnp.bfloat16)
    parts = []
    for start in range(0, table.shape[0], 256):
        count = min(256, table.shape[0] - start)
        part = table[start : start + count]
        parts.append(jnp.dot(mask[: count // 2, :count], part, preferred_element_type=jnp.float32))
    missing = KPAD - table.shape[0] // 2
    if missing:
        parts.append(jnp.zeros((missing, table.shape[1]), jnp.float32))
    return jnp.concatenate(parts, 0).astype(jnp.bfloat16)


def columns_kernel(
    valence_ref, conduction_ref, v_ref, n_ref, k_ref, w_ref,
    table_ref, out_ref, block_ref,
    bands, index, sums, pairs, blocks, in_sems, w_sems, out_sems, pair_sems,
):
    core = core_of()
    split = valence_ref.shape[0]
    count, strips = bands.shape[0], index.shape[1]
    places = [bands.at[pl.ds(0, split), :], bands.at[pl.ds(split, count - split), :], *[index.at[i] for i in range(3)]]
    loads = []
    for i, (ref, place) in enumerate(zip((valence_ref, conduction_ref, v_ref, n_ref, k_ref), places)):
        loads.append(pltpu.make_async_copy(ref, place, in_sems.at[i]))
    for copy in loads:
        copy.start()
    gathers = []
    for part in range(2):
        for place, chip in enumerate(RING):
            lanes = pl.ds(pl.multiple_of((2 * chip + 1 - core) * SLICE, SLICE), SLICE)
            to = blocks.at[pl.ds((part * len(RING) + place) * SLICE, SLICE), :]
            gathers.append(pltpu.make_async_copy(w_ref.at[part, :, lanes], to, w_sems.at[part, place]))
    for copy in gathers:
        copy.start()
    for copy in loads:
        copy.wait()
    stores = [pltpu.make_async_copy(bands, table_ref.at[pl.ds(0, count), :], out_sems.at[0])]
    stores[0].start()
    for copy in gathers:
        copy.wait()
    joined = JOINED * SLICE
    rest = blocks.shape[0] - joined
    to = table_ref.at[pl.ds(count + 2 * strips, joined), :]
    stores.append(pltpu.make_async_copy(blocks.at[pl.ds(0, joined), :], to, out_sems.at[2]))
    stores[-1].start()
    stores.append(pltpu.make_async_copy(blocks.at[pl.ds(joined, rest), :], block_ref, out_sems.at[3]))
    stores[-1].start()
    own = pl.ds(lax.axis_index("col"), 1)
    picked = []
    for which, (width, start, stop) in enumerate(((VAL, 0, split), (CON, split, count))):
        sums[which * strips : (which + 1) * strips, :] = (
            (index[2] * width + index[which]).astype(jnp.float32).astype(jnp.bfloat16)
        )
        here = lane_matrix((index[2, own, :] * width + index[which, own, :]).astype(jnp.float32))
        parts = []
        for parity in range(2):
            hot = one_hot(2.0 * here + parity, stop - start)
            parts.append(jnp.dot(hot, bands[start:stop, :], preferred_element_type=jnp.float32))
        picked.append(jnp.concatenate(parts, 1))
    stores.append(pltpu.make_async_copy(sums, table_ref.at[pl.ds(count, 2 * strips), :], out_sems.at[1]))
    stores[-1].start()
    real, imag = densities(*picked)
    pairs[...] = jnp.concatenate([real.T, imag.T], 1).astype(jnp.bfloat16)
    for place in range(out_ref.shape[0]):
        stores.append(pltpu.make_async_copy(pairs, out_ref.at[place], pair_sems.at[place]))
        stores[-1].start()
    for copy in stores:
        copy.wait()


def rows_kernel(own_ref, partner_ref, density_ref, table, at_ref):
    core = core_of()

    @pl.when(pl.program_id(0) == 0)
    def _():
        strips = at_ref.shape[1]
        split = 2 * VAL * 4
        bands = 2 * (VAL + CON) * 4
        at_ref[0] = own_ref[bands : bands + strips, :].astype(jnp.float32)
        at_ref[1] = own_ref[bands + strips : bands + 2 * strips, :].astype(jnp.float32)
        both = jnp.concatenate([own_ref[0:bands, :], partner_ref[0:bands, :]], 1)
        for parity in range(2):
            lanes = pl.ds(parity * 2 * SLICE, 2 * SLICE)
            table[0:KPAD, lanes] = pick(parity, both[:split])
            table[KPAD:, lanes] = pick(parity, both[split:bands])

    picked = []
    for which in range(2):
        index = []
        for s in range(STRIPS):
            strip = lane_matrix(at_ref[which, pl.ds(pl.program_id(0) * STRIPS + s, 1), :]).reshape(-1, 2, FINE, 128)
            index.append(jnp.where(core == 0, strip[:, 0], strip[:, 1]).reshape(-1, 128))
        hot = one_hot(jnp.concatenate(index, 0), KPAD)
        picked.append(
            jnp.dot(hot, table[which * KPAD : (which + 1) * KPAD, :], preferred_element_type=jnp.float32)
        )
    density_ref[...] = jnp.concatenate(densities(*picked), 1).astype(jnp.bfloat16)


def screened_kernel(pairs_ref, own_ref, joined_ref, block_ref, out_ref, sent_ref, held, sems):
    core = core_of()
    copies = []
    for place, chip in enumerate(RING):
        lanes = pl.ds(pl.multiple_of((2 * chip + core) * SLICE, SLICE), SLICE)
        to = held.at[:, :, place * SLICE : (place + 1) * SLICE]
        copies.append(pltpu.make_async_copy(own_ref.at[:, :, lanes], to, sems.at[place]))
    for copy in copies:
        copy.start()
    pairs = pairs_ref[...].reshape(-1, 2 * WIDTH)
    chips = len(RING)
    start = joined_ref.shape[0] - JOINED * SLICE
    blocks = [joined_ref[start + i * SLICE : start + (i + 1) * SLICE, :] for i in range(JOINED)]
    blocks += [block_ref[i * SLICE : (i + 1) * SLICE, :] for i in range(2 * chips - JOINED)]
    for half in (1, 0):
        if half == 0:
            for copy in copies:
                copy.wait()
        parts = []
        for part in range(2):
            w = jnp.concatenate(blocks[part * chips : (part + 1) * chips], 1) if half else held[part]
            parts.append(jnp.dot(w, pairs, preferred_element_type=jnp.float32))
        real = parts[0][:, :WIDTH] - parts[1][:, WIDTH:]
        imag = parts[0][:, WIDTH:] + parts[1][:, :WIDTH]
        both = jnp.concatenate([real, imag], 1)
        out_ref[half] = both
        sent_ref[half] = both.astype(jnp.bfloat16)


def direct_kernel(mine_ref, other_ref, density_ref, out_ref, screened):
    for half in range(2):
        x = (mine_ref[half] + other_ref[1 - half].astype(jnp.float32)).astype(jnp.bfloat16)
        screened[half * SLICE : (half + 1) * SLICE, :] = x
        screened[(2 + half) * SLICE : (3 + half) * SLICE, :WIDTH] = x[:, WIDTH:]
        screened[(2 + half) * SLICE : (3 + half) * SLICE, WIDTH:] = -x[:, :WIDTH]
    parts = 4
    rows = density_ref.shape[0] // parts
    strips = rows // 64
    for m in range(parts):
        direct = jnp.dot(
            density_ref[m * rows : (m + 1) * rows, :], screened[...], preferred_element_type=jnp.float32
        )
        direct = direct.reshape(strips, -1, FINE, 2 * WIDTH)
        direct = jnp.concatenate([direct[s] for s in range(strips)], 1).astype(jnp.bfloat16)
        for place, chip in enumerate(RING):
            out_ref[place, m * strips * FINE : (m + 1) * strips * FINE, :] = direct[chip]


def total_kernel(in_ref, out_ref):
    for part in range(2):
        lanes = slice(part * WIDTH, (part + 1) * WIDTH)
        total = in_ref[0, :, lanes].astype(jnp.float32)
        for chip in range(1, in_ref.shape[0]):
            total += in_ref[chip, :, lanes].astype(jnp.float32)
        out_ref[part] = total


def whole(array):
    return pl.BlockSpec(array.shape, lambda *_: (0,) * len(array.shape))


def shards(valence_orbitals, conduction_orbitals, screened, valence_index, conduction_index, kpoint_index):
    bf16, f32 = jnp.bfloat16, jnp.float32
    rows = lax.axis_size("row")
    chips = rows // 2
    swap = [(i, i ^ 1) for i in range(rows)]
    same_core = [[2 * chip + core for chip in RING] for core in range(2)]
    anywhere = pl.BlockSpec(memory_space=pl.ANY)
    in_vmem = pl.BlockSpec(memory_space=pltpu.VMEM)
    index = [array.reshape(-1, 128) for array in (valence_index, conduction_index, kpoint_index)]
    strips = index[0].shape[0]
    valence = valence_orbitals.reshape(-1, SLICE)
    conduction = conduction_orbitals.reshape(-1, SLICE)
    raw = (valence, conduction, *index)
    bands = valence.shape[0] + conduction.shape[0]
    dma = pltpu.SemaphoreType.DMA
    tables, pairs, blocks = pl.pallas_call(
        columns_kernel,
        out_shape=(
            jax.ShapeDtypeStruct((bands + 2 * strips + JOINED * SLICE, SLICE), bf16),
            jax.ShapeDtypeStruct((chips, SLICE, 2 * WIDTH), bf16),
            jax.ShapeDtypeStruct(((2 * chips - JOINED) * SLICE, SLICE), bf16),
        ),
        in_specs=[anywhere] * 6,
        out_specs=(anywhere,) * 3,
        scratch_shapes=[
            pltpu.VMEM((bands, SLICE), bf16),
            pltpu.VMEM((3, strips, 128), jnp.int32),
            pltpu.VMEM((2 * strips, 128), bf16),
            pltpu.VMEM((SLICE, 2 * WIDTH), bf16),
            pltpu.VMEM((2 * chips * SLICE, SLICE), bf16),
            dma((5,)),
            dma((2, chips)),
            dma((4,)),
            dma((chips,)),
        ],
        compiler_params=ALL,
        name="columns",
    )(*raw, screened)
    pairs = lax.all_to_all(pairs, "row", 0, 0, axis_index_groups=same_core, tiled=True)
    partner_tables = lax.ppermute(tables, "row", swap)
    blocks = lax.ppermute(blocks, "row", swap)
    density = pl.pallas_call(
        rows_kernel,
        out_shape=jax.ShapeDtypeStruct((strips * 64, 4 * SLICE), bf16),
        grid=(strips // STRIPS,),
        in_specs=[whole(tables), whole(partner_tables)],
        out_specs=pl.BlockSpec((STRIPS * 64, 4 * SLICE), lambda m: (m, 0)),
        scratch_shapes=[pltpu.VMEM((2 * KPAD, 4 * SLICE), bf16), pltpu.VMEM((2, strips, 128), f32)],
        compiler_params=LITTLE,
        cost_estimate=pl.CostEstimate(flops=0, bytes_accessed=0, transcendentals=0),
        name="rows",
    )(tables, partner_tables)
    pairs, density = lax.optimization_barrier((pairs, density))
    mine, other = pl.pallas_call(
        screened_kernel,
        out_shape=tuple(jax.ShapeDtypeStruct((2, SLICE, 2 * WIDTH), kind) for kind in (f32, bf16)),
        in_specs=[in_vmem, anywhere, in_vmem, in_vmem],
        scratch_shapes=[pltpu.VMEM((2, SLICE, chips * SLICE), bf16), pltpu.SemaphoreType.DMA((chips,))],
        compiler_params=MUCH,
        name="screened",
    )(pairs, screened, partner_tables, blocks)
    other = lax.ppermute(other, "row", swap)
    partial = pl.pallas_call(
        direct_kernel,
        out_shape=jax.ShapeDtypeStruct((chips, strips * FINE, 2 * WIDTH), bf16),
        scratch_shapes=[pltpu.VMEM((4 * SLICE, 2 * WIDTH), bf16)],
        compiler_params=LITTLE,
        name="direct",
    )(mine, other, density)
    partial = lax.all_to_all(partial, "row", 0, 0, axis_index_groups=same_core, tiled=True)
    out = pl.pallas_call(
        total_kernel,
        out_shape=jax.ShapeDtypeStruct((2, strips * FINE, WIDTH), f32),
        compiler_params=LITTLE,
        name="total",
    )(partial)
    return out.reshape(2, strips, FINE, WIDTH)


def solution(mesh):
    in_specs = (
        P(None, None, None, "row"),
        P(None, None, None, "row"),
        P(None, "row", None),
        P(),
        P(),
        P(),
    )
    return jax.shard_map(
        shards, mesh=mesh, in_specs=in_specs, out_specs=P(None, None, "row", "col"), check_vma=False
    )
```

```python
import jax
import jax.numpy as jnp
from jax import lax
from jax.experimental import pallas as pl
from jax.experimental.pallas import tpu as pltpu
from jax.sharding import PartitionSpec as P

VAL = 48
CON = 64
FINE = 8
SLICE = 128
WIDTH = 128
KPAD = 256
RING = (0, 4, 1, 5, 2, 6, 3, 7)
STRIPS = 32
JOINED = 5
ROOM = 65536
MIB = 1024 * 1024
LITTLE = pltpu.CompilerParams(vmem_limit_bytes=16 * MIB)
MUCH = pltpu.CompilerParams(vmem_limit_bytes=52 * MIB)
ALL = pltpu.CompilerParams(vmem_limit_bytes=63 * MIB)


def core_of():
    return lax.rem(lax.axis_index("row"), 2)


def lane_matrix(row):
    return jnp.broadcast_to(row, (128, 128)).T


def one_hot(index, width):
    lane = lax.broadcasted_iota(jnp.int32, index.shape, 1).astype(jnp.float32)
    parts = [jnp.where(index == lane + float(at), 1.0, 0.0) for at in range(0, width, index.shape[1])]
    return jnp.concatenate(parts, 1).astype(jnp.bfloat16)


def densities(valence, conduction):
    width = valence.shape[1] // 2
    v_re, v_im = valence[:, :width], valence[:, width:]
    c_re, c_im = conduction[:, :width], conduction[:, width:]
    return v_re * c_re + v_im * c_im, v_re * c_im - v_im * c_re


def pick(parity, table):
    i = lax.broadcasted_iota(jnp.int32, (128, 256), 0)
    j = lax.broadcasted_iota(jnp.int32, (128, 256), 1)
    mask = jnp.where(j == 2 * i + parity, 1.0, 0.0).astype(jnp.bfloat16)
    parts = []
    for start in range(0, table.shape[0], 256):
        count = min(256, table.shape[0] - start)
        part = table[start : start + count]
        parts.append(jnp.dot(mask[: count // 2, :count], part, preferred_element_type=jnp.float32))
    missing = KPAD - table.shape[0] // 2
    if missing:
        parts.append(jnp.zeros((missing, table.shape[1]), jnp.float32))
    return jnp.concatenate(parts, 0).astype(jnp.bfloat16)


def columns_kernel(
    valence_ref, conduction_ref, v_ref, n_ref, k_ref, w_ref,
    table_ref, out_ref, block_ref, own_ref,
    bands, index, sums, pairs, blocks, in_sems, w_sems, out_sems, pair_sems,
):
    core = core_of()
    split = valence_ref.shape[0]
    count, strips = bands.shape[0], index.shape[1]
    places = [bands.at[pl.ds(0, split), :], bands.at[pl.ds(split, count - split), :], *[index.at[i] for i in range(3)]]
    loads = []
    for i, (ref, place) in enumerate(zip((valence_ref, conduction_ref, v_ref, n_ref, k_ref), places)):
        loads.append(pltpu.make_async_copy(ref, place, in_sems.at[i]))
    for copy in loads:
        copy.start()
    gathers = []
    for part in range(2):
        for place, chip in enumerate(RING):
            lanes = pl.ds(pl.multiple_of((2 * chip + 1 - core) * SLICE, SLICE), SLICE)
            to = blocks.at[pl.ds((part * len(RING) + place) * SLICE, SLICE), :]
            gathers.append(pltpu.make_async_copy(w_ref.at[part, :, lanes], to, w_sems.at[part, place]))
    for copy in gathers:
        copy.start()
    for copy in loads:
        copy.wait()
    stores = [
        pltpu.make_async_copy(bands, table_ref.at[pl.ds(0, count), :], out_sems.at[0]),
        pltpu.make_async_copy(bands, own_ref.at[pl.ds(0, count), :], out_sems.at[4]),
    ]
    stores[0].start()
    stores[1].start()
    for copy in gathers:
        copy.wait()
    joined = JOINED * SLICE
    rest = blocks.shape[0] - joined
    to = table_ref.at[pl.ds(count + 2 * strips, joined), :]
    stores.append(pltpu.make_async_copy(blocks.at[pl.ds(0, joined), :], to, out_sems.at[2]))
    stores[-1].start()
    stores.append(pltpu.make_async_copy(blocks.at[pl.ds(joined, rest), :], block_ref, out_sems.at[3]))
    stores[-1].start()
    own = pl.ds(lax.axis_index("col"), 1)
    picked = []
    for which, (width, start, stop) in enumerate(((VAL, 0, split), (CON, split, count))):
        sums[which * strips : (which + 1) * strips, :] = (
            (index[2] * width + index[which]).astype(jnp.float32).astype(jnp.bfloat16)
        )
        here = lane_matrix((index[2, own, :] * width + index[which, own, :]).astype(jnp.float32))
        parts = []
        for parity in range(2):
            hot = one_hot(2.0 * here + parity, stop - start)
            parts.append(jnp.dot(hot, bands[start:stop, :], preferred_element_type=jnp.float32))
        picked.append(jnp.concatenate(parts, 1))
    for i, ref in ((1, table_ref), (5, own_ref)):
        stores.append(pltpu.make_async_copy(sums, ref.at[pl.ds(count, 2 * strips), :], out_sems.at[i]))
        stores[-1].start()
    real, imag = densities(*picked)
    pairs[...] = jnp.concatenate([real.T, imag.T], 1).astype(jnp.bfloat16)
    for place in range(out_ref.shape[0]):
        stores.append(pltpu.make_async_copy(pairs, out_ref.at[place], pair_sems.at[place]))
        stores[-1].start()
    for copy in stores:
        copy.wait()


def rows_kernel(own_ref, partner_ref, density_ref, table, at_ref, held, sem):
    core = core_of()

    copy = pltpu.make_async_copy(own_ref.at[pl.ds(0, held.shape[0]), :], held, sem)
    copy.start()
    strips = at_ref.shape[1]
    split = 2 * VAL * 4
    bands = 2 * (VAL + CON) * 4
    for place, ref in ((1, partner_ref), (0, held)):
        if place == 0:
            copy.wait()
        for parity in range(2):
            lanes = slice((2 * parity + place) * SLICE, (2 * parity + place + 1) * SLICE)
            table[0:KPAD, lanes] = pick(parity, ref[0:split, :])
            table[KPAD:, lanes] = pick(parity, ref[split:bands, :])
    at_ref[0] = held[bands : bands + strips, :].astype(jnp.float32)
    at_ref[1] = held[bands + strips : bands + 2 * strips, :].astype(jnp.float32)
    picked = []
    for which in range(2):
        index = []
        for s in range(STRIPS):
            strip = lane_matrix(at_ref[which, pl.ds(pl.program_id(0) * STRIPS + s, 1), :]).reshape(-1, 2, FINE, 128)
            index.append(jnp.where(core == 0, strip[:, 0], strip[:, 1]).reshape(-1, 128))
        hot = one_hot(jnp.concatenate(index, 0), KPAD)
        picked.append(
            jnp.dot(hot, table[which * KPAD : (which + 1) * KPAD, :], preferred_element_type=jnp.float32)
        )
    density_ref[...] = jnp.concatenate(densities(*picked), 1).astype(jnp.bfloat16)


def screened_kernel(pairs_ref, own_ref, joined_ref, block_ref, out_ref, sent_ref, held, sems):
    core = core_of()
    copies = []
    for place, chip in enumerate(RING):
        lanes = pl.ds(pl.multiple_of((2 * chip + core) * SLICE, SLICE), SLICE)
        to = held.at[:, :, place * SLICE : (place + 1) * SLICE]
        copies.append(pltpu.make_async_copy(own_ref.at[:, :, lanes], to, sems.at[place]))
    for copy in copies:
        copy.start()
    pairs = pairs_ref[...].reshape(-1, 2 * WIDTH)
    chips = len(RING)
    start = joined_ref.shape[0] - JOINED * SLICE
    blocks = [joined_ref[start + i * SLICE : start + (i + 1) * SLICE, :] for i in range(JOINED)]
    blocks += [block_ref[i * SLICE : (i + 1) * SLICE, :] for i in range(2 * chips - JOINED)]
    for half in (1, 0):
        if half == 0:
            for copy in copies:
                copy.wait()
        parts = []
        for part in range(2):
            w = jnp.concatenate(blocks[part * chips : (part + 1) * chips], 1) if half else held[part]
            parts.append(jnp.dot(w, pairs, preferred_element_type=jnp.float32))
        real = parts[0][:, :WIDTH] - parts[1][:, WIDTH:]
        imag = parts[0][:, WIDTH:] + parts[1][:, :WIDTH]
        both = jnp.concatenate([real, imag], 1)
        out_ref[half] = both
        sent_ref[half] = both.astype(jnp.bfloat16)


def direct_kernel(mine_ref, other_ref, density_ref, out_ref, screened):
    for half in range(2):
        x = (mine_ref[half] + other_ref[1 - half].astype(jnp.float32)).astype(jnp.bfloat16)
        screened[half * SLICE : (half + 1) * SLICE, :] = x
        screened[(2 + half) * SLICE : (3 + half) * SLICE, :WIDTH] = x[:, WIDTH:]
        screened[(2 + half) * SLICE : (3 + half) * SLICE, WIDTH:] = -x[:, :WIDTH]
    parts = 4
    rows = density_ref.shape[0] // parts
    strips = rows // 64
    for m in range(parts):
        direct = jnp.dot(
            density_ref[m * rows : (m + 1) * rows, :], screened[...], preferred_element_type=jnp.float32
        )
        direct = direct.reshape(strips, -1, FINE, 2 * WIDTH)
        direct = jnp.concatenate([direct[s] for s in range(strips)], 1).astype(jnp.bfloat16)
        for place, chip in enumerate(RING):
            out_ref[place, m * strips * FINE : (m + 1) * strips * FINE, :] = direct[chip]


def total_kernel(in_ref, out_ref):
    for part in range(2):
        lanes = slice(part * WIDTH, (part + 1) * WIDTH)
        total = in_ref[0, :, lanes].astype(jnp.float32)
        for chip in range(1, in_ref.shape[0]):
            total += in_ref[chip, :, lanes].astype(jnp.float32)
        out_ref[part] = total


def whole(array):
    return pl.BlockSpec(array.shape, lambda *_: (0,) * len(array.shape))


def shards(valence_orbitals, conduction_orbitals, screened, valence_index, conduction_index, kpoint_index):
    bf16, f32 = jnp.bfloat16, jnp.float32
    rows = lax.axis_size("row")
    chips = rows // 2
    swap = [(i, i ^ 1) for i in range(rows)]
    same_core = [[2 * chip + core for chip in RING] for core in range(2)]
    anywhere = pl.BlockSpec(memory_space=pl.ANY)
    in_vmem = pl.BlockSpec(memory_space=pltpu.VMEM)
    index = [array.reshape(-1, 128) for array in (valence_index, conduction_index, kpoint_index)]
    strips = index[0].shape[0]
    valence = valence_orbitals.reshape(-1, SLICE)
    conduction = conduction_orbitals.reshape(-1, SLICE)
    raw = (valence, conduction, *index)
    bands = valence.shape[0] + conduction.shape[0]
    dma = pltpu.SemaphoreType.DMA
    tables, pairs, blocks, own_tables = pl.pallas_call(
        columns_kernel,
        out_shape=(
            jax.ShapeDtypeStruct((bands + 2 * strips + JOINED * SLICE, SLICE), bf16),
            jax.ShapeDtypeStruct((chips, SLICE, 2 * WIDTH), bf16),
            jax.ShapeDtypeStruct(((2 * chips - JOINED) * SLICE, SLICE), bf16),
            jax.ShapeDtypeStruct((ROOM, SLICE), bf16),
        ),
        in_specs=[anywhere] * 6,
        out_specs=(anywhere,) * 4,
        scratch_shapes=[
            pltpu.VMEM((bands, SLICE), bf16),
            pltpu.VMEM((3, strips, 128), jnp.int32),
            pltpu.VMEM((2 * strips, 128), bf16),
            pltpu.VMEM((SLICE, 2 * WIDTH), bf16),
            pltpu.VMEM((2 * chips * SLICE, SLICE), bf16),
            dma((5,)),
            dma((2, chips)),
            dma((6,)),
            dma((chips,)),
        ],
        compiler_params=ALL,
        name="columns",
    )(*raw, screened)
    pairs = lax.all_to_all(pairs, "row", 0, 0, axis_index_groups=same_core, tiled=True)
    partner_tables = lax.ppermute(tables, "row", swap)
    blocks = lax.ppermute(blocks, "row", swap)
    density = pl.pallas_call(
        rows_kernel,
        out_shape=jax.ShapeDtypeStruct((strips * 64, 4 * SLICE), bf16),
        grid=(strips // STRIPS,),
        in_specs=[anywhere, whole(partner_tables)],
        out_specs=pl.BlockSpec((STRIPS * 64, 4 * SLICE), lambda m: (m, 0)),
        scratch_shapes=[
            pltpu.VMEM((2 * KPAD, 4 * SLICE), bf16),
            pltpu.VMEM((2, strips, 128), f32),
            pltpu.VMEM((bands + 2 * strips, SLICE), bf16),
            dma,
        ],
        compiler_params=pltpu.CompilerParams(vmem_limit_bytes=48 * MIB),
        cost_estimate=pl.CostEstimate(flops=0, bytes_accessed=0, transcendentals=0),
        name="rows",
    )(own_tables, partner_tables)
    pairs, density = lax.optimization_barrier((pairs, density))
    mine, other = pl.pallas_call(
        screened_kernel,
        out_shape=tuple(jax.ShapeDtypeStruct((2, SLICE, 2 * WIDTH), kind) for kind in (f32, bf16)),
        in_specs=[in_vmem, anywhere, in_vmem, in_vmem],
        scratch_shapes=[pltpu.VMEM((2, SLICE, chips * SLICE), bf16), pltpu.SemaphoreType.DMA((chips,))],
        compiler_params=MUCH,
        name="screened",
    )(pairs, screened, partner_tables, blocks)
    other = lax.ppermute(other, "row", swap)
    partial = pl.pallas_call(
        direct_kernel,
        out_shape=jax.ShapeDtypeStruct((chips, strips * FINE, 2 * WIDTH), bf16),
        scratch_shapes=[pltpu.VMEM((4 * SLICE, 2 * WIDTH), bf16)],
        compiler_params=LITTLE,
        name="direct",
    )(mine, other, density)
    partial = lax.all_to_all(partial, "row", 0, 0, axis_index_groups=same_core, tiled=True)
    out = pl.pallas_call(
        total_kernel,
        out_shape=jax.ShapeDtypeStruct((2, strips * FINE, WIDTH), f32),
        compiler_params=LITTLE,
        name="total",
    )(partial)
    return out.reshape(2, strips, FINE, WIDTH)


def solution(mesh):
    in_specs = (
        P(None, None, None, "row"),
        P(None, None, None, "row"),
        P(None, "row", None),
        P(),
        P(),
        P(),
    )
    return jax.shard_map(
        shards, mesh=mesh, in_specs=in_specs, out_specs=P(None, None, "row", "col"), check_vma=False
    )
```

```python
import jax
import jax.numpy as jnp
from jax import lax
from jax.experimental import pallas as pl
from jax.experimental.pallas import tpu as pltpu
from jax.sharding import PartitionSpec as P

VAL = 48
CON = 64
FINE = 8
SLICE = 128
WIDTH = 128
KPAD = 256
RING = (0, 4, 1, 5, 2, 6, 3, 7)
JOINED = 5
MIB = 1024 * 1024
LITTLE = pltpu.CompilerParams(vmem_limit_bytes=16 * MIB)
MUCH = pltpu.CompilerParams(vmem_limit_bytes=52 * MIB)
ALL = pltpu.CompilerParams(vmem_limit_bytes=63 * MIB)


def core_of():
    return lax.rem(lax.axis_index("row"), 2)


def lane_matrix(row):
    return jnp.broadcast_to(row, (128, 128)).T


def one_hot(index, width):
    lane = lax.broadcasted_iota(jnp.int32, index.shape, 1).astype(jnp.float32)
    parts = [jnp.where(index == lane + float(at), 1.0, 0.0) for at in range(0, width, index.shape[1])]
    return jnp.concatenate(parts, 1).astype(jnp.bfloat16)


def densities(valence, conduction):
    width = valence.shape[1] // 2
    v_re, v_im = valence[:, :width], valence[:, width:]
    c_re, c_im = conduction[:, :width], conduction[:, width:]
    return v_re * c_re + v_im * c_im, v_re * c_im - v_im * c_re


def pick(parity, table):
    i = lax.broadcasted_iota(jnp.int32, (128, 256), 0)
    j = lax.broadcasted_iota(jnp.int32, (128, 256), 1)
    mask = jnp.where(j == 2 * i + parity, 1.0, 0.0).astype(jnp.bfloat16)
    parts = []
    for start in range(0, table.shape[0], 256):
        count = min(256, table.shape[0] - start)
        part = table[start : start + count]
        parts.append(jnp.dot(mask[: count // 2, :count], part, preferred_element_type=jnp.float32))
    missing = KPAD - table.shape[0] // 2
    if missing:
        parts.append(jnp.zeros((missing, table.shape[1]), jnp.float32))
    return jnp.concatenate(parts, 0).astype(jnp.bfloat16)


def columns_kernel(
    valence_ref, conduction_ref, v_ref, n_ref, k_ref, w_ref,
    table_ref, out_ref, block_ref,
    bands, index, sums, pairs, blocks, in_sems, w_sems, out_sems, pair_sems,
):
    core = core_of()
    split = valence_ref.shape[0]
    count, strips = bands.shape[0], index.shape[1]
    places = [bands.at[pl.ds(0, split), :], bands.at[pl.ds(split, count - split), :], *[index.at[i] for i in range(3)]]
    loads = []
    for i, (ref, place) in enumerate(zip((valence_ref, conduction_ref, v_ref, n_ref, k_ref), places)):
        loads.append(pltpu.make_async_copy(ref, place, in_sems.at[i]))
    for copy in loads:
        copy.start()
    gathers = []
    for part in range(2):
        for place, chip in enumerate(RING):
            lanes = pl.ds(pl.multiple_of((2 * chip + 1 - core) * SLICE, SLICE), SLICE)
            to = blocks.at[pl.ds((part * len(RING) + place) * SLICE, SLICE), :]
            gathers.append(pltpu.make_async_copy(w_ref.at[part, :, lanes], to, w_sems.at[part, place]))
    for copy in gathers:
        copy.start()
    for copy in loads:
        copy.wait()
    stores = [pltpu.make_async_copy(bands, table_ref.at[pl.ds(0, count), :], out_sems.at[0])]
    stores[0].start()
    for copy in gathers:
        copy.wait()
    joined = JOINED * SLICE
    rest = blocks.shape[0] - joined
    to = table_ref.at[pl.ds(count + 2 * strips, joined), :]
    stores.append(pltpu.make_async_copy(blocks.at[pl.ds(0, joined), :], to, out_sems.at[2]))
    stores[-1].start()
    stores.append(pltpu.make_async_copy(blocks.at[pl.ds(joined, rest), :], block_ref, out_sems.at[3]))
    stores[-1].start()
    own = pl.ds(lax.axis_index("col"), 1)
    picked = []
    for which, (width, start, stop) in enumerate(((VAL, 0, split), (CON, split, count))):
        sums[which * strips : (which + 1) * strips, :] = (
            (index[2] * width + index[which]).astype(jnp.float32).astype(jnp.bfloat16)
        )
        here = lane_matrix((index[2, own, :] * width + index[which, own, :]).astype(jnp.float32))
        parts = []
        for parity in range(2):
            hot = one_hot(2.0 * here + parity, stop - start)
            parts.append(jnp.dot(hot, bands[start:stop, :], preferred_element_type=jnp.float32))
        picked.append(jnp.concatenate(parts, 1))
    stores.append(pltpu.make_async_copy(sums, table_ref.at[pl.ds(count, 2 * strips), :], out_sems.at[1]))
    stores[-1].start()
    real, imag = densities(*picked)
    pairs[...] = jnp.concatenate([real.T, imag.T], 1).astype(jnp.bfloat16)
    for place in range(out_ref.shape[0]):
        stores.append(pltpu.make_async_copy(pairs, out_ref.at[place], pair_sems.at[place]))
        stores[-1].start()
    for copy in stores:
        copy.wait()


def rows_kernel(own_ref, partner_ref, density_ref, table, at_ref):
    core = core_of()

    strips = at_ref.shape[1]
    split = 2 * VAL * 4
    bands = 2 * (VAL + CON) * 4
    at_ref[0] = own_ref[bands : bands + strips, :].astype(jnp.float32)
    at_ref[1] = own_ref[bands + strips : bands + 2 * strips, :].astype(jnp.float32)
    both = jnp.concatenate([own_ref[0:bands, :], partner_ref[0:bands, :]], 1)
    for parity in range(2):
        lanes = pl.ds(parity * 2 * SLICE, 2 * SLICE)
        table[0:KPAD, lanes] = pick(parity, both[:split])
        table[KPAD:, lanes] = pick(parity, both[split:bands])
    lane = lax.broadcasted_iota(jnp.int32, (strips // 2, 128), 1)
    low = lane // FINE % 2 == 0
    picked = []
    for which in range(2):
        even = at_ref[which, pl.ds(0, strips // 2, stride=2), :]
        odd = at_ref[which, pl.ds(1, strips // 2, stride=2), :]
        first = jnp.where(low, even, pltpu.roll(odd, FINE, 1))
        second = jnp.where(low, pltpu.roll(even, 128 - FINE, 1), odd)
        pairs = jnp.where(core == 0, first, second)
        index = [lane_matrix(pairs[p : p + 1, :]) for p in range(strips // 2)]
        hot = one_hot(jnp.concatenate(index, 0), KPAD)
        picked.append(
            jnp.dot(hot, table[which * KPAD : (which + 1) * KPAD, :], preferred_element_type=jnp.float32)
        )
    density_ref[...] = jnp.concatenate(densities(*picked), 1).astype(jnp.bfloat16)


def screened_kernel(pairs_ref, own_ref, joined_ref, block_ref, out_ref, sent_ref, held, sems):
    core = core_of()
    copies = []
    for place, chip in enumerate(RING):
        lanes = pl.ds(pl.multiple_of((2 * chip + core) * SLICE, SLICE), SLICE)
        to = held.at[:, :, place * SLICE : (place + 1) * SLICE]
        copies.append(pltpu.make_async_copy(own_ref.at[:, :, lanes], to, sems.at[place]))
    for copy in copies:
        copy.start()
    pairs = pairs_ref[...].reshape(-1, 2 * WIDTH)
    chips = len(RING)
    start = joined_ref.shape[0] - JOINED * SLICE
    blocks = [joined_ref[start + i * SLICE : start + (i + 1) * SLICE, :] for i in range(JOINED)]
    blocks += [block_ref[i * SLICE : (i + 1) * SLICE, :] for i in range(2 * chips - JOINED)]
    for half in (1, 0):
        if half == 0:
            for copy in copies:
                copy.wait()
        parts = []
        for part in range(2):
            w = jnp.concatenate(blocks[part * chips : (part + 1) * chips], 1) if half else held[part]
            parts.append(jnp.dot(w, pairs, preferred_element_type=jnp.float32))
        real = parts[0][:, :WIDTH] - parts[1][:, WIDTH:]
        imag = parts[0][:, WIDTH:] + parts[1][:, :WIDTH]
        both = jnp.concatenate([real, imag], 1)
        out_ref[half] = both
        sent_ref[half] = both.astype(jnp.bfloat16)


def direct_kernel(mine_ref, other_ref, density_ref, out_ref, screened):
    for half in range(2):
        x = (mine_ref[half] + other_ref[1 - half].astype(jnp.float32)).astype(jnp.bfloat16)
        screened[half * SLICE : (half + 1) * SLICE, :] = x
        screened[(2 + half) * SLICE : (3 + half) * SLICE, :WIDTH] = x[:, WIDTH:]
        screened[(2 + half) * SLICE : (3 + half) * SLICE, WIDTH:] = -x[:, :WIDTH]
    parts = 4
    rows = density_ref.shape[0] // parts
    strips = rows // 64
    for m in range(parts):
        direct = jnp.dot(
            density_ref[m * rows : (m + 1) * rows, :], screened[...], preferred_element_type=jnp.float32
        )
        direct = direct.reshape(strips // 2, -1, 2 * FINE, 2 * WIDTH)
        direct = jnp.concatenate([direct[s] for s in range(strips // 2)], 1).astype(jnp.bfloat16)
        for place, chip in enumerate(RING):
            out_ref[place, m * strips * FINE : (m + 1) * strips * FINE, :] = direct[chip]


def total_kernel(in_ref, out_ref):
    for part in range(2):
        lanes = slice(part * WIDTH, (part + 1) * WIDTH)
        total = in_ref[0, :, lanes].astype(jnp.float32)
        for chip in range(1, in_ref.shape[0]):
            total += in_ref[chip, :, lanes].astype(jnp.float32)
        out_ref[part] = total


def whole(array):
    return pl.BlockSpec(array.shape, lambda *_: (0,) * len(array.shape))


def shards(valence_orbitals, conduction_orbitals, screened, valence_index, conduction_index, kpoint_index):
    bf16, f32 = jnp.bfloat16, jnp.float32
    rows = lax.axis_size("row")
    chips = rows // 2
    swap = [(i, i ^ 1) for i in range(rows)]
    same_core = [[2 * chip + core for chip in RING] for core in range(2)]
    anywhere = pl.BlockSpec(memory_space=pl.ANY)
    in_vmem = pl.BlockSpec(memory_space=pltpu.VMEM)
    index = [array.reshape(-1, 128) for array in (valence_index, conduction_index, kpoint_index)]
    strips = index[0].shape[0]
    valence = valence_orbitals.reshape(-1, SLICE)
    conduction = conduction_orbitals.reshape(-1, SLICE)
    raw = (valence, conduction, *index)
    bands = valence.shape[0] + conduction.shape[0]
    dma = pltpu.SemaphoreType.DMA
    tables, pairs, blocks = pl.pallas_call(
        columns_kernel,
        out_shape=(
            jax.ShapeDtypeStruct((bands + 2 * strips + JOINED * SLICE, SLICE), bf16),
            jax.ShapeDtypeStruct((chips, SLICE, 2 * WIDTH), bf16),
            jax.ShapeDtypeStruct(((2 * chips - JOINED) * SLICE, SLICE), bf16),
        ),
        in_specs=[anywhere] * 6,
        out_specs=(anywhere,) * 3,
        scratch_shapes=[
            pltpu.VMEM((bands, SLICE), bf16),
            pltpu.VMEM((3, strips, 128), jnp.int32),
            pltpu.VMEM((2 * strips, 128), bf16),
            pltpu.VMEM((SLICE, 2 * WIDTH), bf16),
            pltpu.VMEM((2 * chips * SLICE, SLICE), bf16),
            dma((5,)),
            dma((2, chips)),
            dma((4,)),
            dma((chips,)),
        ],
        compiler_params=ALL,
        name="columns",
    )(*raw, screened)
    pairs = lax.all_to_all(pairs, "row", 0, 0, axis_index_groups=same_core, tiled=True)
    partner_tables = lax.ppermute(tables, "row", swap)
    blocks = lax.ppermute(blocks, "row", swap)
    density = jax.ShapeDtypeStruct((strips * 64, 4 * SLICE), bf16)
    density = pl.pallas_call(
        rows_kernel,
        out_shape=density,
        grid=(1,),
        in_specs=[whole(tables), whole(partner_tables)],
        out_specs=whole(density),
        scratch_shapes=[pltpu.VMEM((2 * KPAD, 4 * SLICE), bf16), pltpu.VMEM((2, strips, 128), f32)],
        compiler_params=LITTLE,
        cost_estimate=pl.CostEstimate(flops=0, bytes_accessed=0, transcendentals=0),
        name="rows",
    )(tables, partner_tables)
    pairs, density = lax.optimization_barrier((pairs, density))
    mine, other = pl.pallas_call(
        screened_kernel,
        out_shape=tuple(jax.ShapeDtypeStruct((2, SLICE, 2 * WIDTH), kind) for kind in (f32, bf16)),
        in_specs=[in_vmem, anywhere, in_vmem, in_vmem],
        scratch_shapes=[pltpu.VMEM((2, SLICE, chips * SLICE), bf16), pltpu.SemaphoreType.DMA((chips,))],
        compiler_params=MUCH,
        name="screened",
    )(pairs, screened, partner_tables, blocks)
    other = lax.ppermute(other, "row", swap)
    partial = pl.pallas_call(
        direct_kernel,
        out_shape=jax.ShapeDtypeStruct((chips, strips * FINE, 2 * WIDTH), bf16),
        scratch_shapes=[pltpu.VMEM((4 * SLICE, 2 * WIDTH), bf16)],
        compiler_params=LITTLE,
        name="direct",
    )(mine, other, density)
    partial = lax.all_to_all(partial, "row", 0, 0, axis_index_groups=same_core, tiled=True)
    out = pl.pallas_call(
        total_kernel,
        out_shape=jax.ShapeDtypeStruct((2, strips * FINE, WIDTH), f32),
        compiler_params=LITTLE,
        name="total",
    )(partial)
    return out.reshape(2, strips, FINE, WIDTH)


def solution(mesh):
    in_specs = (
        P(None, None, None, "row"),
        P(None, None, None, "row"),
        P(None, "row", None),
        P(),
        P(),
        P(),
    )
    return jax.shard_map(
        shards, mesh=mesh, in_specs=in_specs, out_specs=P(None, None, "row", "col"), check_vma=False
    )
```

```python
import jax
import jax.numpy as jnp
from jax import lax
from jax.experimental import pallas as pl
from jax.experimental.pallas import tpu as pltpu
from jax.sharding import PartitionSpec as P

VAL = 48
CON = 64
FINE = 8
SLICE = 128
WIDTH = 128
KPAD = 256
RING = (0, 4, 1, 5, 2, 6, 3, 7)
STRIPS = 32
JOINED = 5
MIB = 1024 * 1024
LITTLE = pltpu.CompilerParams(vmem_limit_bytes=16 * MIB)
MUCH = pltpu.CompilerParams(vmem_limit_bytes=52 * MIB)
ALL = pltpu.CompilerParams(vmem_limit_bytes=63 * MIB)


def core_of():
    return lax.rem(lax.axis_index("row"), 2)


def lane_matrix(row):
    return jnp.broadcast_to(row, (128, 128)).T


def one_hot(index, width):
    lane = lax.broadcasted_iota(jnp.int32, index.shape, 1).astype(jnp.float32)
    parts = [jnp.where(index == lane + float(at), 1.0, 0.0) for at in range(0, width, index.shape[1])]
    return jnp.concatenate(parts, 1).astype(jnp.bfloat16)


def densities(valence, conduction):
    width = valence.shape[1] // 2
    v_re, v_im = valence[:, :width], valence[:, width:]
    c_re, c_im = conduction[:, :width], conduction[:, width:]
    return v_re * c_re + v_im * c_im, v_re * c_im - v_im * c_re


def pick(parity, table):
    i = lax.broadcasted_iota(jnp.int32, (128, 256), 0)
    j = lax.broadcasted_iota(jnp.int32, (128, 256), 1)
    mask = jnp.where(j == 2 * i + parity, 1.0, 0.0).astype(jnp.bfloat16)
    parts = []
    for start in range(0, table.shape[0], 256):
        count = min(256, table.shape[0] - start)
        part = table[start : start + count]
        parts.append(jnp.dot(mask[: count // 2, :count], part, preferred_element_type=jnp.float32))
    missing = KPAD - table.shape[0] // 2
    if missing:
        parts.append(jnp.zeros((missing, table.shape[1]), jnp.float32))
    return jnp.concatenate(parts, 0).astype(jnp.bfloat16)


def columns_kernel(
    valence_ref, conduction_ref, v_ref, n_ref, k_ref, w_ref,
    table_ref, out_ref, block_ref,
    bands, index, sums, pairs, blocks, in_sems, w_sems, out_sems, pair_sems,
):
    core = core_of()
    split = valence_ref.shape[0]
    count, strips = bands.shape[0], index.shape[1]
    places = [bands.at[pl.ds(0, split), :], bands.at[pl.ds(split, count - split), :], *[index.at[i] for i in range(3)]]
    loads = []
    for i, (ref, place) in enumerate(zip((valence_ref, conduction_ref, v_ref, n_ref, k_ref), places)):
        loads.append(pltpu.make_async_copy(ref, place, in_sems.at[i]))
    for copy in loads[2:] + loads[:2]:
        copy.start()
    gathers = []
    for part in range(2):
        for place, chip in enumerate(RING):
            lanes = pl.ds(pl.multiple_of((2 * chip + 1 - core) * SLICE, SLICE), SLICE)
            to = blocks.at[pl.ds((part * len(RING) + place) * SLICE, SLICE), :]
            gathers.append(pltpu.make_async_copy(w_ref.at[part, :, lanes], to, w_sems.at[part, place]))
    for copy in gathers:
        copy.start()
    for copy in loads[2:]:
        copy.wait()
    own = pl.ds(lax.axis_index("col"), 1)
    hots = []
    for which, (width, size) in enumerate(((VAL, split), (CON, count - split))):
        sums[which * strips : (which + 1) * strips, :] = (
            (index[2] * width + index[which]).astype(jnp.float32).astype(jnp.bfloat16)
        )
        here = lane_matrix((index[2, own, :] * width + index[which, own, :]).astype(jnp.float32))
        hots.append([one_hot(2.0 * here + parity, size) for parity in range(2)])
    for copy in loads[:2]:
        copy.wait()
    stores = [pltpu.make_async_copy(bands, table_ref.at[pl.ds(0, count), :], out_sems.at[0])]
    stores[0].start()
    for copy in gathers:
        copy.wait()
    joined = JOINED * SLICE
    rest = blocks.shape[0] - joined
    to = table_ref.at[pl.ds(count + 2 * strips, joined), :]
    stores.append(pltpu.make_async_copy(blocks.at[pl.ds(0, joined), :], to, out_sems.at[2]))
    stores[-1].start()
    stores.append(pltpu.make_async_copy(blocks.at[pl.ds(joined, rest), :], block_ref, out_sems.at[3]))
    stores[-1].start()
    picked = []
    for pair, (start, stop) in zip(hots, ((0, split), (split, count))):
        parts = [jnp.dot(hot, bands[start:stop, :], preferred_element_type=jnp.float32) for hot in pair]
        picked.append(jnp.concatenate(parts, 1))
    stores.append(pltpu.make_async_copy(sums, table_ref.at[pl.ds(count, 2 * strips), :], out_sems.at[1]))
    stores[-1].start()
    real, imag = densities(*picked)
    pairs[...] = jnp.concatenate([real.T, imag.T], 1).astype(jnp.bfloat16)
    for place in range(out_ref.shape[0]):
        stores.append(pltpu.make_async_copy(pairs, out_ref.at[place], pair_sems.at[place]))
        stores[-1].start()
    for copy in stores:
        copy.wait()


def rows_kernel(own_ref, partner_ref, density_ref, table, at_ref):
    core = core_of()

    @pl.when(pl.program_id(0) == 0)
    def _():
        strips = at_ref.shape[1]
        split = 2 * VAL * 4
        bands = 2 * (VAL + CON) * 4
        at_ref[0] = own_ref[bands : bands + strips, :].astype(jnp.float32)
        at_ref[1] = own_ref[bands + strips : bands + 2 * strips, :].astype(jnp.float32)
        both = jnp.concatenate([own_ref[0:bands, :], partner_ref[0:bands, :]], 1)
        for parity in range(2):
            lanes = pl.ds(parity * 2 * SLICE, 2 * SLICE)
            table[0:KPAD, lanes] = pick(parity, both[:split])
            table[KPAD:, lanes] = pick(parity, both[split:bands])

    picked = []
    for which in range(2):
        index = []
        for s in range(STRIPS):
            strip = lane_matrix(at_ref[which, pl.ds(pl.program_id(0) * STRIPS + s, 1), :]).reshape(-1, 2, FINE, 128)
            index.append(jnp.where(core == 0, strip[:, 0], strip[:, 1]).reshape(-1, 128))
        hot = one_hot(jnp.concatenate(index, 0), KPAD)
        picked.append(
            jnp.dot(hot, table[which * KPAD : (which + 1) * KPAD, :], preferred_element_type=jnp.float32)
        )
    density_ref[...] = jnp.concatenate(densities(*picked), 1).astype(jnp.bfloat16)


def screened_kernel(pairs_ref, own_ref, joined_ref, block_ref, out_ref, sent_ref, held, sems):
    core = core_of()
    copies = []
    for place, chip in enumerate(RING):
        lanes = pl.ds(pl.multiple_of((2 * chip + core) * SLICE, SLICE), SLICE)
        to = held.at[:, :, place * SLICE : (place + 1) * SLICE]
        copies.append(pltpu.make_async_copy(own_ref.at[:, :, lanes], to, sems.at[place]))
    for copy in copies:
        copy.start()
    pairs = pairs_ref[...].reshape(-1, 2 * WIDTH)
    chips = len(RING)
    start = joined_ref.shape[0] - JOINED * SLICE
    blocks = [joined_ref[start + i * SLICE : start + (i + 1) * SLICE, :] for i in range(JOINED)]
    blocks += [block_ref[i * SLICE : (i + 1) * SLICE, :] for i in range(2 * chips - JOINED)]
    for half in (1, 0):
        if half == 0:
            for copy in copies:
                copy.wait()
        parts = []
        for part in range(2):
            w = jnp.concatenate(blocks[part * chips : (part + 1) * chips], 1) if half else held[part]
            parts.append(jnp.dot(w, pairs, preferred_element_type=jnp.float32))
        real = parts[0][:, :WIDTH] - parts[1][:, WIDTH:]
        imag = parts[0][:, WIDTH:] + parts[1][:, :WIDTH]
        both = jnp.concatenate([real, imag], 1)
        out_ref[half] = both
        sent_ref[half] = both.astype(jnp.bfloat16)


def direct_kernel(mine_ref, other_ref, density_ref, out_ref, screened):
    for half in range(2):
        x = (mine_ref[half] + other_ref[1 - half].astype(jnp.float32)).astype(jnp.bfloat16)
        screened[half * SLICE : (half + 1) * SLICE, :] = x
        screened[(2 + half) * SLICE : (3 + half) * SLICE, :WIDTH] = x[:, WIDTH:]
        screened[(2 + half) * SLICE : (3 + half) * SLICE, WIDTH:] = -x[:, :WIDTH]
    parts = 4
    rows = density_ref.shape[0] // parts
    strips = rows // 64
    for m in range(parts):
        direct = jnp.dot(
            density_ref[m * rows : (m + 1) * rows, :], screened[...], preferred_element_type=jnp.float32
        )
        direct = direct.reshape(strips, -1, FINE, 2 * WIDTH)
        direct = jnp.concatenate([direct[s] for s in range(strips)], 1).astype(jnp.bfloat16)
        for place, chip in enumerate(RING):
            out_ref[place, m * strips * FINE : (m + 1) * strips * FINE, :] = direct[chip]


def total_kernel(in_ref, out_ref):
    for part in range(2):
        lanes = slice(part * WIDTH, (part + 1) * WIDTH)
        total = in_ref[0, :, lanes].astype(jnp.float32)
        for chip in range(1, in_ref.shape[0]):
            total += in_ref[chip, :, lanes].astype(jnp.float32)
        out_ref[part] = total


def whole(array):
    return pl.BlockSpec(array.shape, lambda *_: (0,) * len(array.shape))


def shards(valence_orbitals, conduction_orbitals, screened, valence_index, conduction_index, kpoint_index):
    bf16, f32 = jnp.bfloat16, jnp.float32
    rows = lax.axis_size("row")
    chips = rows // 2
    swap = [(i, i ^ 1) for i in range(rows)]
    same_core = [[2 * chip + core for chip in RING] for core in range(2)]
    anywhere = pl.BlockSpec(memory_space=pl.ANY)
    in_vmem = pl.BlockSpec(memory_space=pltpu.VMEM)
    index = [array.reshape(-1, 128) for array in (valence_index, conduction_index, kpoint_index)]
    strips = index[0].shape[0]
    valence = valence_orbitals.reshape(-1, SLICE)
    conduction = conduction_orbitals.reshape(-1, SLICE)
    raw = (valence, conduction, *index)
    bands = valence.shape[0] + conduction.shape[0]
    dma = pltpu.SemaphoreType.DMA
    tables, pairs, blocks = pl.pallas_call(
        columns_kernel,
        out_shape=(
            jax.ShapeDtypeStruct((bands + 2 * strips + JOINED * SLICE, SLICE), bf16),
            jax.ShapeDtypeStruct((chips, SLICE, 2 * WIDTH), bf16),
            jax.ShapeDtypeStruct(((2 * chips - JOINED) * SLICE, SLICE), bf16),
        ),
        in_specs=[anywhere] * 6,
        out_specs=(anywhere,) * 3,
        scratch_shapes=[
            pltpu.VMEM((bands, SLICE), bf16),
            pltpu.VMEM((3, strips, 128), jnp.int32),
            pltpu.VMEM((2 * strips, 128), bf16),
            pltpu.VMEM((SLICE, 2 * WIDTH), bf16),
            pltpu.VMEM((2 * chips * SLICE, SLICE), bf16),
            dma((5,)),
            dma((2, chips)),
            dma((4,)),
            dma((chips,)),
        ],
        compiler_params=ALL,
        name="columns",
    )(*raw, screened)
    pairs = lax.all_to_all(pairs, "row", 0, 0, axis_index_groups=same_core, tiled=True)
    partner_tables = lax.ppermute(tables, "row", swap)
    blocks = lax.ppermute(blocks, "row", swap)
    density = pl.pallas_call(
        rows_kernel,
        out_shape=jax.ShapeDtypeStruct((strips * 64, 4 * SLICE), bf16),
        grid=(strips // STRIPS,),
        in_specs=[whole(tables), whole(partner_tables)],
        out_specs=pl.BlockSpec((STRIPS * 64, 4 * SLICE), lambda m: (m, 0)),
        scratch_shapes=[pltpu.VMEM((2 * KPAD, 4 * SLICE), bf16), pltpu.VMEM((2, strips, 128), f32)],
        compiler_params=LITTLE,
        cost_estimate=pl.CostEstimate(flops=0, bytes_accessed=0, transcendentals=0),
        name="rows",
    )(tables, partner_tables)
    pairs, density = lax.optimization_barrier((pairs, density))
    mine, other = pl.pallas_call(
        screened_kernel,
        out_shape=tuple(jax.ShapeDtypeStruct((2, SLICE, 2 * WIDTH), kind) for kind in (f32, bf16)),
        in_specs=[in_vmem, anywhere, in_vmem, in_vmem],
        scratch_shapes=[pltpu.VMEM((2, SLICE, chips * SLICE), bf16), pltpu.SemaphoreType.DMA((chips,))],
        compiler_params=MUCH,
        name="screened",
    )(pairs, screened, partner_tables, blocks)
    other = lax.ppermute(other, "row", swap)
    partial = pl.pallas_call(
        direct_kernel,
        out_shape=jax.ShapeDtypeStruct((chips, strips * FINE, 2 * WIDTH), bf16),
        scratch_shapes=[pltpu.VMEM((4 * SLICE, 2 * WIDTH), bf16)],
        compiler_params=LITTLE,
        name="direct",
    )(mine, other, density)
    partial = lax.all_to_all(partial, "row", 0, 0, axis_index_groups=same_core, tiled=True)
    out = pl.pallas_call(
        total_kernel,
        out_shape=jax.ShapeDtypeStruct((2, strips * FINE, WIDTH), f32),
        compiler_params=LITTLE,
        name="total",
    )(partial)
    return out.reshape(2, strips, FINE, WIDTH)


def solution(mesh):
    in_specs = (
        P(None, None, None, "row"),
        P(None, None, None, "row"),
        P(None, "row", None),
        P(),
        P(),
        P(),
    )
    return jax.shard_map(
        shards, mesh=mesh, in_specs=in_specs, out_specs=P(None, None, "row", "col"), check_vma=False
    )
```

```python
import jax
import jax.numpy as jnp
from jax import lax
from jax.experimental import pallas as pl
from jax.experimental.pallas import tpu as pltpu
from jax.sharding import PartitionSpec as P

VAL = 48
CON = 64
FINE = 8
SLICE = 128
WIDTH = 128
KPAD = 256
RING = (0, 4, 1, 5, 2, 6, 3, 7)
STRIPS = 32
JOINED = 5
MIB = 1024 * 1024
LITTLE = pltpu.CompilerParams(vmem_limit_bytes=16 * MIB)
MUCH = pltpu.CompilerParams(vmem_limit_bytes=52 * MIB)
ALL = pltpu.CompilerParams(vmem_limit_bytes=63 * MIB)


def core_of():
    return lax.rem(lax.axis_index("row"), 2)


def lane_matrix(row):
    return jnp.broadcast_to(row, (128, 128)).T


def one_hot(index, width):
    lane = lax.broadcasted_iota(jnp.int32, index.shape, 1).astype(jnp.float32)
    parts = [jnp.where(index == lane + float(at), 1.0, 0.0) for at in range(0, width, index.shape[1])]
    return jnp.concatenate(parts, 1).astype(jnp.bfloat16)


def densities(valence, conduction):
    width = valence.shape[1] // 2
    v_re, v_im = valence[:, :width], valence[:, width:]
    c_re, c_im = conduction[:, :width], conduction[:, width:]
    return v_re * c_re + v_im * c_im, v_re * c_im - v_im * c_re


def pick(parity, table):
    i = lax.broadcasted_iota(jnp.int32, (128, 256), 0)
    j = lax.broadcasted_iota(jnp.int32, (128, 256), 1)
    mask = jnp.where(j == 2 * i + parity, 1.0, 0.0).astype(jnp.bfloat16)
    parts = []
    for start in range(0, table.shape[0], 256):
        count = min(256, table.shape[0] - start)
        part = table[start : start + count]
        parts.append(jnp.dot(mask[: count // 2, :count], part, preferred_element_type=jnp.float32))
    missing = KPAD - table.shape[0] // 2
    if missing:
        parts.append(jnp.zeros((missing, table.shape[1]), jnp.float32))
    return jnp.concatenate(parts, 0).astype(jnp.bfloat16)


def columns_kernel(
    valence_ref, conduction_ref, v_ref, n_ref, k_ref, w_ref,
    table_ref, out_ref, block_ref,
    bands, index, sums, pairs, blocks, in_sems, w_sems, out_sems, pair_sems,
):
    core = core_of()
    split = valence_ref.shape[0]
    count, strips = bands.shape[0], index.shape[1]
    places = [bands.at[pl.ds(0, split), :], bands.at[pl.ds(split, count - split), :], *[index.at[i] for i in range(3)]]
    loads = []
    for i, (ref, place) in enumerate(zip((valence_ref, conduction_ref, v_ref, n_ref, k_ref), places)):
        loads.append(pltpu.make_async_copy(ref, place, in_sems.at[i]))
    for copy in loads[2:] + loads[:2]:
        copy.start()
    gathers = []
    for part in range(2):
        for place, chip in enumerate(RING):
            lanes = pl.ds(pl.multiple_of((2 * chip + 1 - core) * SLICE, SLICE), SLICE)
            to = blocks.at[pl.ds((part * len(RING) + place) * SLICE, SLICE), :]
            gathers.append(pltpu.make_async_copy(w_ref.at[part, :, lanes], to, w_sems.at[part, place]))
    for copy in gathers:
        copy.start()
    for copy in loads[2:]:
        copy.wait()
    own = pl.ds(lax.axis_index("col"), 1)
    hots = []
    for which, (width, size) in enumerate(((VAL, split), (CON, count - split))):
        sums[which * strips : (which + 1) * strips, :] = (
            (index[2] * width + index[which]).astype(jnp.float32).astype(jnp.bfloat16)
        )
        here = lane_matrix((index[2, own, :] * width + index[which, own, :]).astype(jnp.float32))
        hots.append([one_hot(2.0 * here + parity, size) for parity in range(2)])
    for copy in loads[:2]:
        copy.wait()
    stores = [pltpu.make_async_copy(bands, table_ref.at[pl.ds(0, count), :], out_sems.at[0])]
    stores[0].start()
    for copy in gathers:
        copy.wait()
    joined = JOINED * SLICE
    rest = blocks.shape[0] - joined
    to = table_ref.at[pl.ds(count + 2 * strips, joined), :]
    stores.append(pltpu.make_async_copy(blocks.at[pl.ds(0, joined), :], to, out_sems.at[2]))
    stores[-1].start()
    stores.append(pltpu.make_async_copy(blocks.at[pl.ds(joined, rest), :], block_ref, out_sems.at[3]))
    stores[-1].start()
    picked = []
    for pair, (start, stop) in zip(hots, ((0, split), (split, count))):
        parts = [jnp.dot(hot, bands[start:stop, :], preferred_element_type=jnp.float32) for hot in pair]
        picked.append(jnp.concatenate(parts, 1))
    stores.append(pltpu.make_async_copy(sums, table_ref.at[pl.ds(count, 2 * strips), :], out_sems.at[1]))
    stores[-1].start()
    real, imag = densities(*picked)
    pairs[...] = jnp.concatenate([real.T, imag.T], 1).astype(jnp.bfloat16)
    for place in range(out_ref.shape[0]):
        stores.append(pltpu.make_async_copy(pairs, out_ref.at[place], pair_sems.at[place]))
        stores[-1].start()
    for copy in stores:
        copy.wait()


def rows_kernel(own_ref, partner_ref, density_ref, table, at_ref):
    core = core_of()

    @pl.when(pl.program_id(0) == 0)
    def _():
        strips = at_ref.shape[1]
        split = 2 * VAL * 4
        bands = 2 * (VAL + CON) * 4
        at_ref[0] = own_ref[bands : bands + strips, :].astype(jnp.float32)
        at_ref[1] = own_ref[bands + strips : bands + 2 * strips, :].astype(jnp.float32)
        both = jnp.concatenate([own_ref[0:bands, :], partner_ref[0:bands, :]], 1)
        for parity in range(2):
            lanes = pl.ds(parity * 2 * SLICE, 2 * SLICE)
            table[0:KPAD, lanes] = pick(parity, both[:split])
            table[KPAD:, lanes] = pick(parity, both[split:bands])

    picked = []
    for which in range(2):
        index = []
        for s in range(STRIPS):
            strip = lane_matrix(at_ref[which, pl.ds(pl.program_id(0) * STRIPS + s, 1), :]).reshape(-1, 2, FINE, 128)
            index.append(jnp.where(core == 0, strip[:, 0], strip[:, 1]).reshape(-1, 128))
        hot = one_hot(jnp.concatenate(index, 0), KPAD)
        picked.append(
            jnp.dot(hot, table[which * KPAD : (which + 1) * KPAD, :], preferred_element_type=jnp.float32)
        )
    density_ref[...] = jnp.concatenate(densities(*picked), 1).astype(jnp.bfloat16)


def screened_kernel(pairs_ref, own_ref, joined_ref, block_ref, out_ref, sent_ref, held, sems):
    core = core_of()
    copies = []
    for place, chip in enumerate(RING):
        lanes = pl.ds(pl.multiple_of((2 * chip + core) * SLICE, SLICE), SLICE)
        to = held.at[:, :, place * SLICE : (place + 1) * SLICE]
        copies.append(pltpu.make_async_copy(own_ref.at[:, :, lanes], to, sems.at[place]))
    for copy in copies:
        copy.start()
    pairs = pairs_ref[...].reshape(-1, 2 * WIDTH)
    chips = len(RING)
    start = joined_ref.shape[0] - JOINED * SLICE
    blocks = [joined_ref[start + i * SLICE : start + (i + 1) * SLICE, :] for i in range(JOINED)]
    blocks += [block_ref[i * SLICE : (i + 1) * SLICE, :] for i in range(2 * chips - JOINED)]
    for half in (1, 0):
        if half == 0:
            for copy in copies:
                copy.wait()
        if half:
            w = jnp.concatenate([jnp.concatenate(blocks[part * chips : (part + 1) * chips], 1) for part in range(2)], 0)
        else:
            w = held[...].reshape(2 * SLICE, -1)
        product = jnp.dot(w, pairs, preferred_element_type=jnp.float32)
        parts = product[:SLICE], product[SLICE:]
        real = parts[0][:, :WIDTH] - parts[1][:, WIDTH:]
        imag = parts[0][:, WIDTH:] + parts[1][:, :WIDTH]
        both = jnp.concatenate([real, imag], 1)
        out_ref[half] = both
        sent_ref[half] = both.astype(jnp.bfloat16)


def direct_kernel(mine_ref, other_ref, density_ref, out_ref, screened):
    for half in range(2):
        x = (mine_ref[half] + other_ref[1 - half].astype(jnp.float32)).astype(jnp.bfloat16)
        screened[half * SLICE : (half + 1) * SLICE, :] = x
        screened[(2 + half) * SLICE : (3 + half) * SLICE, :WIDTH] = x[:, WIDTH:]
        screened[(2 + half) * SLICE : (3 + half) * SLICE, WIDTH:] = -x[:, :WIDTH]
    parts = 4
    rows = density_ref.shape[0] // parts
    strips = rows // 64
    for m in range(parts):
        direct = jnp.dot(
            density_ref[m * rows : (m + 1) * rows, :], screened[...], preferred_element_type=jnp.float32
        )
        direct = direct.reshape(strips, -1, FINE, 2 * WIDTH)
        direct = jnp.concatenate([direct[s] for s in range(strips)], 1).astype(jnp.bfloat16)
        for place, chip in enumerate(RING):
            out_ref[place, m * strips * FINE : (m + 1) * strips * FINE, :] = direct[chip]


def total_kernel(in_ref, out_ref):
    for part in range(2):
        lanes = slice(part * WIDTH, (part + 1) * WIDTH)
        total = in_ref[0, :, lanes].astype(jnp.float32)
        for chip in range(1, in_ref.shape[0]):
            total += in_ref[chip, :, lanes].astype(jnp.float32)
        out_ref[part] = total


def whole(array):
    return pl.BlockSpec(array.shape, lambda *_: (0,) * len(array.shape))


def shards(valence_orbitals, conduction_orbitals, screened, valence_index, conduction_index, kpoint_index):
    bf16, f32 = jnp.bfloat16, jnp.float32
    rows = lax.axis_size("row")
    chips = rows // 2
    swap = [(i, i ^ 1) for i in range(rows)]
    same_core = [[2 * chip + core for chip in RING] for core in range(2)]
    anywhere = pl.BlockSpec(memory_space=pl.ANY)
    in_vmem = pl.BlockSpec(memory_space=pltpu.VMEM)
    index = [array.reshape(-1, 128) for array in (valence_index, conduction_index, kpoint_index)]
    strips = index[0].shape[0]
    valence = valence_orbitals.reshape(-1, SLICE)
    conduction = conduction_orbitals.reshape(-1, SLICE)
    raw = (valence, conduction, *index)
    bands = valence.shape[0] + conduction.shape[0]
    dma = pltpu.SemaphoreType.DMA
    tables, pairs, blocks = pl.pallas_call(
        columns_kernel,
        out_shape=(
            jax.ShapeDtypeStruct((bands + 2 * strips + JOINED * SLICE, SLICE), bf16),
            jax.ShapeDtypeStruct((chips, SLICE, 2 * WIDTH), bf16),
            jax.ShapeDtypeStruct(((2 * chips - JOINED) * SLICE, SLICE), bf16),
        ),
        in_specs=[anywhere] * 6,
        out_specs=(anywhere,) * 3,
        scratch_shapes=[
            pltpu.VMEM((bands, SLICE), bf16),
            pltpu.VMEM((3, strips, 128), jnp.int32),
            pltpu.VMEM((2 * strips, 128), bf16),
            pltpu.VMEM((SLICE, 2 * WIDTH), bf16),
            pltpu.VMEM((2 * chips * SLICE, SLICE), bf16),
            dma((5,)),
            dma((2, chips)),
            dma((4,)),
            dma((chips,)),
        ],
        compiler_params=ALL,
        name="columns",
    )(*raw, screened)
    pairs = lax.all_to_all(pairs, "row", 0, 0, axis_index_groups=same_core, tiled=True)
    partner_tables = lax.ppermute(tables, "row", swap)
    blocks = lax.ppermute(blocks, "row", swap)
    density = pl.pallas_call(
        rows_kernel,
        out_shape=jax.ShapeDtypeStruct((strips * 64, 4 * SLICE), bf16),
        grid=(strips // STRIPS,),
        in_specs=[whole(tables), whole(partner_tables)],
        out_specs=pl.BlockSpec((STRIPS * 64, 4 * SLICE), lambda m: (m, 0)),
        scratch_shapes=[pltpu.VMEM((2 * KPAD, 4 * SLICE), bf16), pltpu.VMEM((2, strips, 128), f32)],
        compiler_params=LITTLE,
        cost_estimate=pl.CostEstimate(flops=0, bytes_accessed=0, transcendentals=0),
        name="rows",
    )(tables, partner_tables)
    pairs, density = lax.optimization_barrier((pairs, density))
    mine, other = pl.pallas_call(
        screened_kernel,
        out_shape=tuple(jax.ShapeDtypeStruct((2, SLICE, 2 * WIDTH), kind) for kind in (f32, bf16)),
        in_specs=[in_vmem, anywhere, in_vmem, in_vmem],
        scratch_shapes=[pltpu.VMEM((2, SLICE, chips * SLICE), bf16), pltpu.SemaphoreType.DMA((chips,))],
        compiler_params=MUCH,
        name="screened",
    )(pairs, screened, partner_tables, blocks)
    other = lax.ppermute(other, "row", swap)
    partial = pl.pallas_call(
        direct_kernel,
        out_shape=jax.ShapeDtypeStruct((chips, strips * FINE, 2 * WIDTH), bf16),
        scratch_shapes=[pltpu.VMEM((4 * SLICE, 2 * WIDTH), bf16)],
        compiler_params=LITTLE,
        name="direct",
    )(mine, other, density)
    partial = lax.all_to_all(partial, "row", 0, 0, axis_index_groups=same_core, tiled=True)
    out = pl.pallas_call(
        total_kernel,
        out_shape=jax.ShapeDtypeStruct((2, strips * FINE, WIDTH), f32),
        compiler_params=LITTLE,
        name="total",
    )(partial)
    return out.reshape(2, strips, FINE, WIDTH)


def solution(mesh):
    in_specs = (
        P(None, None, None, "row"),
        P(None, None, None, "row"),
        P(None, "row", None),
        P(),
        P(),
        P(),
    )
    return jax.shard_map(
        shards, mesh=mesh, in_specs=in_specs, out_specs=P(None, None, "row", "col"), check_vma=False
    )
```

```python
import jax
import jax.numpy as jnp
from jax import lax
from jax.experimental import pallas as pl
from jax.experimental.pallas import tpu as pltpu
from jax.sharding import PartitionSpec as P

VAL = 48
CON = 64
FINE = 8
SLICE = 128
WIDTH = 128
KPAD = 256
RING = (0, 4, 1, 5, 2, 6, 3, 7)
STRIPS = 32
JOINED = 5
MIB = 1024 * 1024
LITTLE = pltpu.CompilerParams(vmem_limit_bytes=16 * MIB)
MUCH = pltpu.CompilerParams(vmem_limit_bytes=52 * MIB)
ALL = pltpu.CompilerParams(vmem_limit_bytes=63 * MIB)


def core_of():
    return lax.rem(lax.axis_index("row"), 2)


def lane_matrix(row):
    return jnp.broadcast_to(row, (128, 128)).T


def one_hot(index, width):
    lane = lax.broadcasted_iota(jnp.int32, index.shape, 1).astype(jnp.float32)
    parts = [jnp.where(index == lane + float(at), 1.0, 0.0) for at in range(0, width, index.shape[1])]
    return jnp.concatenate(parts, 1).astype(jnp.bfloat16)


def densities(valence, conduction):
    width = valence.shape[1] // 2
    v_re, v_im = valence[:, :width], valence[:, width:]
    c_re, c_im = conduction[:, :width], conduction[:, width:]
    return v_re * c_re + v_im * c_im, v_re * c_im - v_im * c_re


def pick(parity, table):
    i = lax.broadcasted_iota(jnp.int32, (128, 256), 0)
    j = lax.broadcasted_iota(jnp.int32, (128, 256), 1)
    mask = jnp.where(j == 2 * i + parity, 1.0, 0.0).astype(jnp.bfloat16)
    parts = []
    for start in range(0, table.shape[0], 256):
        count = min(256, table.shape[0] - start)
        part = table[start : start + count]
        parts.append(jnp.dot(mask[: count // 2, :count], part, preferred_element_type=jnp.float32))
    missing = KPAD - table.shape[0] // 2
    if missing:
        parts.append(jnp.zeros((missing, table.shape[1]), jnp.float32))
    return jnp.concatenate(parts, 0).astype(jnp.bfloat16)


def columns_kernel(
    valence_ref, conduction_ref, v_ref, n_ref, k_ref, w_ref,
    table_ref, out_ref, block_ref,
    bands, index, sums, pairs, blocks, in_sems, w_sems, out_sems, pair_sems,
):
    core = core_of()
    split = valence_ref.shape[0]
    count, strips = bands.shape[0], index.shape[1]
    places = [bands.at[pl.ds(0, split), :], bands.at[pl.ds(split, count - split), :], *[index.at[i] for i in range(3)]]
    loads = []
    for i, (ref, place) in enumerate(zip((valence_ref, conduction_ref, v_ref, n_ref, k_ref), places)):
        loads.append(pltpu.make_async_copy(ref, place, in_sems.at[i]))
    for copy in loads[2:] + loads[:2]:
        copy.start()
    gathers = []
    for part in range(2):
        for place, chip in enumerate(RING):
            lanes = pl.ds(pl.multiple_of((2 * chip + 1 - core) * SLICE, SLICE), SLICE)
            to = blocks.at[pl.ds((part * len(RING) + place) * SLICE, SLICE), :]
            gathers.append(pltpu.make_async_copy(w_ref.at[part, :, lanes], to, w_sems.at[part, place]))
    for copy in gathers:
        copy.start()
    for copy in loads[2:]:
        copy.wait()
    own = pl.ds(lax.axis_index("col"), 1)
    hots = []
    for which, (width, size) in enumerate(((VAL, split), (CON, count - split))):
        sums[which * strips : (which + 1) * strips, :] = (
            (index[2] * width + index[which]).astype(jnp.float32).astype(jnp.bfloat16)
        )
        here = lane_matrix((index[2, own, :] * width + index[which, own, :]).astype(jnp.float32))
        hots.append([one_hot(2.0 * here + parity, size) for parity in range(2)])
    for copy in loads[:2]:
        copy.wait()
    stores = [pltpu.make_async_copy(bands, table_ref.at[pl.ds(0, count), :], out_sems.at[0])]
    stores[0].start()
    for copy in gathers:
        copy.wait()
    joined = JOINED * SLICE
    rest = blocks.shape[0] - joined
    to = table_ref.at[pl.ds(count + 2 * strips, joined), :]
    stores.append(pltpu.make_async_copy(blocks.at[pl.ds(0, joined), :], to, out_sems.at[2]))
    stores[-1].start()
    stores.append(pltpu.make_async_copy(blocks.at[pl.ds(joined, rest), :], block_ref, out_sems.at[3]))
    stores[-1].start()
    picked = []
    for pair, (start, stop) in zip(hots, ((0, split), (split, count))):
        parts = [jnp.dot(hot, bands[start:stop, :], preferred_element_type=jnp.float32) for hot in pair]
        picked.append(jnp.concatenate(parts, 1))
    stores.append(pltpu.make_async_copy(sums, table_ref.at[pl.ds(count, 2 * strips), :], out_sems.at[1]))
    stores[-1].start()
    real, imag = densities(*picked)
    pairs[...] = jnp.concatenate([real.T, imag.T], 1).astype(jnp.bfloat16)
    for place in range(out_ref.shape[0]):
        stores.append(pltpu.make_async_copy(pairs, out_ref.at[place], pair_sems.at[place]))
        stores[-1].start()
    for copy in stores:
        copy.wait()


def rows_kernel(own_ref, partner_ref, density_ref, table, at_ref):
    core = core_of()

    @pl.when(pl.program_id(0) == 0)
    def _():
        strips = at_ref.shape[1]
        split = 2 * VAL * 4
        bands = 2 * (VAL + CON) * 4
        at_ref[0] = own_ref[bands : bands + strips, :].astype(jnp.float32)
        at_ref[1] = own_ref[bands + strips : bands + 2 * strips, :].astype(jnp.float32)
        both = jnp.concatenate([own_ref[0:bands, :], partner_ref[0:bands, :]], 1)
        for parity in range(2):
            lanes = pl.ds(parity * 2 * SLICE, 2 * SLICE)
            table[0:KPAD, lanes] = pick(parity, both[:split])
            table[KPAD:, lanes] = pick(parity, both[split:bands])

    picked = []
    for which in range(2):
        index = []
        for s in range(STRIPS):
            strip = lane_matrix(at_ref[which, pl.ds(pl.program_id(0) * STRIPS + s, 1), :]).reshape(-1, 2, FINE, 128)
            index.append(jnp.where(core == 0, strip[:, 0], strip[:, 1]).reshape(-1, 128))
        hot = one_hot(jnp.concatenate(index, 0), KPAD)
        picked.append(
            jnp.dot(hot, table[which * KPAD : (which + 1) * KPAD, :], preferred_element_type=jnp.float32)
        )
    density_ref[...] = jnp.concatenate(densities(*picked), 1).astype(jnp.bfloat16)


def screened_kernel(pairs_ref, own_ref, joined_ref, block_ref, out_ref, sent_ref, held, sems):
    core = core_of()
    copies = []
    for part in range(2):
        for place, chip in enumerate(RING):
            lanes = pl.ds(pl.multiple_of((2 * chip + core) * SLICE, SLICE), SLICE)
            to = held.at[part, :, pl.ds(place * SLICE, SLICE)]
            copies.append(pltpu.make_async_copy(own_ref.at[part, :, lanes], to, sems.at[part, place]))
    for copy in copies:
        copy.start()
    pairs = pairs_ref[...].reshape(-1, 2 * WIDTH)
    chips = len(RING)
    start = joined_ref.shape[0] - JOINED * SLICE
    blocks = [joined_ref[start + i * SLICE : start + (i + 1) * SLICE, :] for i in range(JOINED)]
    blocks += [block_ref[i * SLICE : (i + 1) * SLICE, :] for i in range(2 * chips - JOINED)]
    for half in (1, 0):
        parts = []
        for part in range(2):
            if half == 0:
                for copy in copies[part * chips : (part + 1) * chips]:
                    copy.wait()
            w = jnp.concatenate(blocks[part * chips : (part + 1) * chips], 1) if half else held[part]
            parts.append(jnp.dot(w, pairs, preferred_element_type=jnp.float32))
        real = parts[0][:, :WIDTH] - parts[1][:, WIDTH:]
        imag = parts[0][:, WIDTH:] + parts[1][:, :WIDTH]
        both = jnp.concatenate([real, imag], 1)
        out_ref[half] = both
        sent_ref[half] = both.astype(jnp.bfloat16)


def direct_kernel(mine_ref, other_ref, density_ref, out_ref, screened):
    for half in range(2):
        x = (mine_ref[half] + other_ref[1 - half].astype(jnp.float32)).astype(jnp.bfloat16)
        screened[half * SLICE : (half + 1) * SLICE, :] = x
        screened[(2 + half) * SLICE : (3 + half) * SLICE, :WIDTH] = x[:, WIDTH:]
        screened[(2 + half) * SLICE : (3 + half) * SLICE, WIDTH:] = -x[:, :WIDTH]
    parts = 4
    rows = density_ref.shape[0] // parts
    strips = rows // 64
    for m in range(parts):
        direct = jnp.dot(
            density_ref[m * rows : (m + 1) * rows, :], screened[...], preferred_element_type=jnp.float32
        )
        direct = direct.reshape(strips, -1, FINE, 2 * WIDTH)
        direct = jnp.concatenate([direct[s] for s in range(strips)], 1).astype(jnp.bfloat16)
        for place, chip in enumerate(RING):
            out_ref[place, m * strips * FINE : (m + 1) * strips * FINE, :] = direct[chip]


def total_kernel(in_ref, out_ref):
    for part in range(2):
        lanes = slice(part * WIDTH, (part + 1) * WIDTH)
        total = in_ref[0, :, lanes].astype(jnp.float32)
        for chip in range(1, in_ref.shape[0]):
            total += in_ref[chip, :, lanes].astype(jnp.float32)
        out_ref[part] = total


def whole(array):
    return pl.BlockSpec(array.shape, lambda *_: (0,) * len(array.shape))


def shards(valence_orbitals, conduction_orbitals, screened, valence_index, conduction_index, kpoint_index):
    bf16, f32 = jnp.bfloat16, jnp.float32
    rows = lax.axis_size("row")
    chips = rows // 2
    swap = [(i, i ^ 1) for i in range(rows)]
    same_core = [[2 * chip + core for chip in RING] for core in range(2)]
    anywhere = pl.BlockSpec(memory_space=pl.ANY)
    in_vmem = pl.BlockSpec(memory_space=pltpu.VMEM)
    index = [array.reshape(-1, 128) for array in (valence_index, conduction_index, kpoint_index)]
    strips = index[0].shape[0]
    valence = valence_orbitals.reshape(-1, SLICE)
    conduction = conduction_orbitals.reshape(-1, SLICE)
    raw = (valence, conduction, *index)
    bands = valence.shape[0] + conduction.shape[0]
    dma = pltpu.SemaphoreType.DMA
    tables, pairs, blocks = pl.pallas_call(
        columns_kernel,
        out_shape=(
            jax.ShapeDtypeStruct((bands + 2 * strips + JOINED * SLICE, SLICE), bf16),
            jax.ShapeDtypeStruct((chips, SLICE, 2 * WIDTH), bf16),
            jax.ShapeDtypeStruct(((2 * chips - JOINED) * SLICE, SLICE), bf16),
        ),
        in_specs=[anywhere] * 6,
        out_specs=(anywhere,) * 3,
        scratch_shapes=[
            pltpu.VMEM((bands, SLICE), bf16),
            pltpu.VMEM((3, strips, 128), jnp.int32),
            pltpu.VMEM((2 * strips, 128), bf16),
            pltpu.VMEM((SLICE, 2 * WIDTH), bf16),
            pltpu.VMEM((2 * chips * SLICE, SLICE), bf16),
            dma((5,)),
            dma((2, chips)),
            dma((4,)),
            dma((chips,)),
        ],
        compiler_params=ALL,
        name="columns",
    )(*raw, screened)
    pairs = lax.all_to_all(pairs, "row", 0, 0, axis_index_groups=same_core, tiled=True)
    partner_tables = lax.ppermute(tables, "row", swap)
    blocks = lax.ppermute(blocks, "row", swap)
    density = pl.pallas_call(
        rows_kernel,
        out_shape=jax.ShapeDtypeStruct((strips * 64, 4 * SLICE), bf16),
        grid=(strips // STRIPS,),
        in_specs=[whole(tables), whole(partner_tables)],
        out_specs=pl.BlockSpec((STRIPS * 64, 4 * SLICE), lambda m: (m, 0)),
        scratch_shapes=[pltpu.VMEM((2 * KPAD, 4 * SLICE), bf16), pltpu.VMEM((2, strips, 128), f32)],
        compiler_params=LITTLE,
        cost_estimate=pl.CostEstimate(flops=0, bytes_accessed=0, transcendentals=0),
        name="rows",
    )(tables, partner_tables)
    pairs, density = lax.optimization_barrier((pairs, density))
    mine, other = pl.pallas_call(
        screened_kernel,
        out_shape=tuple(jax.ShapeDtypeStruct((2, SLICE, 2 * WIDTH), kind) for kind in (f32, bf16)),
        in_specs=[in_vmem, anywhere, in_vmem, in_vmem],
        scratch_shapes=[pltpu.VMEM((2, SLICE, chips * SLICE), bf16), pltpu.SemaphoreType.DMA((2, chips))],
        compiler_params=MUCH,
        name="screened",
    )(pairs, screened, partner_tables, blocks)
    other = lax.ppermute(other, "row", swap)
    partial = pl.pallas_call(
        direct_kernel,
        out_shape=jax.ShapeDtypeStruct((chips, strips * FINE, 2 * WIDTH), bf16),
        scratch_shapes=[pltpu.VMEM((4 * SLICE, 2 * WIDTH), bf16)],
        compiler_params=LITTLE,
        name="direct",
    )(mine, other, density)
    partial = lax.all_to_all(partial, "row", 0, 0, axis_index_groups=same_core, tiled=True)
    out = pl.pallas_call(
        total_kernel,
        out_shape=jax.ShapeDtypeStruct((2, strips * FINE, WIDTH), f32),
        compiler_params=LITTLE,
        name="total",
    )(partial)
    return out.reshape(2, strips, FINE, WIDTH)


def solution(mesh):
    in_specs = (
        P(None, None, None, "row"),
        P(None, None, None, "row"),
        P(None, "row", None),
        P(),
        P(),
        P(),
    )
    return jax.shard_map(
        shards, mesh=mesh, in_specs=in_specs, out_specs=P(None, None, "row", "col"), check_vma=False
    )
```
